32 devices in a mesh: img: 16 (over z, y, core), tile: 2 (over x).
Axes of the slice: x: 2, y: 2, z: 4, core: 2. Of those that a mesh axis runs over, the one named last changes fastest.
Arguments:
- indices: int32 [64, 16, 16], P('img', 'tile'), may hold values from 0 to 6287, as said below
- embed_table: bfloat16 [6288, 768], P('img'), may hold values from -6 to 6
- w_qkv: bfloat16 [768, 2304], P('img'), may hold values from -0.21875 to 0.21875
- bias_q: float32 [768], replicated, may hold values from -1.75 to 1.75
- bias_v: float32 [768], replicated, may hold values from -1.75 to 1.75
- w_out: bfloat16 [768, 768], P('img'), may hold values from -0.875 to 0.875
- bias_out: float32 [768], replicated, may hold values from -1.75 to 1.75
- gain_one: float32 [768], replicated, may hold values from 0.1 to 1.9
- shift_one: float32 [768], replicated, may hold values from -1.75 to 1.75
- gain_two: float32 [768], replicated, may hold values from 0.1 to 1.9
- shift_two: float32 [768], replicated, may hold values from -1.75 to 1.75
- w_up: bfloat16 [768, 3072], P('img'), may hold values from -0.21875 to 0.21875
- bias_up: float32 [3072], replicated, may hold values from -1.75 to 1.75
- w_down: bfloat16 [3072, 768], P('img'), may hold values from -0.109375 to 0.109375
- bias_down: float32 [768], replicated, may hold values from -1.75 to 1.75
- w_conv: bfloat16 [9, 768, 768], P(None, 'img'), may hold values from -0.078125 to 0.078125
- bias_conv: float32 [768], replicated, may hold values from -1.75 to 1.75
- d_pixels: bfloat16 [64, 16, 16, 768], P('img', 'tile'), may hold values from -6 to 6
Outputs:
- pixels: float32 [64, 16, 16, 768], P('img', 'tile')
- grad_embed: float32 [64, 16, 16, 768], P('img', 'tile')
- grad_w_qkv: float32 [768, 2304], P('img')
- grad_bias_q: float32 [768], replicated
- grad_bias_v: float32 [768], replicated
- grad_w_out: float32 [768, 768], P('img')
- grad_bias_out: float32 [768], replicated
- grad_gain_one: float32 [768], replicated
- grad_shift_one: float32 [768], replicated
- grad_gain_two: float32 [768], replicated
- grad_shift_two: float32 [768], replicated
- grad_w_up: float32 [768, 3072], P('img')
- grad_bias_up: float32 [3072], replicated
- grad_w_down: float32 [3072, 768], P('img')
- grad_bias_down: float32 [768], replicated
- grad_w_conv: float32 [9, 768, 768], P(None, 'img')
- grad_bias_conv: float32 [768], replicated
The draws below stay inside these ranges and needn't reach their ends.
Inputs may be any that keep to these rules, and one draw needn't show every extreme that they name: `indices`: the patches of one device (4 images, 8 patch rows of each) take at most 64 ids from any one block of 393 consecutive ids, and on every device exactly 64 from one block, the same block on all devices.
All inputs are finite; a program needn't handle non-finite values.
Results may differ from the reference program's by a relative error of at most 0.013.
Values may be sent and summed in bfloat16 or wider, within the bound.
A program may use at most 320 MiB of HBM per device.

```python
import math
import jax
import jax.numpy as jnp
from jax import lax

D = 768
HEADS = 12
MLP = 3072
PIX = 768
GRID = 16
VOC_DEV = 393
IMG_DEV = 4
HEAD_DIM = 64
HALF = 8
TOK_DEV = 512
IMAGES = 64
VOCAB = 6288
CAP = 64
N_IMG = 16
N_TILE = 2


def draw_indices(key, part):
    shared = jax.random.fold_in(key, 11)
    key = jax.random.fold_in(key, 7)
    full_owner = jax.random.randint(shared, (), 0, N_IMG)
    device_keys = jax.random.split(key, N_IMG * N_TILE)

    def one_device(dev_key):
        first_key, second_key, third_key = jax.random.split(dev_key, 3)
        others = jax.random.permutation(first_key, N_IMG * CAP - CAP).astype(jnp.int32) + CAP
        slots = jnp.concatenate([jnp.arange(CAP, dtype=jnp.int32), others[:TOK_DEV - CAP]])
        slots = jax.random.permutation(second_key, slots)
        owner_dev = (slots // CAP + full_owner) % N_IMG
        offsets = jax.random.randint(third_key, (TOK_DEV,), 0, VOC_DEV)
        return owner_dev * VOC_DEV + offsets
    drawn = jax.vmap(one_device)(device_keys)
    drawn = drawn.reshape(N_IMG, N_TILE, IMG_DEV, HALF, GRID)
    drawn = drawn.transpose(0, 2, 1, 3, 4)
    return drawn.reshape(IMAGES, GRID, GRID).astype(jnp.int32)


def level_of(rng, extent, cuts, least, top_value):
    level, own = 1.0, jax.random.fold_in(rng, 6)
    for axis_at, blocks in cuts:
        heights = jnp.exp(jax.random.uniform(jax.random.fold_in(own, axis_at), (blocks,), jnp.float32, least / len(cuts), top_value / len(cuts)))
        level = level * jnp.repeat(heights, extent[axis_at] // blocks).reshape([-1 if axis == axis_at else 1 for axis in range(len(extent))])
    return level


def bell_draw(rng, extent, scale, reach, shards=(), held_as=jnp.bfloat16):
    values = scale * jax.random.normal(rng, extent, jnp.float32)
    if shards:
        values = values * level_of(rng, extent, shards, -0.22, 0.18)
    return jnp.clip(values, -reach, reach).astype(held_as)


def setup_inputs(seed: int = 0) -> dict:
    keys = jax.random.split(jax.random.key(seed), 19)
    return {
        "indices": draw_indices(jax.random.fold_in(keys[18], 71), 0),
        "embed_table": bell_draw(keys[1], (VOCAB, D), 1.0, 6.0, ((0, 16),)),
        "w_qkv": bell_draw(keys[2], (D, 3 * D), D ** -0.5, 0.21875, ((0, 16),)),
        "bias_q": bell_draw(keys[3], (D,), 0.3, 1.75, (), jnp.float32),
        "bias_v": bell_draw(keys[4], (D,), 0.3, 1.75, (), jnp.float32),
        "w_out": bell_draw(keys[5], (D, D), (D // 16) ** -0.5, 0.875, ((0, 16),)),
        "bias_out": bell_draw(keys[6], (D,), 0.3, 1.75, (), jnp.float32),
        "gain_one": jnp.clip(1.0 + 0.18 * jax.random.normal(keys[7], (D,), jnp.float32), 0.1, 1.9),
        "shift_one": bell_draw(keys[8], (D,), 0.3, 1.75, (), jnp.float32),
        "gain_two": jnp.clip(1.0 + 0.18 * jax.random.normal(keys[9], (D,), jnp.float32), 0.1, 1.9),
        "shift_two": bell_draw(keys[10], (D,), 0.3, 1.75, (), jnp.float32),
        "w_up": bell_draw(keys[11], (D, MLP), D ** -0.5, 0.21875, ((0, 16),)),
        "bias_up": bell_draw(keys[12], (MLP,), 0.3, 1.75, (), jnp.float32),
        "w_down": bell_draw(keys[13], (MLP, D), MLP ** -0.5, 0.109375, ((0, 16),)),
        "bias_down": bell_draw(keys[14], (D,), 0.3, 1.75, (), jnp.float32),
        "w_conv": bell_draw(keys[15], (9, D, PIX), (9 * D) ** -0.5, 0.078125, ((1, 16),)),
        "bias_conv": bell_draw(keys[16], (PIX,), 0.3, 1.75, (), jnp.float32),
        "d_pixels": bell_draw(keys[17], (IMAGES, GRID, GRID, PIX), 1.0, 6.0, ((0, 16), (1, 2))),
    }


EPS = 1e-06
HIGH = lax.Precision.HIGHEST

@jax.custom_vjp
def low(v):
    return lax.optimization_barrier(v.astype(jnp.bfloat16)).astype(jnp.float32)

@jax.custom_vjp
def low_back(v):
    return v

def low_keep(v):
    return (low(v), None)

def low_pass(kept, grad):
    return (grad,)

def back_keep(v):
    return (v, None)

def back_low(kept, grad):
    return (low(grad),)
low.defvjp(low_keep, low_pass)
low_back.defvjp(back_keep, back_low)

def norm_rows(values, gain, shift):
    center = values - lax.optimization_barrier(jnp.mean(values, axis=-1, keepdims=True))
    spread = lax.optimization_barrier(jnp.mean(center * center, axis=-1, keepdims=True))
    return center * lax.rsqrt(spread + EPS) * gain + shift

def layer(embedded, params):
    w_qkv, bias_q, bias_v, w_out, bias_out, gain_one, shift_one, gain_two, shift_two, w_up, bias_up, w_down, bias_down, w_conv, bias_conv = params
    n_images = embedded.shape[0]
    tokens = embedded.reshape(n_images, GRID * GRID, D)
    normed = low(norm_rows(tokens, gain_one, shift_one))
    zeros_k = jnp.zeros_like(bias_q)
    joined = jnp.einsum('bte,ef->btf', normed, w_qkv, precision=HIGH) + jnp.concatenate([bias_q, zeros_k, bias_v])
    joined = low(low_back(joined))
    shaped = joined.reshape(n_images, GRID * GRID, 3, HEADS, HEAD_DIM)
    queries = shaped[:, :, 0]
    all_keys = shaped[:, :, 1]
    all_values = shaped[:, :, 2]
    scale = 1.0 / math.sqrt(HEAD_DIM)
    scores = low_back(jnp.einsum('bqhd,bkhd->bhqk', queries, all_keys, precision=HIGH) * scale)
    probs = low(jax.nn.softmax(scores, axis=-1))
    mixed = jnp.einsum('bhqk,bkhd->bqhd', probs, all_values, precision=HIGH).reshape(n_images, GRID * GRID, D)
    mixed = low(low_back(mixed))
    stream_one = tokens + low_back(jnp.einsum('bte,ef->btf', mixed, w_out, precision=HIGH) + bias_out)
    normed_two = low(norm_rows(stream_one, gain_two, shift_two))
    hidden = low_back(jnp.einsum('bte,em->btm', normed_two, w_up, precision=HIGH) + bias_up)
    activated = low(jax.nn.gelu(hidden))
    stream_two = stream_one + low_back(jnp.einsum('btm,me->bte', activated, w_down, precision=HIGH) + bias_down)
    surface = low(stream_two).reshape(n_images, GRID, GRID, D)
    padded = jnp.pad(surface, ((0, 0), (1, 1), (1, 1), (0, 0)))
    pixels = bias_conv
    for row_off in range(3):
        for col_off in range(3):
            window = padded[:, row_off:row_off + GRID, col_off:col_off + GRID]
            pixels = pixels + jnp.einsum('brce,ef->brcf', window, w_conv[3 * row_off + col_off], precision=HIGH)
    return pixels

def reference(indices, embed_table, w_qkv, bias_q, bias_v, w_out, bias_out, gain_one, shift_one, gain_two, shift_two, w_up, bias_up, w_down, bias_down, w_conv, bias_conv, d_pixels):
    params = tuple((item.astype(jnp.float32) for item in (w_qkv, bias_q, bias_v, w_out, bias_out, gain_one, shift_one, gain_two, shift_two, w_up, bias_up, w_down, bias_down, w_conv, bias_conv)))
    group = min(16, IMAGES)
    rounds = IMAGES // group
    id_groups = indices.reshape(rounds, group, GRID, GRID)
    cot_groups = d_pixels.reshape(rounds, group, GRID, GRID, PIX)

    def one_group(carry, inputs):
        group_ids, group_cot = inputs
        embedded = embed_table[group_ids].astype(jnp.float32)
        outputs, pull = jax.vjp(layer, embedded, params)
        d_embedded, d_params = pull(group_cot.astype(jnp.float32))
        carry = jax.tree.map(jnp.add, carry, d_params)
        return (carry, (outputs, d_embedded))
    start = jax.tree.map(jnp.zeros_like, params)
    totals, (pixels, grad_embed) = lax.scan(one_group, start, (id_groups, cot_groups))
    pixels = pixels.reshape(IMAGES, GRID, GRID, PIX)
    grad_embed = grad_embed.reshape(IMAGES, GRID, GRID, D)
    g_qkv, g_bias_q, g_bias_v, g_out, g_bias_out, g_gain_one, g_shift_one, g_gain_two, g_shift_two, g_up, g_bias_up, g_down, g_bias_down, g_conv, g_bias_conv = totals
    return (pixels, grad_embed, g_qkv, g_bias_q, g_bias_v, g_out, g_bias_out, g_gain_one, g_shift_one, g_gain_two, g_shift_two, g_up, g_bias_up, g_down, g_bias_down, g_conv, g_bias_conv)
```

```python
import math

import jax
import jax.numpy as jnp
from jax import lax
from jax.experimental import pallas as pl
from jax.experimental.pallas import tpu as pltpu
from jax.sharding import PartitionSpec as P

HEADS = 12


EPS = 1e-06


def extended_2(block, sides, width):
    for axis, dim in sides:
        count = lax.axis_size(axis)
        forward = [(i, i + 1) for i in range(count - 1)]
        backward = [(target, source) for source, target in forward]
        low = lax.ppermute(
            lax.slice_in_dim(block, block.shape[dim] - width, None, axis=dim), axis, forward
        )
        high = lax.ppermute(lax.slice_in_dim(block, 0, width, axis=dim), axis, backward)
        block = jnp.concatenate([low, block, high], axis=dim)
    return block


def norm_rows(values, gain, shift):
    center = values - jnp.mean(values, axis=-1, keepdims=True)
    spread = jnp.mean(center * center, axis=-1, keepdims=True)
    return center * lax.rsqrt(spread + EPS) * gain + shift


def shards(
    indices,
    embed_table,
    w_qkv,
    bias_q,
    bias_v,
    w_out,
    bias_out,
    gain_one,
    shift_one,
    gain_two,
    shift_two,
    w_up,
    bias_up,
    w_down,
    bias_down,
    w_conv,
    bias_conv,
    d_pixels,
):
    n_images, half_rows, grid_cols = indices.shape
    vocab_rows, model_width = embed_table.shape
    n_img = lax.axis_size("img")
    local_tokens = half_rows * grid_cols
    all_tokens = n_images * local_tokens
    capacity = max(2, 2 * all_tokens // n_img)
    flat_ids = indices.reshape(all_tokens)
    owner_dev = flat_ids // vocab_rows
    within = flat_ids - owner_dev * vocab_rows
    hits = (owner_dev[:, None] == jnp.arange(n_img, dtype=jnp.int32)[None, :]).astype(jnp.int32)
    slot_rank = jnp.sum((jnp.cumsum(hits, axis=0) - hits) * hits, axis=1)
    slot_index = owner_dev * capacity + slot_rank
    requests = (
        jnp.zeros((n_img * capacity,), jnp.int32)
        .at[slot_index]
        .set(within)
        .reshape(n_img, capacity)
    )
    found = jnp.take(
        embed_table,
        lax.all_to_all(requests, "img", split_axis=0, concat_axis=0, tiled=True),
        axis=0,
    )
    answers = lax.all_to_all(found, "img", split_axis=0, concat_axis=0, tiled=True)
    embedded = jnp.take(answers.reshape(n_img * capacity, model_width), slot_index, axis=0)
    token_rows = embedded.astype(jnp.float32).reshape(n_images, local_tokens, model_width)
    full_qkv, full_out, full_up, full_down, full_conv = (
        lax.all_gather(w_qkv, "img", axis=0, tiled=True),
        lax.all_gather(w_out, "img", axis=0, tiled=True),
        lax.all_gather(w_up, "img", axis=0, tiled=True),
        lax.all_gather(w_down, "img", axis=0, tiled=True),
        lax.all_gather(w_conv, "img", axis=1, tiled=True),
    )
    normed_one, pull_one = jax.vjp(norm_rows, token_rows, gain_one, shift_one)
    normed_low = normed_one.astype(jnp.bfloat16)
    zeros_k = jnp.zeros_like(bias_q)
    joined = jnp.einsum("bte,ef->btf", normed_low, full_qkv, preferred_element_type=jnp.float32)
    joined = joined + jnp.concatenate([bias_q, zeros_k, bias_v])
    joined_low = joined.astype(jnp.bfloat16).reshape(n_images, local_tokens, 3, HEADS, -1)
    queries = joined_low[:, :, 0]
    own_keys = joined_low[:, :, 1]
    own_values = joined_low[:, :, 2]
    all_keys, all_values = (
        lax.all_gather(own_keys, "tile", axis=1, tiled=True),
        lax.all_gather(own_values, "tile", axis=1, tiled=True),
    )
    scale = 1.0 / math.sqrt(queries.shape[-1])
    scores = (
        jnp.einsum("bqhd,bkhd->bhqk", queries, all_keys, preferred_element_type=jnp.float32) * scale
    )
    row_max = jnp.max(scores, axis=-1, keepdims=True)
    shifted = jnp.exp(scores - row_max)
    row_total = jnp.sum(shifted, axis=-1, keepdims=True)
    log_total = row_max + jnp.log(row_total)
    probs_low = (shifted / row_total).astype(jnp.bfloat16)
    mixed = jnp.einsum("bhqk,bkhd->bqhd", probs_low, all_values, preferred_element_type=jnp.float32)
    mixed_low = mixed.reshape(n_images, local_tokens, model_width).astype(jnp.bfloat16)
    stream_one = token_rows + (
        jnp.einsum("bte,ef->btf", mixed_low, full_out, preferred_element_type=jnp.float32)
        + bias_out
    )
    normed_two, pull_two = jax.vjp(norm_rows, stream_one, gain_two, shift_two)
    normed_two_low = normed_two.astype(jnp.bfloat16)
    hidden = (
        jnp.einsum("bte,em->btm", normed_two_low, full_up, preferred_element_type=jnp.float32)
        + bias_up
    )
    activated, pull_act = jax.vjp(jax.nn.gelu, hidden)
    activated_low = activated.astype(jnp.bfloat16)
    stream_two = stream_one + (
        jnp.einsum("btm,me->bte", activated_low, full_down, preferred_element_type=jnp.float32)
        + bias_down
    )
    surface = stream_two.astype(jnp.bfloat16).reshape(n_images, half_rows, grid_cols, model_width)
    extended = extended_2(surface, (("tile", 1),), 1)
    padded = jnp.pad(extended, ((0, 0), (0, 0), (1, 1), (0, 0)))
    pixels = bias_conv
    for row_off in range(3):
        for col_off in range(3):
            window = padded[:, row_off : row_off + half_rows, col_off : col_off + grid_cols]
            pixels = pixels + jnp.einsum(
                "brce,ef->brcf",
                window,
                full_conv[3 * row_off + col_off],
                preferred_element_type=jnp.float32,
            )
    back_qkv, back_out, back_up, back_down, back_conv = (
        lax.all_gather(w_qkv, "img", axis=0, tiled=True),
        lax.all_gather(w_out, "img", axis=0, tiled=True),
        lax.all_gather(w_up, "img", axis=0, tiled=True),
        lax.all_gather(w_down, "img", axis=0, tiled=True),
        lax.all_gather(w_conv, "img", axis=1, tiled=True),
    )
    conv_terms = []
    for row_off in range(3):
        for col_off in range(3):
            window = padded[:, row_off : row_off + half_rows, col_off : col_off + grid_cols]
            conv_terms.append(
                jnp.einsum("brce,brcf->ef", window, d_pixels, preferred_element_type=jnp.float32)
            )
    grad_w_conv = jnp.stack(conv_terms)
    grad_bias_conv = jnp.sum(d_pixels.astype(jnp.float32), axis=(0, 1, 2))
    cot_ext = extended_2(d_pixels, (("tile", 1),), 1)
    cot_pad = jnp.pad(cot_ext, ((0, 0), (0, 0), (1, 1), (0, 0)))
    d_surface = jnp.zeros((n_images, half_rows, grid_cols, model_width), jnp.float32)
    for row_off in range(3):
        for col_off in range(3):
            window = cot_pad[
                :, 2 - row_off : 2 - row_off + half_rows, 2 - col_off : 2 - col_off + grid_cols
            ]
            d_surface = d_surface + jnp.einsum(
                "brcf,ef->brce",
                window,
                back_conv[3 * row_off + col_off],
                preferred_element_type=jnp.float32,
            )
    d_stream_two = d_surface.reshape(n_images, local_tokens, model_width)
    branch_two = d_stream_two.astype(jnp.bfloat16)
    grad_w_down = jnp.einsum(
        "btm,bte->me", activated_low, branch_two, preferred_element_type=jnp.float32
    )
    grad_bias_down = jnp.sum(branch_two.astype(jnp.float32), axis=(0, 1))
    d_activated = jnp.einsum(
        "bte,me->btm", branch_two, back_down, preferred_element_type=jnp.float32
    )
    (d_hidden,) = pull_act(d_activated)
    d_hidden_low = d_hidden.astype(jnp.bfloat16)
    grad_w_up = jnp.einsum(
        "bte,btm->em", normed_two_low, d_hidden_low, preferred_element_type=jnp.float32
    )
    grad_bias_up = jnp.sum(d_hidden_low.astype(jnp.float32), axis=(0, 1))
    d_normed_two = jnp.einsum(
        "btm,em->bte", d_hidden_low, back_up, preferred_element_type=jnp.float32
    )
    d_from_two, grad_gain_two, grad_shift_two = pull_two(d_normed_two)
    d_stream_one = d_stream_two + d_from_two
    branch_one = d_stream_one.astype(jnp.bfloat16)
    grad_w_out = jnp.einsum(
        "bte,btf->ef", mixed_low, branch_one, preferred_element_type=jnp.float32
    )
    grad_bias_out = jnp.sum(branch_one.astype(jnp.float32), axis=(0, 1))
    d_mixed = jnp.einsum("btf,ef->bte", branch_one, back_out, preferred_element_type=jnp.float32)
    d_mixed = d_mixed.astype(jnp.bfloat16).reshape(n_images, local_tokens, HEADS, -1)
    scores_again = (
        jnp.einsum("bqhd,bkhd->bhqk", queries, all_keys, preferred_element_type=jnp.float32) * scale
    )
    probs_again = jnp.exp(scores_again - log_total)
    d_probs = jnp.einsum("bqhd,bkhd->bhqk", d_mixed, all_values, preferred_element_type=jnp.float32)
    inner = jnp.sum(probs_again * d_probs, axis=-1, keepdims=True)
    d_scores = (probs_again * (d_probs - inner)).astype(jnp.bfloat16)
    d_queries = (
        jnp.einsum("bhqk,bkhd->bqhd", d_scores, all_keys, preferred_element_type=jnp.float32)
        * scale
    )
    d_keys_all = (
        jnp.einsum("bhqk,bqhd->bkhd", d_scores, queries, preferred_element_type=jnp.float32) * scale
    )
    d_values_all = jnp.einsum(
        "bhqk,bqhd->bkhd",
        probs_again.astype(jnp.bfloat16),
        d_mixed,
        preferred_element_type=jnp.float32,
    )
    d_keys, d_values = (
        lax.psum_scatter(
            d_keys_all.astype(jnp.bfloat16), "tile", scatter_dimension=1, tiled=True
        ).astype(jnp.float32),
        lax.psum_scatter(
            d_values_all.astype(jnp.bfloat16), "tile", scatter_dimension=1, tiled=True
        ).astype(jnp.float32),
    )
    d_joined = jnp.stack([d_queries, d_keys, d_values], axis=2).astype(jnp.bfloat16)
    d_joined = d_joined.reshape(n_images, local_tokens, 3 * model_width)
    grad_w_qkv = jnp.einsum("bte,btf->ef", normed_low, d_joined, preferred_element_type=jnp.float32)
    joined_sums = jnp.sum(d_joined.astype(jnp.float32), axis=(0, 1))
    grad_bias_q = joined_sums[:model_width]
    grad_bias_v = joined_sums[2 * model_width :]
    d_normed_one = jnp.einsum("btf,ef->bte", d_joined, back_qkv, preferred_element_type=jnp.float32)
    d_from_one, grad_gain_one, grad_shift_one = pull_one(d_normed_one)
    grad_embed = (d_stream_one + d_from_one).reshape(n_images, half_rows, grid_cols, model_width)
    part_qkv, part_out, part_up, part_down, part_conv = (
        lax.psum_scatter(grad_w_qkv, "img", scatter_dimension=0, tiled=True),
        lax.psum_scatter(grad_w_out, "img", scatter_dimension=0, tiled=True),
        lax.psum_scatter(grad_w_up, "img", scatter_dimension=0, tiled=True),
        lax.psum_scatter(grad_w_down, "img", scatter_dimension=0, tiled=True),
        lax.psum_scatter(grad_w_conv, "img", scatter_dimension=1, tiled=True),
    )
    sum_qkv, sum_out, sum_up, sum_down, sum_conv = (
        lax.psum(part_qkv.astype(jnp.bfloat16), "tile").astype(jnp.float32),
        lax.psum(part_out.astype(jnp.bfloat16), "tile").astype(jnp.float32),
        lax.psum(part_up.astype(jnp.bfloat16), "tile").astype(jnp.float32),
        lax.psum(part_down.astype(jnp.bfloat16), "tile").astype(jnp.float32),
        lax.psum(part_conv.astype(jnp.bfloat16), "tile").astype(jnp.float32),
    )
    (
        sum_bias_q,
        sum_bias_v,
        sum_bias_out,
        sum_gain_one,
        sum_shift_one,
        sum_gain_two,
        sum_shift_two,
        sum_bias_up,
        sum_bias_down,
        sum_bias_conv,
    ) = lax.psum(
        (
            grad_bias_q,
            grad_bias_v,
            grad_bias_out,
            grad_gain_one,
            grad_shift_one,
            grad_gain_two,
            grad_shift_two,
            grad_bias_up,
            grad_bias_down,
            grad_bias_conv,
        ),
        ("img", "tile"),
    )
    return (
        pixels,
        grad_embed,
        sum_qkv,
        sum_bias_q,
        sum_bias_v,
        sum_out,
        sum_bias_out,
        sum_gain_one,
        sum_shift_one,
        sum_gain_two,
        sum_shift_two,
        sum_up,
        sum_bias_up,
        sum_down,
        sum_bias_down,
        sum_conv,
        sum_bias_conv,
    )


MESH = pl.DeviceIdType.MESH
DIM = 768


def unit_list():
    return (
        [("qkv", k) for k in range(3)]
        + [("out", 0)]
        + [("up", k) for k in range(4)]
        + [("down", k) for k in range(4)]
        + [("conv", t) for t in range(9)]
    )


def piece(refs, unit, where, columns):
    name, k = unit
    start, width = columns
    ref = refs[name]
    rows = pl.ds(0, 48)
    if name == "conv":
        where = (k,) + where
    if name == "down":
        rows = pl.ds(48 * k, 48)
    if name in ("qkv", "up"):
        start = start + DIM * k
    return ref.at[where + (rows, pl.ds(aligned(start), width))]


def aligned(start):
    return start if isinstance(start, int) else pl.multiple_of(start, 128)


def place():
    img, tile = lax.axis_index("img"), lax.axis_index("tile")
    return img // 4, lax.rem(img // 2, 2), lax.rem(img, 2), tile


def device(z, y, c, x):
    return (z * 4 + y * 2 + c, x)


def greet(others):
    barrier = pltpu.get_barrier_semaphore()
    for other in others:
        pl.semaphore_signal(barrier, inc=1, device_id=other, device_id_type=MESH)
    pl.semaphore_wait(barrier, len(others))


def neighbours():
    z, y, c, x = place()
    turn = [device(lax.rem(z + step, 4), y, c, x) for step in (1, 2, 3)]
    return turn, device(z, 1 - y, c, x), device(z, y, c, 1 - x), device(z, y, 1 - c, x)


class Gather:
    def __init__(self, shards, full, send, recv, local):
        self.shards, self.full, self.send, self.recv, self.local = shards, full, send, recv, local
        z, y, c, x = place()
        self.z, self.y, self.c, self.x = z, y, c, x
        self.turn, self.dev_y, self.dev_x, self.dev_c = neighbours()
        self.one = (0, 256)
        self.mine = (256 + 256 * x, 256)
        self.theirs = (512 - 256 * x, 256)

    def copy(self, u, slot, src, dst, dev):
        return pltpu.make_async_remote_copy(
            src_ref=src,
            dst_ref=dst,
            send_sem=self.send.at[u, slot],
            recv_sem=self.recv.at[u, slot],
            device_id=dev,
            device_id_type=MESH,
        )

    def at(self, u, where, columns):
        return piece(self.full, UNITS[u], where, columns)

    def hop(self, u, slot, where, columns, dev):
        ref = self.at(u, where, columns)
        return self.copy(u, slot, ref, ref, dev)

    def own(self, u):
        here = (self.z, self.y, self.c)
        return [
            pltpu.make_async_copy(
                piece(self.shards, UNITS[u], (), columns),
                self.at(u, here, columns),
                self.local.at[u, n],
            )
            for n, columns in enumerate((self.one, self.mine))
        ]

    def along_z(self, u):
        here = (self.z, self.y, self.c)
        return [
            self.copy(
                u,
                3 * n + step,
                piece(self.shards, UNITS[u], (), columns),
                self.at(u, here, columns),
                self.turn[step],
            )
            for n, columns in enumerate((self.one, self.mine))
            for step in range(3)
        ]

    def came_z(self, u):
        out = []
        for n, columns in enumerate((self.one, self.mine)):
            for step in range(3):
                ref = self.at(u, (lax.rem(self.z + 3 - step, 4), self.y, self.c), columns)
                out.append(self.copy(u, 3 * n + step, ref, ref, self.turn[step]))
        return out

    def second(self, u, y, came=False):
        c = 1 - self.c if came else self.c
        y_out = 1 - self.y if came else self.y
        all_z = slice(None)
        return [
            self.hop(u, 6, (all_z, y_out, self.c), self.one, self.dev_y),
            self.hop(u, 7, (all_z, y_out, self.c), self.mine, self.dev_y),
        ]

    def to_x(self, u, slot, y, came=False):
        columns = self.theirs if came else self.mine
        return self.hop(u, slot, (slice(None), y, self.c), columns, self.dev_x)

    def to_core(self, u, slot, y, columns, came=False):
        c = 1 - self.c if came else self.c
        return self.hop(u, slot, (slice(None), y, c), columns, self.dev_c)

    def stage(self, u, step):
        y = self.y
        if step == 0:
            for copy in self.along_z(u) + self.own(u):
                copy.start()
        if step == 1:
            for copy in self.own(u):
                copy.wait()
            for copy in self.came_z(u):
                copy.wait_recv()
            for copy in self.second(u, y):
                copy.start()
            self.to_x(u, 8, y).start()
            self.to_core(u, 10, y, self.one).start()
            self.to_core(u, 11, y, self.mine).start()
        if step == 2:
            for copy in self.second(u, y, True):
                copy.wait_recv()
            self.to_x(u, 9, 1 - y).start()
            self.to_core(u, 12, 1 - y, self.one).start()
            self.to_core(u, 13, 1 - y, self.mine).start()
        if step == 3:
            self.to_x(u, 8, y, True).wait_recv()
            self.to_x(u, 9, 1 - y, True).wait_recv()
            self.to_core(u, 14, slice(None), self.theirs).start()
        if step == 4:
            self.to_core(u, 10, y, self.one, True).wait_recv()
            self.to_core(u, 11, y, self.mine, True).wait_recv()
            self.to_core(u, 12, 1 - y, self.one, True).wait_recv()
            self.to_core(u, 13, 1 - y, self.mine, True).wait_recv()
            self.to_core(u, 14, slice(None), self.theirs, True).wait_recv()
        if step == 5:
            for copy in self.along_z(u) + self.second(u, y):
                copy.wait_send()
            self.to_x(u, 8, y).wait_send()
            self.to_x(u, 9, 1 - y).wait_send()
            self.to_core(u, 10, y, self.one).wait_send()
            self.to_core(u, 11, y, self.mine).wait_send()
            self.to_core(u, 12, 1 - y, self.one).wait_send()
            self.to_core(u, 13, 1 - y, self.mine).wait_send()
            self.to_core(u, 14, slice(None), self.theirs).wait_send()


UNITS = unit_list()
NAMES = ("qkv", "out", "up", "down", "conv")


def gather_kernel(*refs):
    shards = dict(zip(NAMES, refs[:5]))
    full = dict(zip(NAMES, refs[5:10]))
    send, recv, local = refs[10:]
    turn, dev_y, dev_x, dev_c = neighbours()
    greet(turn + [dev_y, dev_x, dev_c])
    gather = Gather(shards, full, send, recv, local)
    count = len(UNITS)
    for tick in range(count + 5):
        for step in range(6):
            if 0 <= tick - step < count:
                gather.stage(tick - step, step)


FULL = {
    "qkv": (4, 2, 2, 48, 2304),
    "out": (4, 2, 2, 48, 768),
    "up": (4, 2, 2, 48, 3072),
    "down": (4, 2, 2, 192, 768),
    "conv": (9, 4, 2, 2, 48, 768),
}


def gather_weights(*shards):
    count = len(UNITS)
    return pl.pallas_call(
        gather_kernel,
        out_shape=[jax.ShapeDtypeStruct(FULL[name], jnp.bfloat16) for name in NAMES],
        in_specs=[pl.BlockSpec(memory_space=pl.ANY)] * 5,
        out_specs=[pl.BlockSpec(memory_space=pl.ANY)] * 5,
        scratch_shapes=[
            pltpu.SemaphoreType.DMA((count, 15)),
            pltpu.SemaphoreType.DMA((count, 15)),
            pltpu.SemaphoreType.DMA((count, 2)),
        ],
        compiler_params=pltpu.CompilerParams(collective_id=0, has_side_effects=True),
        name="gather_weights",
    )(*shards)


class Scatter:
    def __init__(self, partial, sums, buffers, send, recv, local, order):
        self.partial, self.sums, self.order = partial, sums, order
        self.own, self.core, self.ax, self.y_one, self.y_two, self.z_one, self.z_two, self.x_one, self.x_two = buffers
        self.send, self.recv, self.local = send, recv, local
        z, y, c, x = place()
        self.z, self.y, self.c, self.x = z, y, c, x
        self.turn, self.dev_y, self.dev_x, self.dev_c = neighbours()
        self.one = (0, 512)
        self.mine = (512 + 128 * x, 128)
        self.theirs = (640 - 128 * x, 128)

    def copy(self, n, slot, src, dst, dev):
        return pltpu.make_async_remote_copy(
            src_ref=src,
            dst_ref=dst,
            send_sem=self.send.at[n, slot],
            recv_sem=self.recv.at[n, slot],
            device_id=dev,
            device_id_type=MESH,
        )

    def cols(self, columns):
        return pl.ds(aligned(columns[0]), columns[1])

    def sent(self, n, name, step=0):
        y, y_cols = self.y, self.cols(self.one)
        there = lax.rem(self.z + step + 1, 4)
        if name == "core":
            source = piece(self.partial, self.order[n], (slice(None), slice(None), 1 - self.c), (0, DIM))
            return self.copy(n, 0, source, self.core.at[n], self.dev_c)
        if name == "x":
            return self.copy(n, 1, self.core.at[n, :, :, :, self.cols(self.theirs)], self.ax.at[n], self.dev_x)
        if name == "y1":
            return self.copy(n, 2, self.core.at[n, :, 1 - y, :, y_cols], self.y_one.at[n], self.dev_y)
        if name == "y2":
            return self.copy(n, 3, self.ax.at[n, :, 1 - y], self.y_two.at[n], self.dev_y)
        if name == "z1":
            return self.copy(n, 4 + step, self.y_one.at[n, there], self.z_one.at[n, step], self.turn[step])
        if name == "z2":
            return self.copy(n, 7 + step, self.y_two.at[n, there], self.z_two.at[n, step], self.turn[step])
        if name == "x1":
            return self.copy(n, 10, self.x_one.at[n, 0], self.x_one.at[n, 1], self.dev_x)
        return self.copy(n, 11, self.x_two.at[n, 0], self.x_two.at[n, 1], self.dev_x)

    def load(self, n):
        u = self.order[n]
        every = slice(None)
        return pltpu.make_async_copy(
            piece(self.partial, u, (every, every, self.c), (0, DIM)),
            self.own.at[n % self.own.shape[0]],
            self.local.at[n],
        )

    def stage(self, n, step):
        f32, bf16 = jnp.float32, jnp.bfloat16
        if step == 0:
            self.sent(n, "core").start()
            self.load(n).start()
        if step == 1:
            self.load(n).wait()
            self.sent(n, "core").wait_recv()
            mine = self.own.at[n % self.own.shape[0]]

            @pl.loop(0, 4)
            def _(i):
                self.core[n, i] = (self.core[n, i].astype(f32) + mine[i].astype(f32)).astype(bf16)

            self.sent(n, "x").start()
            self.sent(n, "y1").start()
        if step == 2:
            self.sent(n, "x").wait_recv()
            columns = self.cols(self.mine)

            @pl.loop(0, 4)
            def _(i):
                self.ax[n, i] = (self.ax[n, i].astype(f32) + self.core[n, i, :, :, columns].astype(f32)).astype(bf16)

            self.sent(n, "y2").start()
            self.sent(n, "y1").wait_recv()
            columns = self.cols(self.one)

            @pl.loop(0, 4)
            def _(i):
                self.y_one[n, i] = (
                    self.y_one[n, i].astype(f32) + self.core[n, i, self.y, :, columns].astype(f32)
                ).astype(bf16)

            for step_z in range(3):
                self.sent(n, "z1", step_z).start()
        if step == 3:
            self.sent(n, "y2").wait_recv()

            @pl.loop(0, 4)
            def _(i):
                self.y_two[n, i] = (self.y_two[n, i].astype(f32) + self.ax[n, i, self.y].astype(f32)).astype(bf16)

            for step_z in range(3):
                self.sent(n, "z2", step_z).start()
            for step_z in range(3):
                self.sent(n, "z1", step_z).wait_recv()
            total = self.y_one[n, self.z].astype(f32)
            for step_z in range(3):
                total = total + self.z_one[n, step_z].astype(f32)
            self.x_one[n, 0] = total.astype(bf16)
            self.sent(n, "x1").start()
        if step == 4:
            for step_z in range(3):
                self.sent(n, "z2", step_z).wait_recv()
            total = self.y_two[n, self.z].astype(f32)
            for step_z in range(3):
                total = total + self.z_two[n, step_z].astype(f32)
            self.x_two[n, 0] = total.astype(bf16)
            self.sent(n, "x2").start()
            self.sent(n, "x1").wait_recv()
            self.out(n, self.one)[...] = self.x_one[n, 0].astype(f32) + self.x_one[n, 1].astype(f32)
        if step == 5:
            self.sent(n, "x2").wait_recv()
            self.out(n, self.mine)[...] = self.x_two[n, 0].astype(f32)
            self.out(n, self.theirs)[...] = self.x_two[n, 1].astype(f32)
            for name in ("core", "x", "y1", "y2", "x1", "x2"):
                self.sent(n, name).wait_send()
            for name in ("z1", "z2"):
                for step_z in range(3):
                    self.sent(n, name, step_z).wait_send()

    def out(self, n, columns):
        return piece(self.sums, self.order[n], (), columns)


ORDER = (
    [("conv", t) for t in range(9)]
    + [("down", k) for k in range(4)]
    + [("up", k) for k in range(4)]
    + [("out", 0)]
    + [("qkv", k) for k in range(3)]
)


def scatter_scratch():
    count = len(ORDER)
    bf16 = jnp.bfloat16
    return [
        pltpu.VMEM((3, 4, 2, 48, DIM), bf16),
        pltpu.VMEM((count, 4, 2, 48, DIM), bf16),
        pltpu.VMEM((count, 4, 2, 48, 128), bf16),
        pltpu.VMEM((count, 4, 48, 512), bf16),
        pltpu.VMEM((count, 4, 48, 128), bf16),
        pltpu.VMEM((count, 3, 48, 512), bf16),
        pltpu.VMEM((count, 3, 48, 128), bf16),
        pltpu.VMEM((count, 2, 48, 512), bf16),
        pltpu.VMEM((count, 2, 48, 128), bf16),
        pltpu.SemaphoreType.DMA((count, 12)),
        pltpu.SemaphoreType.DMA((count, 12)),
        pltpu.SemaphoreType.DMA((count,)),
    ]


def scatter_kernel(*refs):
    partial = dict(zip(NAMES, refs[:5]))
    sums = dict(zip(NAMES, refs[5:10]))
    buffers, (send, recv, local) = refs[10:19], refs[19:]
    turn, dev_y, dev_x, dev_c = neighbours()
    greet(turn + [dev_y, dev_x, dev_c])
    scatter = Scatter(partial, sums, buffers, send, recv, local, ORDER)
    count = len(ORDER)
    for tick in range(count + 5):
        for step in range(6):
            if 0 <= tick - step < count:
                scatter.stage(tick - step, step)


SUMS = {"qkv": (48, 2304), "out": (48, 768), "up": (48, 3072), "down": (192, 768), "conv": (9, 48, 768)}


def scatter_grads(*partial):
    return pl.pallas_call(
        scatter_kernel,
        out_shape=[jax.ShapeDtypeStruct(SUMS[name], jnp.float32) for name in NAMES],
        in_specs=[pl.BlockSpec(memory_space=pl.ANY)] * 5,
        out_specs=[pl.BlockSpec(memory_space=pltpu.VMEM)] * 5,
        scratch_shapes=scatter_scratch(),
        compiler_params=pltpu.CompilerParams(
            collective_id=1, has_side_effects=True, vmem_limit_bytes=60 * 2**20
        ),
        name="scatter_grads",
    )(*[part.reshape(FULL[name]) for name, part in zip(NAMES, partial)])


def fast_shards(
    indices,
    embed_table,
    w_qkv,
    bias_q,
    bias_v,
    w_out,
    bias_out,
    gain_one,
    shift_one,
    gain_two,
    shift_two,
    w_up,
    bias_up,
    w_down,
    bias_down,
    w_conv,
    bias_conv,
    d_pixels,
):
    n_images, half_rows, grid_cols = indices.shape
    vocab_rows, model_width = embed_table.shape
    n_img = lax.axis_size("img")
    local_tokens = half_rows * grid_cols
    all_tokens = n_images * local_tokens
    capacity = max(2, 2 * all_tokens // n_img)
    flat_ids = indices.reshape(all_tokens)
    owner_dev = flat_ids // vocab_rows
    within = flat_ids - owner_dev * vocab_rows
    hits = (owner_dev[:, None] == jnp.arange(n_img, dtype=jnp.int32)[None, :]).astype(jnp.int32)
    slot_rank = jnp.sum((jnp.cumsum(hits, axis=0) - hits) * hits, axis=1)
    slot_index = owner_dev * capacity + slot_rank
    requests = (
        jnp.zeros((n_img * capacity,), jnp.int32)
        .at[slot_index]
        .set(within)
        .reshape(n_img, capacity)
    )
    found = jnp.take(
        embed_table,
        lax.all_to_all(requests, "img", split_axis=0, concat_axis=0, tiled=True),
        axis=0,
    )
    answers = lax.all_to_all(found, "img", split_axis=0, concat_axis=0, tiled=True)
    embedded = jnp.take(answers.reshape(n_img * capacity, model_width), slot_index, axis=0)
    token_rows = embedded.astype(jnp.float32).reshape(n_images, local_tokens, model_width)
    gathered = gather_weights(w_qkv, w_out, w_up, w_down, w_conv)
    full_qkv, full_out, full_up, full_down, full_conv = (
        gathered[0].reshape(768, 2304),
        gathered[1].reshape(768, 768),
        gathered[2].reshape(768, 3072),
        gathered[3].reshape(3072, 768),
        gathered[4].reshape(9, 768, 768),
    )
    back_qkv, back_out, back_up, back_down, back_conv = full_qkv, full_out, full_up, full_down, full_conv
    normed_one, pull_one = jax.vjp(norm_rows, token_rows, gain_one, shift_one)
    normed_low = normed_one.astype(jnp.bfloat16)
    zeros_k = jnp.zeros_like(bias_q)
    joined = jnp.einsum("bte,ef->btf", normed_low, full_qkv, preferred_element_type=jnp.float32)
    joined = joined + jnp.concatenate([bias_q, zeros_k, bias_v])
    joined_low = joined.astype(jnp.bfloat16).reshape(n_images, local_tokens, 3, HEADS, -1)
    queries = joined_low[:, :, 0]
    own_keys = joined_low[:, :, 1]
    own_values = joined_low[:, :, 2]
    all_keys, all_values = (
        lax.all_gather(own_keys, "tile", axis=1, tiled=True),
        lax.all_gather(own_values, "tile", axis=1, tiled=True),
    )
    scale = 1.0 / math.sqrt(queries.shape[-1])
    scores = (
        jnp.einsum("bqhd,bkhd->bhqk", queries, all_keys, preferred_element_type=jnp.float32) * scale
    )
    row_max = jnp.max(scores, axis=-1, keepdims=True)
    shifted = jnp.exp(scores - row_max)
    row_total = jnp.sum(shifted, axis=-1, keepdims=True)
    log_total = row_max + jnp.log(row_total)
    probs_low = (shifted / row_total).astype(jnp.bfloat16)
    mixed = jnp.einsum("bhqk,bkhd->bqhd", probs_low, all_values, preferred_element_type=jnp.float32)
    mixed_low = mixed.reshape(n_images, local_tokens, model_width).astype(jnp.bfloat16)
    stream_one = token_rows + (
        jnp.einsum("bte,ef->btf", mixed_low, full_out, preferred_element_type=jnp.float32)
        + bias_out
    )
    normed_two, pull_two = jax.vjp(norm_rows, stream_one, gain_two, shift_two)
    normed_two_low = normed_two.astype(jnp.bfloat16)
    hidden = (
        jnp.einsum("bte,em->btm", normed_two_low, full_up, preferred_element_type=jnp.float32)
        + bias_up
    )
    activated, pull_act = jax.vjp(jax.nn.gelu, hidden)
    activated_low = activated.astype(jnp.bfloat16)
    stream_two = stream_one + (
        jnp.einsum("btm,me->bte", activated_low, full_down, preferred_element_type=jnp.float32)
        + bias_down
    )
    surface = stream_two.astype(jnp.bfloat16).reshape(n_images, half_rows, grid_cols, model_width)
    extended = extended_2(surface, (("tile", 1),), 1)
    padded = jnp.pad(extended, ((0, 0), (0, 0), (1, 1), (0, 0)))
    pixels = bias_conv
    for row_off in range(3):
        for col_off in range(3):
            window = padded[:, row_off : row_off + half_rows, col_off : col_off + grid_cols]
            pixels = pixels + jnp.einsum(
                "brce,ef->brcf",
                window,
                full_conv[3 * row_off + col_off],
                preferred_element_type=jnp.float32,
            )
    conv_terms = []
    for row_off in range(3):
        for col_off in range(3):
            window = padded[:, row_off : row_off + half_rows, col_off : col_off + grid_cols]
            conv_terms.append(
                jnp.einsum("brce,brcf->ef", window, d_pixels, preferred_element_type=jnp.float32)
            )
    grad_w_conv = jnp.stack(conv_terms)
    grad_bias_conv = jnp.sum(d_pixels.astype(jnp.float32), axis=(0, 1, 2))
    cot_ext = extended_2(d_pixels, (("tile", 1),), 1)
    cot_pad = jnp.pad(cot_ext, ((0, 0), (0, 0), (1, 1), (0, 0)))
    d_surface = jnp.zeros((n_images, half_rows, grid_cols, model_width), jnp.float32)
    for row_off in range(3):
        for col_off in range(3):
            window = cot_pad[
                :, 2 - row_off : 2 - row_off + half_rows, 2 - col_off : 2 - col_off + grid_cols
            ]
            d_surface = d_surface + jnp.einsum(
                "brcf,ef->brce",
                window,
                back_conv[3 * row_off + col_off],
                preferred_element_type=jnp.float32,
            )
    d_stream_two = d_surface.reshape(n_images, local_tokens, model_width)
    branch_two = d_stream_two.astype(jnp.bfloat16)
    grad_w_down = jnp.einsum(
        "btm,bte->me", activated_low, branch_two, preferred_element_type=jnp.float32
    )
    grad_bias_down = jnp.sum(branch_two.astype(jnp.float32), axis=(0, 1))
    d_activated = jnp.einsum(
        "bte,me->btm", branch_two, back_down, preferred_element_type=jnp.float32
    )
    (d_hidden,) = pull_act(d_activated)
    d_hidden_low = d_hidden.astype(jnp.bfloat16)
    grad_w_up = jnp.einsum(
        "bte,btm->em", normed_two_low, d_hidden_low, preferred_element_type=jnp.float32
    )
    grad_bias_up = jnp.sum(d_hidden_low.astype(jnp.float32), axis=(0, 1))
    d_normed_two = jnp.einsum(
        "btm,em->bte", d_hidden_low, back_up, preferred_element_type=jnp.float32
    )
    d_from_two, grad_gain_two, grad_shift_two = pull_two(d_normed_two)
    d_stream_one = d_stream_two + d_from_two
    branch_one = d_stream_one.astype(jnp.bfloat16)
    grad_w_out = jnp.einsum(
        "bte,btf->ef", mixed_low, branch_one, preferred_element_type=jnp.float32
    )
    grad_bias_out = jnp.sum(branch_one.astype(jnp.float32), axis=(0, 1))
    d_mixed = jnp.einsum("btf,ef->bte", branch_one, back_out, preferred_element_type=jnp.float32)
    d_mixed = d_mixed.astype(jnp.bfloat16).reshape(n_images, local_tokens, HEADS, -1)
    scores_again = (
        jnp.einsum("bqhd,bkhd->bhqk", queries, all_keys, preferred_element_type=jnp.float32) * scale
    )
    probs_again = jnp.exp(scores_again - log_total)
    d_probs = jnp.einsum("bqhd,bkhd->bhqk", d_mixed, all_values, preferred_element_type=jnp.float32)
    inner = jnp.sum(probs_again * d_probs, axis=-1, keepdims=True)
    d_scores = (probs_again * (d_probs - inner)).astype(jnp.bfloat16)
    d_queries = (
        jnp.einsum("bhqk,bkhd->bqhd", d_scores, all_keys, preferred_element_type=jnp.float32)
        * scale
    )
    d_keys_all = (
        jnp.einsum("bhqk,bqhd->bkhd", d_scores, queries, preferred_element_type=jnp.float32) * scale
    )
    d_values_all = jnp.einsum(
        "bhqk,bqhd->bkhd",
        probs_again.astype(jnp.bfloat16),
        d_mixed,
        preferred_element_type=jnp.float32,
    )
    d_keys, d_values = (
        lax.psum_scatter(
            d_keys_all.astype(jnp.bfloat16), "tile", scatter_dimension=1, tiled=True
        ).astype(jnp.float32),
        lax.psum_scatter(
            d_values_all.astype(jnp.bfloat16), "tile", scatter_dimension=1, tiled=True
        ).astype(jnp.float32),
    )
    d_joined = jnp.stack([d_queries, d_keys, d_values], axis=2).astype(jnp.bfloat16)
    d_joined = d_joined.reshape(n_images, local_tokens, 3 * model_width)
    grad_w_qkv = jnp.einsum("bte,btf->ef", normed_low, d_joined, preferred_element_type=jnp.float32)
    joined_sums = jnp.sum(d_joined.astype(jnp.float32), axis=(0, 1))
    grad_bias_q = joined_sums[:model_width]
    grad_bias_v = joined_sums[2 * model_width :]
    d_normed_one = jnp.einsum("btf,ef->bte", d_joined, back_qkv, preferred_element_type=jnp.float32)
    d_from_one, grad_gain_one, grad_shift_one = pull_one(d_normed_one)
    grad_embed = (d_stream_one + d_from_one).reshape(n_images, half_rows, grid_cols, model_width)
    sum_qkv, sum_out, sum_up, sum_down, sum_conv = scatter_grads(
        *[grad.astype(jnp.bfloat16) for grad in (grad_w_qkv, grad_w_out, grad_w_up, grad_w_down, grad_w_conv)]
    )
    (
        sum_bias_q,
        sum_bias_v,
        sum_bias_out,
        sum_gain_one,
        sum_shift_one,
        sum_gain_two,
        sum_shift_two,
        sum_bias_up,
        sum_bias_down,
        sum_bias_conv,
    ) = lax.psum(
        (
            grad_bias_q,
            grad_bias_v,
            grad_bias_out,
            grad_gain_one,
            grad_shift_one,
            grad_gain_two,
            grad_shift_two,
            grad_bias_up,
            grad_bias_down,
            grad_bias_conv,
        ),
        ("img", "tile"),
    )
    return (
        pixels,
        grad_embed,
        sum_qkv,
        sum_bias_q,
        sum_bias_v,
        sum_out,
        sum_bias_out,
        sum_gain_one,
        sum_shift_one,
        sum_gain_two,
        sum_shift_two,
        sum_up,
        sum_bias_up,
        sum_down,
        sum_bias_down,
        sum_conv,
        sum_bias_conv,
    )


def solution(mesh):
    placed = (
        P("img", "tile", None),
        P("img", None),
        P("img", None),
        P(),
        P(),
        P("img", None),
        P(),
        P(),
        P(),
        P(),
        P(),
        P("img", None),
        P(),
        P("img", None),
        P(),
        P(None, "img", None),
        P(),
        P("img", "tile", None, None),
    )
    return jax.shard_map(
        fast_shards if dict(mesh.shape) == {"img": 16, "tile": 2} else shards,
        mesh=mesh,
        in_specs=placed,
        out_specs=(
            P("img", "tile", None, None),
            P("img", "tile", None, None),
            P("img", None),
            P(),
            P(),
            P("img", None),
            P(),
            P(),
            P(),
            P(),
            P(),
            P("img", None),
            P(),
            P("img", None),
            P(),
            P(None, "img", None),
            P(),
        ),
        check_vma=False,
    )
```

```python
import functools
import math

import jax
import jax.numpy as jnp
from jax import lax
from jax.experimental import pallas as pl
from jax.experimental.pallas import tpu as pltpu
from jax.sharding import PartitionSpec as P

HEADS = 12


EPS = 1e-06


def extended_2(block, sides, width):
    for axis, dim in sides:
        count = lax.axis_size(axis)
        forward = [(i, i + 1) for i in range(count - 1)]
        backward = [(target, source) for source, target in forward]
        low = lax.ppermute(
            lax.slice_in_dim(block, block.shape[dim] - width, None, axis=dim), axis, forward
        )
        high = lax.ppermute(lax.slice_in_dim(block, 0, width, axis=dim), axis, backward)
        block = jnp.concatenate([low, block, high], axis=dim)
    return block


def norm_rows(values, gain, shift):
    center = values - jnp.mean(values, axis=-1, keepdims=True)
    spread = jnp.mean(center * center, axis=-1, keepdims=True)
    return center * lax.rsqrt(spread + EPS) * gain + shift


def shards(
    indices,
    embed_table,
    w_qkv,
    bias_q,
    bias_v,
    w_out,
    bias_out,
    gain_one,
    shift_one,
    gain_two,
    shift_two,
    w_up,
    bias_up,
    w_down,
    bias_down,
    w_conv,
    bias_conv,
    d_pixels,
):
    n_images, half_rows, grid_cols = indices.shape
    vocab_rows, model_width = embed_table.shape
    n_img = lax.axis_size("img")
    local_tokens = half_rows * grid_cols
    all_tokens = n_images * local_tokens
    capacity = max(2, 2 * all_tokens // n_img)
    flat_ids = indices.reshape(all_tokens)
    owner_dev = flat_ids // vocab_rows
    within = flat_ids - owner_dev * vocab_rows
    hits = (owner_dev[:, None] == jnp.arange(n_img, dtype=jnp.int32)[None, :]).astype(jnp.int32)
    slot_rank = jnp.sum((jnp.cumsum(hits, axis=0) - hits) * hits, axis=1)
    slot_index = owner_dev * capacity + slot_rank
    requests = (
        jnp.zeros((n_img * capacity,), jnp.int32)
        .at[slot_index]
        .set(within)
        .reshape(n_img, capacity)
    )
    found = jnp.take(
        embed_table,
        lax.all_to_all(requests, "img", split_axis=0, concat_axis=0, tiled=True),
        axis=0,
    )
    answers = lax.all_to_all(found, "img", split_axis=0, concat_axis=0, tiled=True)
    embedded = jnp.take(answers.reshape(n_img * capacity, model_width), slot_index, axis=0)
    token_rows = embedded.astype(jnp.float32).reshape(n_images, local_tokens, model_width)
    full_qkv, full_out, full_up, full_down, full_conv = (
        lax.all_gather(w_qkv, "img", axis=0, tiled=True),
        lax.all_gather(w_out, "img", axis=0, tiled=True),
        lax.all_gather(w_up, "img", axis=0, tiled=True),
        lax.all_gather(w_down, "img", axis=0, tiled=True),
        lax.all_gather(w_conv, "img", axis=1, tiled=True),
    )
    normed_one, pull_one = jax.vjp(norm_rows, token_rows, gain_one, shift_one)
    normed_low = normed_one.astype(jnp.bfloat16)
    zeros_k = jnp.zeros_like(bias_q)
    joined = jnp.einsum("bte,ef->btf", normed_low, full_qkv, preferred_element_type=jnp.float32)
    joined = joined + jnp.concatenate([bias_q, zeros_k, bias_v])
    joined_low = joined.astype(jnp.bfloat16).reshape(n_images, local_tokens, 3, HEADS, -1)
    queries = joined_low[:, :, 0]
    own_keys = joined_low[:, :, 1]
    own_values = joined_low[:, :, 2]
    all_keys, all_values = (
        lax.all_gather(own_keys, "tile", axis=1, tiled=True),
        lax.all_gather(own_values, "tile", axis=1, tiled=True),
    )
    scale = 1.0 / math.sqrt(queries.shape[-1])
    scores = (
        jnp.einsum("bqhd,bkhd->bhqk", queries, all_keys, preferred_element_type=jnp.float32) * scale
    )
    row_max = jnp.max(scores, axis=-1, keepdims=True)
    shifted = jnp.exp(scores - row_max)
    row_total = jnp.sum(shifted, axis=-1, keepdims=True)
    log_total = row_max + jnp.log(row_total)
    probs_low = (shifted / row_total).astype(jnp.bfloat16)
    mixed = jnp.einsum("bhqk,bkhd->bqhd", probs_low, all_values, preferred_element_type=jnp.float32)
    mixed_low = mixed.reshape(n_images, local_tokens, model_width).astype(jnp.bfloat16)
    stream_one = token_rows + (
        jnp.einsum("bte,ef->btf", mixed_low, full_out, preferred_element_type=jnp.float32)
        + bias_out
    )
    normed_two, pull_two = jax.vjp(norm_rows, stream_one, gain_two, shift_two)
    normed_two_low = normed_two.astype(jnp.bfloat16)
    hidden = (
        jnp.einsum("bte,em->btm", normed_two_low, full_up, preferred_element_type=jnp.float32)
        + bias_up
    )
    activated, pull_act = jax.vjp(jax.nn.gelu, hidden)
    activated_low = activated.astype(jnp.bfloat16)
    stream_two = stream_one + (
        jnp.einsum("btm,me->bte", activated_low, full_down, preferred_element_type=jnp.float32)
        + bias_down
    )
    surface = stream_two.astype(jnp.bfloat16).reshape(n_images, half_rows, grid_cols, model_width)
    extended = extended_2(surface, (("tile", 1),), 1)
    padded = jnp.pad(extended, ((0, 0), (0, 0), (1, 1), (0, 0)))
    pixels = bias_conv
    for row_off in range(3):
        for col_off in range(3):
            window = padded[:, row_off : row_off + half_rows, col_off : col_off + grid_cols]
            pixels = pixels + jnp.einsum(
                "brce,ef->brcf",
                window,
                full_conv[3 * row_off + col_off],
                preferred_element_type=jnp.float32,
            )
    back_qkv, back_out, back_up, back_down, back_conv = (
        lax.all_gather(w_qkv, "img", axis=0, tiled=True),
        lax.all_gather(w_out, "img", axis=0, tiled=True),
        lax.all_gather(w_up, "img", axis=0, tiled=True),
        lax.all_gather(w_down, "img", axis=0, tiled=True),
        lax.all_gather(w_conv, "img", axis=1, tiled=True),
    )
    conv_terms = []
    for row_off in range(3):
        for col_off in range(3):
            window = padded[:, row_off : row_off + half_rows, col_off : col_off + grid_cols]
            conv_terms.append(
                jnp.einsum("brce,brcf->ef", window, d_pixels, preferred_element_type=jnp.float32)
            )
    grad_w_conv = jnp.stack(conv_terms)
    grad_bias_conv = jnp.sum(d_pixels.astype(jnp.float32), axis=(0, 1, 2))
    cot_ext = extended_2(d_pixels, (("tile", 1),), 1)
    cot_pad = jnp.pad(cot_ext, ((0, 0), (0, 0), (1, 1), (0, 0)))
    d_surface = jnp.zeros((n_images, half_rows, grid_cols, model_width), jnp.float32)
    for row_off in range(3):
        for col_off in range(3):
            window = cot_pad[
                :, 2 - row_off : 2 - row_off + half_rows, 2 - col_off : 2 - col_off + grid_cols
            ]
            d_surface = d_surface + jnp.einsum(
                "brcf,ef->brce",
                window,
                back_conv[3 * row_off + col_off],
                preferred_element_type=jnp.float32,
            )
    d_stream_two = d_surface.reshape(n_images, local_tokens, model_width)
    branch_two = d_stream_two.astype(jnp.bfloat16)
    grad_w_down = jnp.einsum(
        "btm,bte->me", activated_low, branch_two, preferred_element_type=jnp.float32
    )
    grad_bias_down = jnp.sum(branch_two.astype(jnp.float32), axis=(0, 1))
    d_activated = jnp.einsum(
        "bte,me->btm", branch_two, back_down, preferred_element_type=jnp.float32
    )
    (d_hidden,) = pull_act(d_activated)
    d_hidden_low = d_hidden.astype(jnp.bfloat16)
    grad_w_up = jnp.einsum(
        "bte,btm->em", normed_two_low, d_hidden_low, preferred_element_type=jnp.float32
    )
    grad_bias_up = jnp.sum(d_hidden_low.astype(jnp.float32), axis=(0, 1))
    d_normed_two = jnp.einsum(
        "btm,em->bte", d_hidden_low, back_up, preferred_element_type=jnp.float32
    )
    d_from_two, grad_gain_two, grad_shift_two = pull_two(d_normed_two)
    d_stream_one = d_stream_two + d_from_two
    branch_one = d_stream_one.astype(jnp.bfloat16)
    grad_w_out = jnp.einsum(
        "bte,btf->ef", mixed_low, branch_one, preferred_element_type=jnp.float32
    )
    grad_bias_out = jnp.sum(branch_one.astype(jnp.float32), axis=(0, 1))
    d_mixed = jnp.einsum("btf,ef->bte", branch_one, back_out, preferred_element_type=jnp.float32)
    d_mixed = d_mixed.astype(jnp.bfloat16).reshape(n_images, local_tokens, HEADS, -1)
    scores_again = (
        jnp.einsum("bqhd,bkhd->bhqk", queries, all_keys, preferred_element_type=jnp.float32) * scale
    )
    probs_again = jnp.exp(scores_again - log_total)
    d_probs = jnp.einsum("bqhd,bkhd->bhqk", d_mixed, all_values, preferred_element_type=jnp.float32)
    inner = jnp.sum(probs_again * d_probs, axis=-1, keepdims=True)
    d_scores = (probs_again * (d_probs - inner)).astype(jnp.bfloat16)
    d_queries = (
        jnp.einsum("bhqk,bkhd->bqhd", d_scores, all_keys, preferred_element_type=jnp.float32)
        * scale
    )
    d_keys_all = (
        jnp.einsum("bhqk,bqhd->bkhd", d_scores, queries, preferred_element_type=jnp.float32) * scale
    )
    d_values_all = jnp.einsum(
        "bhqk,bqhd->bkhd",
        probs_again.astype(jnp.bfloat16),
        d_mixed,
        preferred_element_type=jnp.float32,
    )
    d_keys, d_values = (
        lax.psum_scatter(
            d_keys_all.astype(jnp.bfloat16), "tile", scatter_dimension=1, tiled=True
        ).astype(jnp.float32),
        lax.psum_scatter(
            d_values_all.astype(jnp.bfloat16), "tile", scatter_dimension=1, tiled=True
        ).astype(jnp.float32),
    )
    d_joined = jnp.stack([d_queries, d_keys, d_values], axis=2).astype(jnp.bfloat16)
    d_joined = d_joined.reshape(n_images, local_tokens, 3 * model_width)
    grad_w_qkv = jnp.einsum("bte,btf->ef", normed_low, d_joined, preferred_element_type=jnp.float32)
    joined_sums = jnp.sum(d_joined.astype(jnp.float32), axis=(0, 1))
    grad_bias_q = joined_sums[:model_width]
    grad_bias_v = joined_sums[2 * model_width :]
    d_normed_one = jnp.einsum("btf,ef->bte", d_joined, back_qkv, preferred_element_type=jnp.float32)
    d_from_one, grad_gain_one, grad_shift_one = pull_one(d_normed_one)
    grad_embed = (d_stream_one + d_from_one).reshape(n_images, half_rows, grid_cols, model_width)
    part_qkv, part_out, part_up, part_down, part_conv = (
        lax.psum_scatter(grad_w_qkv, "img", scatter_dimension=0, tiled=True),
        lax.psum_scatter(grad_w_out, "img", scatter_dimension=0, tiled=True),
        lax.psum_scatter(grad_w_up, "img", scatter_dimension=0, tiled=True),
        lax.psum_scatter(grad_w_down, "img", scatter_dimension=0, tiled=True),
        lax.psum_scatter(grad_w_conv, "img", scatter_dimension=1, tiled=True),
    )
    sum_qkv, sum_out, sum_up, sum_down, sum_conv = (
        lax.psum(part_qkv.astype(jnp.bfloat16), "tile").astype(jnp.float32),
        lax.psum(part_out.astype(jnp.bfloat16), "tile").astype(jnp.float32),
        lax.psum(part_up.astype(jnp.bfloat16), "tile").astype(jnp.float32),
        lax.psum(part_down.astype(jnp.bfloat16), "tile").astype(jnp.float32),
        lax.psum(part_conv.astype(jnp.bfloat16), "tile").astype(jnp.float32),
    )
    (
        sum_bias_q,
        sum_bias_v,
        sum_bias_out,
        sum_gain_one,
        sum_shift_one,
        sum_gain_two,
        sum_shift_two,
        sum_bias_up,
        sum_bias_down,
        sum_bias_conv,
    ) = lax.psum(
        (
            grad_bias_q,
            grad_bias_v,
            grad_bias_out,
            grad_gain_one,
            grad_shift_one,
            grad_gain_two,
            grad_shift_two,
            grad_bias_up,
            grad_bias_down,
            grad_bias_conv,
        ),
        ("img", "tile"),
    )
    return (
        pixels,
        grad_embed,
        sum_qkv,
        sum_bias_q,
        sum_bias_v,
        sum_out,
        sum_bias_out,
        sum_gain_one,
        sum_shift_one,
        sum_gain_two,
        sum_shift_two,
        sum_up,
        sum_bias_up,
        sum_down,
        sum_bias_down,
        sum_conv,
        sum_bias_conv,
    )


class Tag:
    def __getattr__(self, name):
        return name


tag = Tag()
MESH = pl.DeviceIdType.MESH
F32, BF16 = jnp.float32, jnp.bfloat16
DIM, TOKENS, SLOTS = 768, 512, 64
UNITS = 21
QKV, OUT, UP, DOWN, CONV = 0, 3, 4, 8, 12
EVERY = slice(None)


def aligned(start, unit=128):
    return start if isinstance(start, int) else pl.multiple_of(start, unit)


def cols(start, width=256):
    return pl.ds(aligned(start), width)


def place():
    img, tile = lax.axis_index("img"), lax.axis_index("tile")
    return img // 4, lax.rem(img // 2, 2), lax.rem(img, 2), tile


def device(z, y, c, x):
    return (z * 4 + y * 2 + c, x)


def neighbours():
    z, y, c, x = place()
    turn = [device(lax.rem(z + step, 4), y, c, x) for step in (1, 2, 3)]
    return turn, device(z, 1 - y, c, x), device(z, y, c, 1 - x), device(z, y, 1 - c, x)


def remote(src, dst, send, recv, dev):
    return pltpu.make_async_remote_copy(
        src_ref=src, dst_ref=dst, send_sem=send, recv_sem=recv, device_id=dev, device_id_type=MESH
    )


def within(number, count):
    return (number >= 0) & (number < count)


def nt_dot(a, b):
    return lax.dot_general(a, b, (((1,), (1,)), ((), ())), preferred_element_type=F32)


def tn_dot(a, b):
    return lax.dot_general(a, b, (((0,), (0,)), ((), ())), preferred_element_type=F32)


def dot(a, b):
    return jnp.dot(a, b, preferred_element_type=F32)


class Gather:
    LAG = (0, 2, 4, 6, 7, 8)
    TURN = (0, 1, 2, 3, 4, 5)

    def __init__(self, shards, full, send, recv, local):
        self.shards, self.full, self.send, self.recv, self.local = shards, full, send, recv, local
        z, y, c, x = place()
        self.z, self.y, self.c, self.x = z, y, c, x
        self.turn, self.dev_y, self.dev_x, self.dev_c = neighbours()
        self.most = (256 * x, 512)
        self.mine = (512 * x, 256)
        self.theirs = (512 - 512 * x, 256)
        self.now = [0, 0]
        self.done = 0

    def at(self, u, z, y, c, columns):
        return self.full.at[u, z, y, c, :, cols(*columns)]

    def hop(self, u, slot, z, y, c, columns, dev):
        ref = self.at(u, z, y, c, columns)
        return remote(ref, ref, self.send.at[u, slot], self.recv.at[u, slot], dev)

    def own(self, u):
        return pltpu.make_async_copy(
            self.shards.at[u, :, cols(*self.most)], self.at(u, self.z, self.y, self.c, self.most), self.local.at[u]
        )

    def along_z(self, u, turn):
        ref = self.shards.at[u, :, cols(*self.most)]
        there = self.at(u, self.z, self.y, self.c, self.most)
        return remote(ref, there, self.send.at[u, turn], self.recv.at[u, turn], self.turn[turn])

    def came_z(self, u, turn):
        ref = self.at(u, lax.rem(self.z + 3 - turn, 4), self.y, self.c, self.most)
        return remote(ref, ref, self.send.at[u, turn], self.recv.at[u, turn], self.turn[turn])

    def along_y(self, u, came=False):
        return self.hop(u, 6, EVERY, 1 - self.y if came else self.y, self.c, self.most, self.dev_y)

    def along_x(self, u, n, came=False):
        y = 1 - self.y if n else self.y
        return self.hop(u, 7 + n, EVERY, y, self.c, self.theirs if came else self.mine, self.dev_x)

    def to_core(self, u, n, came=False):
        c = 1 - self.c if came else self.c
        if n == 2:
            return self.hop(u, 11, EVERY, EVERY, c, self.theirs, self.dev_c)
        return self.hop(u, 9 + n, EVERY, 1 - self.y if n else self.y, c, self.most, self.dev_c)

    def stage(self, u, step):
        if step == 0:
            self.own(u).start()
            for turn in range(3):
                self.along_z(u, turn).start()
        if step == 1:
            self.own(u).wait()
            for turn in range(3):
                self.came_z(u, turn).wait_recv()
            self.along_y(u).start()
            self.along_x(u, 0).start()
            self.to_core(u, 0).start()
        if step == 2:
            self.along_y(u, True).wait_recv()
            self.along_x(u, 1).start()
            self.to_core(u, 1).start()
        if step == 3:
            self.along_x(u, 0, True).wait_recv()
            self.along_x(u, 1, True).wait_recv()
            self.to_core(u, 2).start()
        if step == 4:
            for n in range(3):
                self.to_core(u, n, True).wait_recv()
        if step == 5:
            for turn in range(3):
                self.along_z(u, turn).wait_send()
            self.along_y(u).wait_send()
            for n in (0, 1):
                self.along_x(u, n).wait_send()
            for n in range(3):
                self.to_core(u, n).wait_send()

    def step(self, count=1):
        while count > 0:
            if self.now[0] >= UNITS + self.LAG[5]:
                return
            stage = self.TURN[self.now[1]]
            u = self.now[0] - self.LAG[stage]
            if 0 <= u < UNITS:
                self.stage(u, stage)
                count -= 1
                if stage == 4:
                    self.done = u + 1
            self.now[1] += 1
            if self.now[1] == 6:
                self.now = [self.now[0] + 1, 0]

    def until(self, u):
        while self.done <= u:
            self.step()

    def round(self, tick, turns):
        for turn in turns:
            stage = self.TURN[turn]
            u = tick - self.LAG[stage]

            @pl.when(within(u, UNITS))
            def _(u=u, stage=stage):
                self.stage(u, stage)


def gelu_both(value):
    inner = 0.7978845608028654 * (value + 0.044715 * value * value * value)
    bend = jnp.tanh(inner)
    slope = 0.7978845608028654 * (1.0 + 3 * 0.044715 * value * value)
    half = 0.5 * (1.0 + bend)
    return value * half, half + 0.5 * value * (1.0 - bend * bend) * slope


def normed(value, gain, shift):
    center = value - jnp.mean(value, axis=-1, keepdims=True)
    spread = jnp.mean(center * center, axis=-1, keepdims=True)
    return center * lax.rsqrt(spread + EPS) * gain + shift


def shifted_copies(out):
    @pl.loop(0, 4)
    def _(b):
        value = out[1, b].astype(F32)
        column = lax.rem(lax.broadcasted_iota(jnp.int32, value.shape, 0), 16)
        rows = value.shape[0]
        out[0, b] = jnp.where(column == 0, 0.0, pltpu.roll(value, 1, axis=0)).astype(BF16)
        out[2, b] = jnp.where(column == 15, 0.0, pltpu.roll(value, rows - 1, axis=0)).astype(BF16)


FORWARD_IN = (
    [tag.indices, tag.table, tag.d_pixels, tag.bias_q, tag.bias_v, tag.bias_out, tag.gain_one, tag.shift_one]
    + [tag.gain_two, tag.shift_two, tag.bias_up, tag.bias_down, tag.shards]
)
KEPT = {
    tag.emb: ((TOKENS, DIM), BF16),
    tag.normed_one: ((TOKENS, DIM), BF16),
    tag.q: ((TOKENS, DIM), BF16),
    tag.keys: ((4, 256, DIM), BF16),
    tag.values: ((4, 256, DIM), BF16),
    tag.mixed: ((TOKENS, DIM), BF16),
    tag.stream_one: ((TOKENS, DIM), F32),
    tag.normed_two: ((TOKENS, DIM), BF16),
    tag.act: ((4, TOKENS, DIM), BF16),
    tag.slope: ((4, TOKENS, DIM), BF16),
    tag.d_two: ((TOKENS, DIM), F32),
    tag.surface: ((4, 128, DIM), BF16),
    tag.q_x: ((TOKENS, DIM), BF16),
}
FORWARD_OUT = {
    tag.full: ((UNITS, 4, 2, 2, 48, DIM), BF16),
    tag.grad_conv: ((9, 4, 2, 2, 48, DIM), BF16),
    **{tag.kept_ + name: kind for name, kind in KEPT.items()},
}
FORWARD_SCRATCH = {
    **KEPT,
    tag.ids: ((8, TOKENS), jnp.int32),
    tag.ids_all: ((16, 8, TOKENS), jnp.int32),
    tag.bias_qkv: ((3, DIM), F32),
    tag.onehot: None,
    tag.rows_out: ((16, SLOTS, DIM), BF16),
    tag.answers: ((16, SLOTS, DIM), BF16),
    tag.slot: ((TOKENS, 8), F32),
    tag.normed_x: ((TOKENS, DIM), BF16),
    tag.w_qkv: ((3, DIM, DIM), BF16),
    tag.w_out: ((DIM, DIM), BF16),
    tag.w_up: ((4, DIM, DIM), BF16),
    tag.w_down: ((16, 4, 48, DIM), BF16),
    tag.w_conv: ((2, DIM, DIM), BF16),
    tag.halo_cot: ((4, 16, DIM), BF16),
    tag.cot: ((3, 4, 160, DIM), BF16),
    tag.made: ((2, DIM, DIM), BF16),
}
FORWARD_SEMS = {
    tag.g_send: (UNITS, 12),
    tag.g_recv: (UNITS, 12),
    tag.g_local: (UNITS,),
    tag.load: (UNITS,),
    tag.ids_send: (16,),
    tag.ids_recv: (16,),
    tag.rows_send: (16,),
    tag.rows_recv: (16,),
    tag.x_send: (2,),
    tag.x_recv: (2,),
    tag.keep: (len(KEPT),),
    tag.made_sem: (9,),
}


class Refs:
    def __init__(self, names, refs):
        self.__dict__.update(dict(zip(names, refs)))


def extend(ext, own, halo, x):
    nothing = jnp.zeros((4, 16, DIM), BF16)
    came = halo[...]
    ext[1, :, 0:16] = jnp.where(x == 1, came, nothing)
    ext[1, :, 16:144] = own[...]
    ext[1, :, 144:160] = jnp.where(x == 0, came, nothing)
    shifted_copies(ext)


def forward_kernel(vocab, *refs):
    k = Refs(FORWARD_IN + list(FORWARD_OUT) + list(FORWARD_SCRATCH) + list(FORWARD_SEMS), refs)
    z, y, c, x = place()
    me = z * 4 + y * 2 + c
    turn, dev_y, dev_x, dev_c = neighbours()
    barrier = pltpu.get_barrier_semaphore()

    @pl.loop(1, 16)
    def _(step):
        pl.semaphore_signal(barrier, inc=1, device_id=(lax.rem(me + step, 16), x), device_id_type=MESH)

    pl.semaphore_signal(barrier, inc=1, device_id=dev_x, device_id_type=MESH)
    pl.semaphore_wait(barrier, 16)

    gather = Gather(k.shards, k.full, k.g_send, k.g_recv, k.g_local)

    def ids_copy(step):
        return remote(k.ids, k.ids_all.at[me], k.ids_send.at[step], k.ids_recv.at[me], (lax.rem(me + step, 16), x))

    def ids_came(step):
        there = lax.rem(me + 16 - step, 16)
        return remote(k.ids, k.ids_all.at[there], k.ids_send.at[step], k.ids_recv.at[there], (there, x))

    def rows_copy(step):
        there = lax.rem(me + step, 16)
        return remote(k.rows_out.at[there], k.answers.at[me], k.rows_send.at[step], k.rows_recv.at[me], (there, x))

    def rows_came(step):
        there = lax.rem(me + 16 - step, 16)
        return remote(k.rows_out.at[there], k.answers.at[there], k.rows_send.at[step], k.rows_recv.at[there], (there, x))

    grid = jnp.concatenate([k.indices[b] for b in range(4)], axis=0).astype(F32)
    spread = (
        lax.broadcasted_iota(jnp.int32, (16, TOKENS), 0)
        == lax.rem(lax.broadcasted_iota(jnp.int32, (16, TOKENS), 1), 16)
    ).astype(F32)
    wide = jnp.dot(grid, spread, precision=lax.Precision.HIGHEST, preferred_element_type=F32)
    line = lax.broadcasted_iota(jnp.int32, (32, TOKENS), 1) // 16
    wide = jnp.where(line == lax.broadcasted_iota(jnp.int32, (32, TOKENS), 0), wide, 0.0)
    ids = jnp.broadcast_to(jnp.sum(wide, axis=0, keepdims=True), (8, TOKENS)).astype(jnp.int32)
    k.ids[...] = ids

    @pl.loop(1, 16)
    def _(step):
        ids_copy(step).start()

    gather.step(3)
    edge = pl.ds(aligned(112 - 112 * x, 16), 16)
    halo_cot = remote(k.d_pixels.at[:, edge], k.halo_cot, k.x_send.at[0], k.x_recv.at[0], dev_x)
    halo_cot.start()
    k.bias_qkv[0:1] = k.bias_q[...].reshape(1, DIM)
    k.bias_qkv[1:2] = jnp.zeros((1, DIM), F32)
    k.bias_qkv[2:3] = k.bias_v[...].reshape(1, DIM)

    k.ids_all[me] = k.ids[...]
    before = (
        lax.broadcasted_iota(jnp.int32, (TOKENS, TOKENS), 0) < lax.broadcasted_iota(jnp.int32, (TOKENS, TOKENS), 1)
    ).astype(F32).astype(BF16)
    block = vocab


    @pl.loop(1, 16)
    def _(step):
        ids_came(step).wait_recv()

    asked = k.ids_all[:, 0, :] - vocab * me
    hit = (asked >= 0) & (asked < vocab)
    rank = dot(hit.astype(F32).astype(BF16), before)
    rank = jnp.where(hit, rank, -1.0)
    asked = jnp.where(hit, asked, 0).astype(F32)
    slots = lax.broadcasted_iota(jnp.int32, (SLOTS, TOKENS), 0).astype(F32)
    entries = lax.broadcasted_iota(jnp.int32, (SLOTS, block), 1).astype(F32)
    for d in range(16):
        entry = jnp.sum(jnp.where(slots == rank[d : d + 1], asked[d : d + 1], 0.0), axis=1, keepdims=True)
        k.onehot[SLOTS * d : SLOTS * d + SLOTS] = (entries == entry).astype(F32).astype(BF16)

    @pl.loop(0, 3)
    def _(nb):
        rows = dot(k.onehot[...], k.table[:, cols(256 * nb)]).astype(BF16)
        k.rows_out[:, :, cols(256 * nb)] = rows.reshape(16, SLOTS, 256)

    @pl.loop(1, 16)
    def _(step):
        rows_copy(step).start()

    k.answers[me] = k.rows_out[me]
    first = lax.broadcasted_iota(jnp.int32, (16, TOKENS), 0)
    own = (ids[0:1] >= vocab * first) & (ids[0:1] < vocab * (first + 1))
    rank = dot(own.astype(F32).astype(BF16), before)
    slot = jnp.sum(jnp.where(own, rank + (SLOTS * first).astype(F32), 0.0), axis=0, keepdims=True)
    k.slot[...] = jnp.broadcast_to(slot, (8, TOKENS)).T

    gather.step(EARLY[0])
    halo_cot.wait_recv()
    extend(k.cot, k.d_pixels, k.halo_cot, x)
    gather.step(EARLY[1])

    @pl.loop(1, 16)
    def _(step):
        rows_came(step).wait_recv()

    @pl.loop(0, 4)
    def _(b):
        rows = pl.ds(pl.multiple_of(b * 128, 128), 128)
        choice = (
            (lax.broadcasted_iota(jnp.int32, (128, 16 * SLOTS), 1).astype(F32) == k.slot[rows, 0:1])
            .astype(F32)
            .astype(BF16)
        )
        value = dot(choice, k.answers[...].reshape(16 * SLOTS, DIM))
        k.emb[rows] = value.astype(BF16)
        k.normed_one[rows] = normed(value, k.gain_one[...].reshape(1, DIM), k.shift_one[...].reshape(1, DIM)).astype(BF16)

    normed_x = remote(k.normed_one, k.normed_x, k.x_send.at[1], k.x_recv.at[1], dev_x)
    normed_x.start()

    def keep(name):
        n = list(KEPT).index(name)
        return pltpu.make_async_copy(getattr(k, name), getattr(k, tag.kept_ + name), k.keep.at[n])

    def load(u):
        source = k.full.at[u]
        if isinstance(u, int) and u < DOWN:
            to = k.w_qkv.at[u] if u < OUT else k.w_out if u == OUT else k.w_up.at[u - UP]
            return pltpu.make_async_copy(source.reshape(DIM, DIM), to, k.load.at[u])
        if isinstance(u, int) and u < CONV:
            return pltpu.make_async_copy(source.reshape(16, 48, DIM), k.w_down.at[:, u - DOWN], k.load.at[u])
        return pltpu.make_async_copy(source.reshape(DIM, DIM), k.w_conv.at[lax.rem(u, 2)], k.load.at[u])

    keep(tag.emb).start()
    keep(tag.normed_one).start()
    asked_for = set()

    def steps(count):
        gather.step(count)
        for u in range(min(gather.done, CONV)):
            if u not in asked_for:
                asked_for.add(u)
                load(u).start()

    def ready(u):
        while u not in asked_for:
            steps(1)
        load(u).wait()

    steps(0)
    ready(0)

    def query(into, source):
        @pl.loop(0, 3)
        def _(nb):
            at = cols(256 * nb)
            into[:, at] = (dot(source[...], k.w_qkv[0, :, at]) + k.bias_qkv[0:1, at]).astype(BF16)

    query(k.q, k.normed_one)
    keep(tag.q).start()
    steps(PACE[0])

    def project(into, which, source, start):
        @pl.loop(0, 3)
        def _(nb):
            at = cols(256 * nb)
            value = (dot(source[...], k.w_qkv[which, :, at]) + k.bias_qkv[which : which + 1, at]).astype(BF16)
            into[:, pl.ds(start, 128), at] = value.reshape(4, 128, 256)

    ready(1)
    project(k.keys, 1, k.normed_one, 0)
    steps(PACE[0])
    ready(2)
    project(k.values, 2, k.normed_one, 0)
    steps(PACE[0])
    normed_x.wait_recv()
    project(k.keys, 1, k.normed_x, 128)
    steps(PACE[0])
    project(k.values, 2, k.normed_x, 128)
    keep(tag.keys).start()
    keep(tag.values).start()
    query(k.q_x, k.normed_x)
    keep(tag.q_x).start()
    steps(PACE[0])

    def attend(b):
        rows = pl.ds(aligned(b * 128), 128)
        low = lax.broadcasted_iota(jnp.int32, (128, 128), 1) < 64
        for block in range(6):
            at = slice(128 * block, 128 * block + 128)
            q = k.q[rows, at]
            both = jnp.concatenate([jnp.where(low, q, 0), jnp.where(low, 0, q)], axis=0)
            scores = nt_dot(both, k.keys[b, :, at]) * 0.125
            power = jnp.exp(scores - jnp.max(scores, axis=-1, keepdims=True))
            probs = (power / jnp.sum(power, axis=-1, keepdims=True)).astype(BF16)
            value = dot(probs, k.values[b, :, at])
            k.mixed[rows, at] = jnp.where(low, value[:128], value[128:]).astype(BF16)

    for half in range(2):

        @pl.loop(2 * half, 2 * half + 2)
        def _(b):
            attend(b)

        steps(PACE[1])
    keep(tag.mixed).start()
    ready(OUT)

    @pl.loop(0, 4)
    def _(b):
        rows = pl.ds(pl.multiple_of(b * 128, 128), 128)
        value = k.emb[rows].astype(F32) + (dot(k.mixed[rows], k.w_out[...]) + k.bias_out[...].reshape(1, DIM))
        k.stream_one[rows] = value
        k.normed_two[rows] = normed(value, k.gain_two[...].reshape(1, DIM), k.shift_two[...].reshape(1, DIM)).astype(BF16)

    keep(tag.stream_one).start()
    keep(tag.normed_two).start()
    steps(PACE[2])
    for u in range(4):
        ready(UP + u)

        @pl.loop(0, 3)
        def _(nb):
            at = cols(256 * nb)
            value = dot(k.normed_two[...], k.w_up[u, :, at]) + k.bias_up[cols(256 * nb + DIM * u)].reshape(1, 256)
            act, slope = gelu_both(value)
            k.act[u, :, at] = act.astype(BF16)
            k.slope[u, :, at] = slope.astype(BF16)

        steps(PACE[2])
    keep(tag.act).start()
    keep(tag.slope).start()
    for u in range(DOWN, CONV):
        ready(u)

    @pl.loop(0, 3)
    def _(nb):
        at = cols(256 * nb)
        value = k.bias_down[at].reshape(1, 256)
        for u in range(4):
            value = value + dot(k.act[u], k.w_down[4 * u : 4 * u + 4, :, :, at].reshape(DIM, 256))
        k.surface[:, :, at] = (k.stream_one[:, at] + value).astype(BF16).reshape(4, 128, 256)

    keep(tag.surface).start()
    k.d_two[...] = jnp.zeros_like(k.d_two)
    while gather.now[1] or gather.done <= CONV:
        steps(1)
    start = gather.now[0]
    load(CONV).start()

    def save_made(t):
        return pltpu.make_async_copy(k.made.at[lax.rem(t, 2)], k.grad_conv.at[t].reshape(DIM, DIM), k.made_sem.at[t])

    @pl.loop(0, 9)
    def _(t):
        i, j = t // 3, lax.rem(t, 3)
        slab = pl.ds(pl.multiple_of(16 * (2 - i), 16), 128)
        here = lax.rem(t, 2)
        gather.round(start + t, range(0, 3))

        @pl.when(t >= 2)
        def _():
            save_made(t - 2).wait()

        @pl.loop(0, 3)
        def _(nb):
            at = cols(256 * nb)
            cot = k.cot[2 - j, :, slab, at].reshape(TOKENS, 256)
            k.made[here, :, at] = tn_dot(k.surface[...].reshape(TOKENS, DIM), cot).astype(BF16)

        save_made(t).start()
        gather.round(start + t, range(3, 6))
        load(CONV + t).wait()

        @pl.when(t < 8)
        def _():
            load(CONV + t + 1).start()

        @pl.loop(0, 3)
        def _(nb):
            at = cols(256 * nb)
            k.d_two[:, at] += nt_dot(k.cot[2 - j, :, slab].reshape(TOKENS, DIM), k.w_conv[here, at, :])

    for tick in range(start + 9, UNITS + gather.LAG[5]):
        for step in range(6):
            if 0 <= tick - gather.LAG[step] < UNITS:
                gather.stage(tick - gather.LAG[step], step)
    keep(tag.d_two).start()
    save_made(7).wait()
    save_made(8).wait()
    for name in KEPT:
        keep(name).wait()
    halo_cot.wait_send()
    normed_x.wait_send()

    @pl.loop(1, 16)
    def _(step):
        ids_copy(step).wait_send()
        rows_copy(step).wait_send()


EARLY = (12, 16)
PACE = (5, 5, 5)


def forward_pass(vocab, *args):
    any_space, vmem = pl.BlockSpec(memory_space=pl.ANY), pl.BlockSpec(memory_space=pltpu.VMEM)
    scratch = dict(FORWARD_SCRATCH, onehot=((16 * SLOTS, vocab), BF16))
    outs = pl.pallas_call(
        functools.partial(forward_kernel, vocab),
        out_shape=[jax.ShapeDtypeStruct(*kind) for kind in FORWARD_OUT.values()],
        in_specs=[vmem] * len(FORWARD_IN),
        out_specs=[any_space] * len(FORWARD_OUT),
        scratch_shapes=[pltpu.VMEM(*kind) for kind in scratch.values()]
        + [pltpu.SemaphoreType.DMA(shape) for shape in FORWARD_SEMS.values()],
        compiler_params=pltpu.CompilerParams(
            collective_id=0, has_side_effects=True, vmem_limit_bytes=62 * 2**20
        ),
        name=tag.forward_pass,
    )(*args)
    return dict(zip(FORWARD_OUT, outs))


def packed_shards(w_qkv, w_out, w_up, w_down, w_conv):
    split = lambda value, count: value.reshape(48, count, DIM).transpose(1, 0, 2)
    return jnp.concatenate(
        [split(w_qkv, 3), w_out[None], split(w_up, 4), w_down.reshape(4, 48, DIM), w_conv], axis=0
    )


class Scatter:
    LAG = (0, 1, 3, 5, 7, 8)

    def __init__(self, k):
        self.k = k
        z, y, c, x = place()
        self.z, self.y, self.c, self.x = z, y, c, x
        self.turn, self.dev_y, self.dev_x, self.dev_c = neighbours()
        self.one = (0, 512)
        self.mine = (512 + 128 * x, 128)
        self.theirs = (640 - 128 * x, 128)

    def copy(self, n, slot, src, dst, dev):
        return remote(src, dst, self.k.s_send.at[n, slot], self.k.s_recv.at[n, slot], dev)

    def core(self, n):
        return self.k.core.at[lax.rem(n, CORE_SLOTS)]

    def sent(self, n, name, step=0, source=None):
        k, y, one = self.k, self.y, cols(*self.one)
        there = lax.rem(self.z + step + 1, 4)
        if name == tag.core:
            return self.copy(n, 0, self.core(n) if source is None else source, self.core(n), self.dev_c)
        if name == tag.x:
            return self.copy(n, 1, self.core(n).at[:, :, :, cols(*self.theirs)], k.ax.at[n], self.dev_x)
        if name == tag.y1:
            return self.copy(n, 2, self.core(n).at[:, 1 - y, :, one], k.y_one.at[n], self.dev_y)
        if name == tag.y2:
            return self.copy(n, 3, k.ax.at[n, :, 1 - y], k.y_two.at[n], self.dev_y)
        if name == tag.z1:
            return self.copy(n, 4 + step, k.y_one.at[n, there], k.z_one.at[n, step], self.turn[step])
        if name == tag.z2:
            return self.copy(n, 7 + step, k.y_two.at[n, there], k.z_two.at[n, step], self.turn[step])
        if name == tag.x1:
            return self.copy(n, 10, k.x_one.at[n, 0], k.x_one.at[n, 1], self.dev_x)
        return self.copy(n, 11, k.x_two.at[n, 0], k.x_two.at[n, 1], self.dev_x)

    def load(self, n, source):
        return pltpu.make_async_copy(source, self.k.own.at[lax.rem(n, 3)], self.k.s_local.at[n])

    def open(self, n, partial, index):
        k = self.k

        def go():
            pl.semaphore_wait(k.credit, 1)

        if isinstance(n, int):
            if n >= CORE_SLOTS:
                go()
        else:
            pl.when(n >= CORE_SLOTS)(go)
        self.sent(n, tag.core, source=partial.at[index, :, :, 1 - self.c]).start()
        self.load(n, partial.at[index, :, :, self.c]).start()

    def save(self, n):
        return pltpu.make_async_copy(self.k.total.at[lax.rem(n, 4)], self.k.sums.at[n], self.k.s_out.at[n])

    def stage(self, n, step):
        k = self.k
        core = self.core(n)
        if step == 0:
            if isinstance(n, int) and n < 9:
                self.open(n, k.grad_conv, n)
            else:
                self.open(n, k.grad, n - 9)
        if step == 1:
            self.load(n, core).wait()
            self.sent(n, tag.core).wait_recv()
            own = k.own.at[lax.rem(n, 3)]

            @pl.loop(0, 4)
            def _(i):
                core[i] = (core[i].astype(F32) + own[i].astype(F32)).astype(BF16)

            self.sent(n, tag.x).start()
            self.sent(n, tag.y1).start()
        if step == 2:
            self.sent(n, tag.x).wait_recv()
            mine = cols(*self.mine)

            @pl.loop(0, 4)
            def _(i):
                k.ax[n, i] = (k.ax[n, i].astype(F32) + core[i, :, :, mine].astype(F32)).astype(BF16)

            self.sent(n, tag.y2).start()
            self.sent(n, tag.y1).wait_recv()

            @pl.loop(0, 4)
            def _(i):
                k.y_one[n, i] = (k.y_one[n, i].astype(F32) + core[i, self.y, :, 0:512].astype(F32)).astype(BF16)

            for turn in range(3):
                self.sent(n, tag.z1, turn).start()
        if step == 3:
            self.sent(n, tag.y2).wait_recv()

            @pl.loop(0, 4)
            def _(i):
                k.y_two[n, i] = (k.y_two[n, i].astype(F32) + k.ax[n, i, self.y].astype(F32)).astype(BF16)

            for turn in range(3):
                self.sent(n, tag.z2, turn).start()
            for turn in range(3):
                self.sent(n, tag.z1, turn).wait_recv()
            total = k.y_one[n, self.z].astype(F32)
            for turn in range(3):
                total = total + k.z_one[n, turn].astype(F32)
            k.x_one[n, 0] = total.astype(BF16)
            self.sent(n, tag.x1).start()
            self.sent(n, tag.x).wait_send()
            self.sent(n, tag.y1).wait_send()

            def release():
                pl.semaphore_signal(k.credit, inc=1, device_id=self.dev_c, device_id_type=MESH)

            if isinstance(n, int):
                if n < UNITS - CORE_SLOTS:
                    release()
            else:
                pl.when(n < UNITS - CORE_SLOTS)(release)
        if step == 4:
            if isinstance(n, int):
                if n >= 4:
                    self.save(n - 4).wait()
            else:

                @pl.when(n >= 4)
                def _():
                    self.save(lax.max(n - 4, 0)).wait()

            for turn in range(3):
                self.sent(n, tag.z2, turn).wait_recv()
            total = k.y_two[n, self.z].astype(F32)
            for turn in range(3):
                total = total + k.z_two[n, turn].astype(F32)
            k.x_two[n, 0] = total.astype(BF16)
            self.sent(n, tag.x2).start()
            self.sent(n, tag.x1).wait_recv()
            out = k.total.at[lax.rem(n, 4)]
            out[:, 0:512] = k.x_one[n, 0].astype(F32) + k.x_one[n, 1].astype(F32)
        if step == 5:
            self.sent(n, tag.x2).wait_recv()
            out = k.total.at[lax.rem(n, 4)]
            out[:, cols(*self.mine)] = k.x_two[n, 0].astype(F32)
            out[:, cols(*self.theirs)] = k.x_two[n, 1].astype(F32)
            self.save(n).start()
            for name in (tag.core, tag.y2, tag.x1, tag.x2):
                self.sent(n, name).wait_send()
            for turn in range(3):
                self.sent(n, tag.z1, turn).wait_send()
                self.sent(n, tag.z2, turn).wait_send()

    def part(self, tick, step):
        n = tick - self.LAG[step]
        if isinstance(tick, int):
            if 0 <= n < UNITS:
                self.stage(n, step)
                return True
            return False

        @pl.when(within(n, UNITS))
        def _():
            self.stage(n, step)

    def ticks(self, first, last):
        @pl.loop(first, last)
        def _(tick):
            for step in range(6):
                self.part(tick, step)


CORE_SLOTS = 6
BACKWARD_IN = [tag.gain_one, tag.gain_two, tag.bias_conv, tag.d_pixels, tag.full, tag.grad_conv] + [tag.kept_ + name for name in KEPT]
BACKWARD_OUT = {
    tag.grad: ((12, 4, 2, 2, 48, DIM), BF16),
    tag.pixels: ((TOKENS, DIM), F32),
    tag.sums: ((UNITS, 48, DIM), F32),
    tag.grad_embed: ((TOKENS, DIM), F32),
    tag.small_sum: ((16, DIM), F32),
}
BACKWARD_SCRATCH = {
    **{name: kind for name, kind in KEPT.items() if name != tag.surface},
    tag.halo: ((4, 16, DIM), BF16),
    tag.core: ((CORE_SLOTS, 4, 2, 48, DIM), BF16),
    tag.own: ((3, 4, 2, 48, DIM), BF16),
    tag.ax: ((UNITS, 4, 2, 48, 128), BF16),
    tag.y_one: ((UNITS, 4, 48, 512), BF16),
    tag.y_two: ((UNITS, 4, 48, 128), BF16),
    tag.z_one: ((UNITS, 3, 48, 512), BF16),
    tag.z_two: ((UNITS, 3, 48, 128), BF16),
    tag.x_one: ((UNITS, 2, 48, 512), BF16),
    tag.x_two: ((UNITS, 2, 48, 128), BF16),
    tag.total: ((4, 48, DIM), F32),
    tag.w_down: ((4 * DIM, DIM), BF16),
    tag.w_up: ((4, DIM, DIM), BF16),
    tag.branch: ((TOKENS, DIM), BF16),
    tag.made: ((2, DIM, DIM), BF16),
    tag.d_mixed: ((TOKENS, DIM), BF16),
    tag.d_joined: ((3, TOKENS, DIM), BF16),
    tag.d_own: ((2, TOKENS, DIM), F32),
    tag.d_mixed_x: ((TOKENS, DIM), BF16),
    tag.small: ((4, 16, DIM), F32),
    tag.small_in: ((3, 16, DIM), F32),
    tag.small_z: ((4, 16, DIM), F32),
}
BACKWARD_SEMS = {
    tag.s_send: (UNITS, 12),
    tag.s_recv: (UNITS, 12),
    tag.s_local: (UNITS,),
    tag.s_out: (UNITS,),
    tag.fetch: (len(KEPT),),
    tag.load: (UNITS,),
    tag.made_sem: (4, 4),
    tag.x_send: (2,),
    tag.x_recv: (2,),
    tag.out_sem: (1,),
    tag.load_conv: (9,),
    tag.small_send: (6,),
    tag.small_recv: (6,),
}
SMALL = (
    [tag.bias_q, tag.bias_v, tag.bias_out, tag.gain_one, tag.shift_one, tag.gain_two, tag.shift_two]
    + [tag.bias_up0, tag.bias_up1, tag.bias_up2, tag.bias_up3, tag.bias_down, tag.bias_conv]
)


def norm_back(value, gain, change):
    center = value - jnp.mean(value, axis=-1, keepdims=True)
    scale = lax.rsqrt(jnp.mean(center * center, axis=-1, keepdims=True) + EPS)
    unit = center * scale
    scaled = change * gain
    back = scale * (
        scaled - jnp.mean(scaled, axis=-1, keepdims=True) - unit * jnp.mean(scaled * unit, axis=-1, keepdims=True)
    )
    return back, jnp.sum(change * unit, axis=0, keepdims=True), jnp.sum(change, axis=0, keepdims=True)


def column_sums(value):
    return jnp.sum(value.astype(F32), axis=0, keepdims=True)


def backward_kernel(*refs):
    names = BACKWARD_IN + list(BACKWARD_OUT) + list(BACKWARD_SCRATCH) + list(BACKWARD_SEMS) + [tag.credit]
    k = Refs(names, refs)
    z, y, c, x = place()
    turn, dev_y, dev_x, dev_c = neighbours()
    barrier = pltpu.get_barrier_semaphore()
    for other in turn + [dev_y, dev_x, dev_c]:
        pl.semaphore_signal(barrier, inc=1, device_id=other, device_id_type=MESH)

    k.surf = k.act.reshape(4 * TOKENS, DIM).at[pl.ds(0, 1920)].reshape(3, 4, 160, DIM)
    k.w_conv = k.slope.reshape(4 * TOKENS, DIM)
    k.surface = k.normed_two.reshape(4, 128, DIM)
    k.pixel_sum = k.stream_one

    def fetch(name):
        return pltpu.make_async_copy(getattr(k, tag.kept_ + name), getattr(k, name), k.fetch.at[list(KEPT).index(name)])

    def load(u):
        source = k.full.at[u]
        if u >= DOWN:
            to = k.w_down.reshape(16, 4, 48, DIM).at[:, u - DOWN]
            return pltpu.make_async_copy(source.reshape(16, 48, DIM), to, k.load.at[u])
        if u >= UP:
            return pltpu.make_async_copy(source.reshape(DIM, DIM), k.w_up.at[u - UP], k.load.at[u])
        return pltpu.make_async_copy(source.reshape(DIM, DIM), k.w_down.at[pl.ds(DIM * u, DIM)], k.load.at[u])

    order = [tag.d_two, tag.act, tag.slope, tag.normed_two, tag.stream_one, tag.mixed, tag.q, tag.keys, tag.values, tag.q_x, tag.normed_one, tag.emb]
    fetch(tag.d_two).start()
    fetch(tag.act).start()
    for u in range(DOWN, CONV):
        load(u).start()
    for name in order[2:]:
        fetch(name).start()
    for u in range(UP, DOWN):
        load(u).start()
    k.small[0] = jnp.zeros((16, DIM), F32)
    pl.semaphore_wait(barrier, 6)
    scatter = Scatter(k)
    state = {tag.tick: 0, tag.which: 0, tag.ready: 9}

    def step(count=1):
        while count > 0 and state[tag.tick] < UNITS + scatter.LAG[5]:
            which = state[tag.which]
            n = state[tag.tick] - scatter.LAG[which]
            if which == 0 and state[tag.ready] <= n < UNITS:
                return
            count -= scatter.part(state[tag.tick], which)
            state[tag.which] += 1
            if state[tag.which] == 6:
                state[tag.tick], state[tag.which] = state[tag.tick] + 1, 0

    def note(name, value, at=None):
        row = SMALL.index(name)
        where = EVERY if at is None else at
        k.small[0, row : row + 1, where] = value

    def add_note(name, value):
        row = SMALL.index(name)
        k.small[0, row : row + 1, :] += value

    step(RATE[0])
    fetch(tag.d_two).wait()
    k.branch[...] = k.d_two[...].astype(BF16)
    note(tag.bias_down, column_sums(k.branch[...]))
    note(tag.bias_conv, column_sums(k.d_pixels[...]))
    fetch(tag.act).wait()
    step(RATE[0])

    def save_down(m, piece):
        source = k.made.at[m % 2].reshape(2, 2, 4, 48, DIM).at[:, :, piece]
        return pltpu.make_async_copy(source, k.grad.at[piece, m], k.made_sem.at[m, piece])

    for m in range(4):
        if m >= 2:
            for piece in range(4):
                save_down(m - 2, piece).wait()

        @pl.loop(0, 3)
        def _(nb):
            at = cols(256 * nb)
            k.made[m % 2, :, at] = tn_dot(k.act[m], k.branch[:, at]).astype(BF16)

        for piece in range(4):
            save_down(m, piece).start()
        step(RATE[1])
    for m in (2, 3):
        for piece in range(4):
            save_down(m, piece).wait()
    state[tag.ready] = 13

    fetch(tag.slope).wait()
    for u in range(DOWN, CONV):
        load(u).wait()
    for part in range(4):

        @pl.loop(0, 3)
        def _(nb):
            at = cols(256 * nb)
            value = nt_dot(k.branch[...], k.w_down[cols(DIM * part + 256 * nb), :])
            value = (value * k.slope[part, :, at].astype(F32)).astype(BF16)
            k.slope[part, :, at] = value
            note(tag.bias_up + str(part), column_sums(value), cols(256 * nb))

        step(RATE[1])
    for u in range(QKV, UP):
        load(u).start()
    fetch(tag.normed_two).wait()

    def finish(n, slot):
        save_made(n, slot).wait()
        state[tag.ready] = 10 + n

    def save_made(n, slot):
        return pltpu.make_async_copy(k.made.at[slot], k.grad.at[n].reshape(DIM, DIM), k.made_sem.at[slot, n % 4])

    def weight_grad(n, slot, left, right, start=0):
        @pl.loop(0, 3)
        def _(nb):
            k.made[slot, :, cols(256 * nb)] = tn_dot(left[...], right[:, cols(start + 256 * nb)]).astype(BF16)

        save_made(n, slot).start()

    for part in range(4):
        if part >= 2:
            finish(2 + part, part % 2)
        weight_grad(4 + part, part % 2, k.normed_two, k.slope.at[part])
        step(RATE[1])

    for u in range(UP, DOWN):
        load(u).wait()
    k.grad_embed[...] = jnp.zeros_like(k.grad_embed)
    for part in range(4):

        @pl.loop(0, 3)
        def _(nb):
            at = cols(256 * nb)
            k.grad_embed[:, at] += nt_dot(k.slope[part], k.w_up[part, at, :])

        step(RATE[1])
        if part == 0:
            finish(6, 0)
            finish(7, 1)
    fetch(tag.surface).start()
    fetch(tag.stream_one).wait()

    @pl.loop(0, 8)
    def _(b):
        rows = pl.ds(pl.multiple_of(b * 64, 64), 64)
        back, gain, shift = norm_back(k.stream_one[rows], k.gain_two[...].reshape(1, DIM), k.grad_embed[rows])
        add_note(tag.gain_two, gain)
        add_note(tag.shift_two, shift)
        value = k.d_two[rows] + back
        k.d_two[rows] = value
        low = value.astype(BF16)
        k.branch[rows] = low
        add_note(tag.bias_out, column_sums(low))

    step(RATE[1])
    fetch(tag.mixed).wait()
    weight_grad(8, 0, k.mixed, k.branch)
    step(RATE[1])
    load(OUT).wait()

    @pl.loop(0, 3)
    def _(nb):
        at = cols(256 * nb)
        k.d_mixed[:, at] = nt_dot(k.branch[...], k.w_down[cols(DIM * OUT + 256 * nb), :]).astype(BF16)

    exchange = remote(k.d_mixed, k.d_mixed_x, k.x_send.at[0], k.x_recv.at[0], dev_x)
    exchange.start()
    finish(8, 0)
    step(RATE[1])
    for name in (tag.q, tag.keys, tag.values, tag.q_x, tag.normed_one, tag.emb):
        fetch(name).wait()

    def attend(b, own):
        rows = pl.ds(aligned(b * 128), 128)
        low = lax.broadcasted_iota(jnp.int32, (128, 128), 1) < 64

        def both(value):
            return jnp.concatenate([jnp.where(low, value, 0), jnp.where(low, 0, value)], axis=0)

        for block in range(6):
            at = slice(128 * block, 128 * block + 128)
            query = both((k.q if own else k.q_x)[rows, at])
            change = both((k.d_mixed if own else k.d_mixed_x)[rows, at])
            keys, values = k.keys[b, :, at], k.values[b, :, at]
            scores = nt_dot(keys, query) * 0.125
            power = jnp.exp(scores - jnp.max(scores, axis=0, keepdims=True))
            probs = power * (1.0 / jnp.sum(power, axis=0, keepdims=True))
            d_probs = nt_dot(values, change)
            inner = jnp.sum(probs * d_probs, axis=0, keepdims=True)
            if own:
                d_scores = (probs * (d_probs - inner)).astype(BF16)
                d_query = tn_dot(d_scores, keys) * 0.125
                k.d_joined[0, rows, at] = jnp.where(low, d_query[:128], d_query[128:]).astype(BF16)
                d_scores = d_scores[:128]
            else:
                d_scores = (probs[:128] * (d_probs[:128] - inner)).astype(BF16)
            d_keys = dot(d_scores, query) * 0.125
            d_values = dot(probs[:128].astype(BF16), change)
            if own:
                k.d_own[0, rows, at] = d_keys
                k.d_own[1, rows, at] = d_values
            else:
                k.d_joined[1, rows, at] = (k.d_own[0, rows, at] + d_keys).astype(BF16)
                k.d_joined[2, rows, at] = (k.d_own[1, rows, at] + d_values).astype(BF16)

    fetch(tag.surface).wait()
    edge = pl.ds(aligned(112 - 112 * x, 16), 16)
    halo = remote(k.surface.at[:, edge], k.halo, k.x_send.at[1], k.x_recv.at[1], dev_x)
    for half in range(2):

        @pl.loop(2 * half, 2 * half + 2)
        def _(b):
            attend(b, True)

        step(RATE[2])
    halo.start()
    weight_grad(9, 1, k.normed_one, k.d_joined.at[0])
    step(RATE[3])
    finish(9, 1)
    exchange.wait_recv()
    for half in range(2):

        @pl.loop(2 * half, 2 * half + 2)
        def _(b):
            attend(b, False)

        step(RATE[4])
    weight_grad(10, 0, k.normed_one, k.d_joined.at[1])
    step(RATE[5])
    weight_grad(11, 1, k.normed_one, k.d_joined.at[2])
    finish(10, 0)
    step(RATE[5])
    note(tag.bias_q, column_sums(k.d_joined[0]))
    note(tag.bias_v, column_sums(k.d_joined[2]))
    for u in range(QKV, OUT):
        load(u).wait()
    for part in range(3):

        @pl.loop(0, 3)
        def _(nb):
            at = cols(256 * nb)
            value = nt_dot(k.d_joined[part], k.w_down[cols(DIM * part + 256 * nb), :])
            if part == 0:
                k.grad_embed[:, at] = value
            else:
                k.grad_embed[:, at] += value

        if part == 0:
            finish(11, 1)
        step(RATE[5])

    @pl.loop(0, 8)
    def _(b):
        rows = pl.ds(pl.multiple_of(b * 64, 64), 64)
        back, gain, shift = norm_back(k.emb[rows].astype(F32), k.gain_one[...].reshape(1, DIM), k.grad_embed[rows])
        add_note(tag.gain_one, gain)
        add_note(tag.shift_one, shift)
        k.grad_embed[rows] = k.d_two[rows] + back


    def load_conv(t):
        to = k.w_conv.at[pl.ds(pl.multiple_of(DIM * lax.rem(t, 2), DIM), DIM)]
        return pltpu.make_async_copy(k.full.at[CONV + t].reshape(DIM, DIM), to, k.load_conv.at[t])

    load_conv(0).start()
    halo.wait_recv()
    extend(k.surf, k.surface, k.halo, x)
    k.pixel_sum[...] = jnp.broadcast_to(k.bias_conv[...].reshape(1, DIM), (TOKENS, DIM))
    def small(hop, dev):
        return remote(k.small.at[hop], k.small_in.at[hop], k.small_send.at[hop], k.small_recv.at[hop], dev)

    for hop, dev in enumerate((dev_c, dev_x, dev_y)):
        small(hop, dev).start()
        step(6)
        small(hop, dev).wait_recv()
        k.small[hop + 1] = k.small[hop] + k.small_in[hop]

    def small_z(step):
        return remote(
            k.small.at[3], k.small_z.at[z], k.small_send.at[3 + step], k.small_recv.at[3 + step], turn[step]
        )

    for step_z in range(3):
        small_z(step_z).start()
    k.small_z[z] = k.small[3]
    while state[tag.which]:
        step()
    rest = state[tag.tick]
    assert rest >= 9

    @pl.loop(0, 9)
    def _(t):
        i, j = t // 3, lax.rem(t, 3)
        window = pl.ds(pl.multiple_of(16 * i, 16), 128)
        here = lax.rem(t, 2) * DIM
        load_conv(t).wait()

        @pl.when(t < 8)
        def _():
            load_conv(t + 1).start()

        for part in range(3):
            k.pixel_sum[:, 256 * part : 256 * part + 256] += dot(
                k.surf[j, :, window].reshape(TOKENS, DIM),
                k.w_conv[pl.ds(pl.multiple_of(here, DIM), DIM), 256 * part : 256 * part + 256],
            )
            for step in (2 * part, 2 * part + 1):
                scatter.part(rest + t, step)

    pixels = pltpu.make_async_copy(k.pixel_sum, k.pixels, k.out_sem.at[0])
    pixels.start()
    for tick in range(rest + 9, UNITS + scatter.LAG[5]):
        for which in range(6):
            scatter.part(tick, which)
    pixels.wait()
    for step_z in range(3):
        there = lax.rem(z + 3 - step_z, 4)
        remote(
            k.small.at[3], k.small_z.at[there], k.small_send.at[3 + step_z], k.small_recv.at[3 + step_z], turn[step_z]
        ).wait_recv()
    k.small_sum[...] = (k.small_z[0] + k.small_z[1]) + (k.small_z[2] + k.small_z[3])
    for hop, dev in enumerate((dev_c, dev_x, dev_y)):
        small(hop, dev).wait_send()
    for step_z in range(3):
        small_z(step_z).wait_send()
    halo.wait_send()
    exchange.wait_send()
    for n in range(UNITS - 4, UNITS):
        scatter.save(n).wait()


RATE = (3, 3, 6, 3, 6, 3)


def backward_pass(*args):
    any_space, vmem = pl.BlockSpec(memory_space=pl.ANY), pl.BlockSpec(memory_space=pltpu.VMEM)
    outs = pl.pallas_call(
        backward_kernel,
        out_shape=[jax.ShapeDtypeStruct(*kind) for kind in BACKWARD_OUT.values()],
        in_specs=[vmem] * 4 + [any_space] * (len(BACKWARD_IN) - 4),
        out_specs=[any_space] * 3 + [vmem] * 2,
        scratch_shapes=[pltpu.VMEM(*kind) for kind in BACKWARD_SCRATCH.values()]
        + [pltpu.SemaphoreType.DMA(shape) for shape in BACKWARD_SEMS.values()]
        + [pltpu.SemaphoreType.REGULAR],
        compiler_params=pltpu.CompilerParams(
            collective_id=1, has_side_effects=True, vmem_limit_bytes=63 * 2**20
        ),
        name=tag.backward_pass,
    )(*args)
    return dict(zip(BACKWARD_OUT, outs))


def deliver_kernel(sums, small, *refs):
    outs, sem = refs[:-1], refs[-1]
    qkv, out, up, down, conv = outs[:5]
    copies = [pltpu.make_async_copy(sums.at[pl.ds(0, 9)], conv, sem.at[0])]
    copies.append(pltpu.make_async_copy(sums.at[17], out, sem.at[1]))
    for n in range(3):
        copies.append(pltpu.make_async_copy(sums.at[18 + n], qkv.at[:, pl.ds(DIM * n, DIM)], sem.at[2 + n]))
    for n in range(4):
        copies.append(pltpu.make_async_copy(sums.at[13 + n], up.at[:, pl.ds(DIM * n, DIM)], sem.at[5 + n]))
        copies.append(pltpu.make_async_copy(sums.at[9 + n], down.at[pl.ds(48 * n, 48)], sem.at[9 + n]))
    for copy in copies:
        copy.start()
    rows = [(0,), (1,), (2,), (3,), (4,), (5,), (6,), (7, 8, 9, 10), (11,), (12,)]
    for ref, which in zip(outs[5:], rows):
        for n, row in enumerate(which):
            ref[pl.ds(DIM * n, DIM)] = small[row : row + 1].reshape(DIM)
    for copy in copies:
        copy.wait()


def deliver(sums, small):
    any_space, vmem = pl.BlockSpec(memory_space=pl.ANY), pl.BlockSpec(memory_space=pltpu.VMEM)
    large = [(48, 3 * DIM), (48, DIM), (48, 4 * DIM), (4 * 48, DIM), (9, 48, DIM)]
    vectors = [(DIM,)] * 7 + [(4 * DIM,)] + [(DIM,)] * 2
    return pl.pallas_call(
        deliver_kernel,
        out_shape=[jax.ShapeDtypeStruct(shape, F32) for shape in large + vectors],
        in_specs=[vmem] * 2,
        out_specs=[any_space] * 5 + [vmem] * 10,
        scratch_shapes=[pltpu.SemaphoreType.DMA((13,))],
        compiler_params=pltpu.CompilerParams(vmem_limit_bytes=16 * 2**20),
        name=tag.deliver,
    )(sums, small)


def fast_shards(
    indices,
    embed_table,
    w_qkv,
    bias_q,
    bias_v,
    w_out,
    bias_out,
    gain_one,
    shift_one,
    gain_two,
    shift_two,
    w_up,
    bias_up,
    w_down,
    bias_down,
    w_conv,
    bias_conv,
    d_pixels,
):
    out = forward_pass(
        embed_table.shape[0],
        indices,
        embed_table,
        d_pixels.reshape(4, 128, DIM),
        bias_q,
        bias_v,
        bias_out,
        gain_one,
        shift_one,
        gain_two,
        shift_two,
        bias_up,
        bias_down,
        packed_shards(w_qkv, w_out, w_up, w_down, w_conv),
    )
    kept = [out[tag.kept_ + name] for name in KEPT]
    back = backward_pass(gain_one, gain_two, bias_conv, d_pixels.reshape(TOKENS, DIM), out[tag.full], out[tag.grad_conv], *kept)
    g_qkv, g_out, g_up, g_down, g_conv, *small = deliver(back[tag.sums], back[tag.small_sum])
    g_bias_q, g_bias_v, g_bias_out, g_gain_one, g_shift_one, g_gain_two, g_shift_two = small[:7]
    g_bias_up, g_bias_down, g_bias_conv = small[7:]
    return (
        back[tag.pixels].reshape(4, 8, 16, DIM),
        back[tag.grad_embed].reshape(4, 8, 16, DIM),
        g_qkv,
        g_bias_q,
        g_bias_v,
        g_out,
        g_bias_out,
        g_gain_one,
        g_shift_one,
        g_gain_two,
        g_shift_two,
        g_up,
        g_bias_up,
        g_down,
        g_bias_down,
        g_conv,
        g_bias_conv,
    )


def solution(mesh):
    placed = (
        P("img", "tile", None),
        P("img", None),
        P("img", None),
        P(),
        P(),
        P("img", None),
        P(),
        P(),
        P(),
        P(),
        P(),
        P("img", None),
        P(),
        P("img", None),
        P(),
        P(None, "img", None),
        P(),
        P("img", "tile", None, None),
    )
    return jax.shard_map(
        fast_shards if dict(mesh.shape) == {"img": 16, "tile": 2} else shards,
        mesh=mesh,
        in_specs=placed,
        out_specs=(
            P("img", "tile", None, None),
            P("img", "tile", None, None),
            P("img", None),
            P(),
            P(),
            P("img", None),
            P(),
            P(),
            P(),
            P(),
            P(),
            P("img", None),
            P(),
            P("img", None),
            P(),
            P(None, "img", None),
            P(),
        ),
        check_vma=False,
    )
```

```python
import functools
import math

import jax
import jax.numpy as jnp
from jax import lax
from jax.experimental import pallas as pl
from jax.experimental.pallas import tpu as pltpu
from jax.sharding import PartitionSpec as P

HEADS = 12


EPS = 1e-06


def extended_2(block, sides, width):
    for axis, dim in sides:
        count = lax.axis_size(axis)
        forward = [(i, i + 1) for i in range(count - 1)]
        backward = [(target, source) for source, target in forward]
        low = lax.ppermute(
            lax.slice_in_dim(block, block.shape[dim] - width, None, axis=dim), axis, forward
        )
        high = lax.ppermute(lax.slice_in_dim(block, 0, width, axis=dim), axis, backward)
        block = jnp.concatenate([low, block, high], axis=dim)
    return block


def norm_rows(values, gain, shift):
    center = values - jnp.mean(values, axis=-1, keepdims=True)
    spread = jnp.mean(center * center, axis=-1, keepdims=True)
    return center * lax.rsqrt(spread + EPS) * gain + shift


def shards(
    indices,
    embed_table,
    w_qkv,
    bias_q,
    bias_v,
    w_out,
    bias_out,
    gain_one,
    shift_one,
    gain_two,
    shift_two,
    w_up,
    bias_up,
    w_down,
    bias_down,
    w_conv,
    bias_conv,
    d_pixels,
):
    n_images, half_rows, grid_cols = indices.shape
    vocab_rows, model_width = embed_table.shape
    n_img = lax.axis_size("img")
    local_tokens = half_rows * grid_cols
    all_tokens = n_images * local_tokens
    capacity = max(2, 2 * all_tokens // n_img)
    flat_ids = indices.reshape(all_tokens)
    owner_dev = flat_ids // vocab_rows
    within = flat_ids - owner_dev * vocab_rows
    hits = (owner_dev[:, None] == jnp.arange(n_img, dtype=jnp.int32)[None, :]).astype(jnp.int32)
    slot_rank = jnp.sum((jnp.cumsum(hits, axis=0) - hits) * hits, axis=1)
    slot_index = owner_dev * capacity + slot_rank
    requests = (
        jnp.zeros((n_img * capacity,), jnp.int32)
        .at[slot_index]
        .set(within)
        .reshape(n_img, capacity)
    )
    found = jnp.take(
        embed_table,
        lax.all_to_all(requests, "img", split_axis=0, concat_axis=0, tiled=True),
        axis=0,
    )
    answers = lax.all_to_all(found, "img", split_axis=0, concat_axis=0, tiled=True)
    embedded = jnp.take(answers.reshape(n_img * capacity, model_width), slot_index, axis=0)
    token_rows = embedded.astype(jnp.float32).reshape(n_images, local_tokens, model_width)
    full_qkv, full_out, full_up, full_down, full_conv = (
        lax.all_gather(w_qkv, "img", axis=0, tiled=True),
        lax.all_gather(w_out, "img", axis=0, tiled=True),
        lax.all_gather(w_up, "img", axis=0, tiled=True),
        lax.all_gather(w_down, "img", axis=0, tiled=True),
        lax.all_gather(w_conv, "img", axis=1, tiled=True),
    )
    normed_one, pull_one = jax.vjp(norm_rows, token_rows, gain_one, shift_one)
    normed_low = normed_one.astype(jnp.bfloat16)
    zeros_k = jnp.zeros_like(bias_q)
    joined = jnp.einsum("bte,ef->btf", normed_low, full_qkv, preferred_element_type=jnp.float32)
    joined = joined + jnp.concatenate([bias_q, zeros_k, bias_v])
    joined_low = joined.astype(jnp.bfloat16).reshape(n_images, local_tokens, 3, HEADS, -1)
    queries = joined_low[:, :, 0]
    own_keys = joined_low[:, :, 1]
    own_values = joined_low[:, :, 2]
    all_keys, all_values = (
        lax.all_gather(own_keys, "tile", axis=1, tiled=True),
        lax.all_gather(own_values, "tile", axis=1, tiled=True),
    )
    scale = 1.0 / math.sqrt(queries.shape[-1])
    scores = (
        jnp.einsum("bqhd,bkhd->bhqk", queries, all_keys, preferred_element_type=jnp.float32) * scale
    )
    row_max = jnp.max(scores, axis=-1, keepdims=True)
    shifted = jnp.exp(scores - row_max)
    row_total = jnp.sum(shifted, axis=-1, keepdims=True)
    log_total = row_max + jnp.log(row_total)
    probs_low = (shifted / row_total).astype(jnp.bfloat16)
    mixed = jnp.einsum("bhqk,bkhd->bqhd", probs_low, all_values, preferred_element_type=jnp.float32)
    mixed_low = mixed.reshape(n_images, local_tokens, model_width).astype(jnp.bfloat16)
    stream_one = token_rows + (
        jnp.einsum("bte,ef->btf", mixed_low, full_out, preferred_element_type=jnp.float32)
        + bias_out
    )
    normed_two, pull_two = jax.vjp(norm_rows, stream_one, gain_two, shift_two)
    normed_two_low = normed_two.astype(jnp.bfloat16)
    hidden = (
        jnp.einsum("bte,em->btm", normed_two_low, full_up, preferred_element_type=jnp.float32)
        + bias_up
    )
    activated, pull_act = jax.vjp(jax.nn.gelu, hidden)
    activated_low = activated.astype(jnp.bfloat16)
    stream_two = stream_one + (
        jnp.einsum("btm,me->bte", activated_low, full_down, preferred_element_type=jnp.float32)
        + bias_down
    )
    surface = stream_two.astype(jnp.bfloat16).reshape(n_images, half_rows, grid_cols, model_width)
    extended = extended_2(surface, (("tile", 1),), 1)
    padded = jnp.pad(extended, ((0, 0), (0, 0), (1, 1), (0, 0)))
    pixels = bias_conv
    for row_off in range(3):
        for col_off in range(3):
            window = padded[:, row_off : row_off + half_rows, col_off : col_off + grid_cols]
            pixels = pixels + jnp.einsum(
                "brce,ef->brcf",
                window,
                full_conv[3 * row_off + col_off],
                preferred_element_type=jnp.float32,
            )
    back_qkv, back_out, back_up, back_down, back_conv = (
        lax.all_gather(w_qkv, "img", axis=0, tiled=True),
        lax.all_gather(w_out, "img", axis=0, tiled=True),
        lax.all_gather(w_up, "img", axis=0, tiled=True),
        lax.all_gather(w_down, "img", axis=0, tiled=True),
        lax.all_gather(w_conv, "img", axis=1, tiled=True),
    )
    conv_terms = []
    for row_off in range(3):
        for col_off in range(3):
            window = padded[:, row_off : row_off + half_rows, col_off : col_off + grid_cols]
            conv_terms.append(
                jnp.einsum("brce,brcf->ef", window, d_pixels, preferred_element_type=jnp.float32)
            )
    grad_w_conv = jnp.stack(conv_terms)
    grad_bias_conv = jnp.sum(d_pixels.astype(jnp.float32), axis=(0, 1, 2))
    cot_ext = extended_2(d_pixels, (("tile", 1),), 1)
    cot_pad = jnp.pad(cot_ext, ((0, 0), (0, 0), (1, 1), (0, 0)))
    d_surface = jnp.zeros((n_images, half_rows, grid_cols, model_width), jnp.float32)
    for row_off in range(3):
        for col_off in range(3):
            window = cot_pad[
                :, 2 - row_off : 2 - row_off + half_rows, 2 - col_off : 2 - col_off + grid_cols
            ]
            d_surface = d_surface + jnp.einsum(
                "brcf,ef->brce",
                window,
                back_conv[3 * row_off + col_off],
                preferred_element_type=jnp.float32,
            )
    d_stream_two = d_surface.reshape(n_images, local_tokens, model_width)
    branch_two = d_stream_two.astype(jnp.bfloat16)
    grad_w_down = jnp.einsum(
        "btm,bte->me", activated_low, branch_two, preferred_element_type=jnp.float32
    )
    grad_bias_down = jnp.sum(branch_two.astype(jnp.float32), axis=(0, 1))
    d_activated = jnp.einsum(
        "bte,me->btm", branch_two, back_down, preferred_element_type=jnp.float32
    )
    (d_hidden,) = pull_act(d_activated)
    d_hidden_low = d_hidden.astype(jnp.bfloat16)
    grad_w_up = jnp.einsum(
        "bte,btm->em", normed_two_low, d_hidden_low, preferred_element_type=jnp.float32
    )
    grad_bias_up = jnp.sum(d_hidden_low.astype(jnp.float32), axis=(0, 1))
    d_normed_two = jnp.einsum(
        "btm,em->bte", d_hidden_low, back_up, preferred_element_type=jnp.float32
    )
    d_from_two, grad_gain_two, grad_shift_two = pull_two(d_normed_two)
    d_stream_one = d_stream_two + d_from_two
    branch_one = d_stream_one.astype(jnp.bfloat16)
    grad_w_out = jnp.einsum(
        "bte,btf->ef", mixed_low, branch_one, preferred_element_type=jnp.float32
    )
    grad_bias_out = jnp.sum(branch_one.astype(jnp.float32), axis=(0, 1))
    d_mixed = jnp.einsum("btf,ef->bte", branch_one, back_out, preferred_element_type=jnp.float32)
    d_mixed = d_mixed.astype(jnp.bfloat16).reshape(n_images, local_tokens, HEADS, -1)
    scores_again = (
        jnp.einsum("bqhd,bkhd->bhqk", queries, all_keys, preferred_element_type=jnp.float32) * scale
    )
    probs_again = jnp.exp(scores_again - log_total)
    d_probs = jnp.einsum("bqhd,bkhd->bhqk", d_mixed, all_values, preferred_element_type=jnp.float32)
    inner = jnp.sum(probs_again * d_probs, axis=-1, keepdims=True)
    d_scores = (probs_again * (d_probs - inner)).astype(jnp.bfloat16)
    d_queries = (
        jnp.einsum("bhqk,bkhd->bqhd", d_scores, all_keys, preferred_element_type=jnp.float32)
        * scale
    )
    d_keys_all = (
        jnp.einsum("bhqk,bqhd->bkhd", d_scores, queries, preferred_element_type=jnp.float32) * scale
    )
    d_values_all = jnp.einsum(
        "bhqk,bqhd->bkhd",
        probs_again.astype(jnp.bfloat16),
        d_mixed,
        preferred_element_type=jnp.float32,
    )
    d_keys, d_values = (
        lax.psum_scatter(
            d_keys_all.astype(jnp.bfloat16), "tile", scatter_dimension=1, tiled=True
        ).astype(jnp.float32),
        lax.psum_scatter(
            d_values_all.astype(jnp.bfloat16), "tile", scatter_dimension=1, tiled=True
        ).astype(jnp.float32),
    )
    d_joined = jnp.stack([d_queries, d_keys, d_values], axis=2).astype(jnp.bfloat16)
    d_joined = d_joined.reshape(n_images, local_tokens, 3 * model_width)
    grad_w_qkv = jnp.einsum("bte,btf->ef", normed_low, d_joined, preferred_element_type=jnp.float32)
    joined_sums = jnp.sum(d_joined.astype(jnp.float32), axis=(0, 1))
    grad_bias_q = joined_sums[:model_width]
    grad_bias_v = joined_sums[2 * model_width :]
    d_normed_one = jnp.einsum("btf,ef->bte", d_joined, back_qkv, preferred_element_type=jnp.float32)
    d_from_one, grad_gain_one, grad_shift_one = pull_one(d_normed_one)
    grad_embed = (d_stream_one + d_from_one).reshape(n_images, half_rows, grid_cols, model_width)
    part_qkv, part_out, part_up, part_down, part_conv = (
        lax.psum_scatter(grad_w_qkv, "img", scatter_dimension=0, tiled=True),
        lax.psum_scatter(grad_w_out, "img", scatter_dimension=0, tiled=True),
        lax.psum_scatter(grad_w_up, "img", scatter_dimension=0, tiled=True),
        lax.psum_scatter(grad_w_down, "img", scatter_dimension=0, tiled=True),
        lax.psum_scatter(grad_w_conv, "img", scatter_dimension=1, tiled=True),
    )
    sum_qkv, sum_out, sum_up, sum_down, sum_conv = (
        lax.psum(part_qkv.astype(jnp.bfloat16), "tile").astype(jnp.float32),
        lax.psum(part_out.astype(jnp.bfloat16), "tile").astype(jnp.float32),
        lax.psum(part_up.astype(jnp.bfloat16), "tile").astype(jnp.float32),
        lax.psum(part_down.astype(jnp.bfloat16), "tile").astype(jnp.float32),
        lax.psum(part_conv.astype(jnp.bfloat16), "tile").astype(jnp.float32),
    )
    (
        sum_bias_q,
        sum_bias_v,
        sum_bias_out,
        sum_gain_one,
        sum_shift_one,
        sum_gain_two,
        sum_shift_two,
        sum_bias_up,
        sum_bias_down,
        sum_bias_conv,
    ) = lax.psum(
        (
            grad_bias_q,
            grad_bias_v,
            grad_bias_out,
            grad_gain_one,
            grad_shift_one,
            grad_gain_two,
            grad_shift_two,
            grad_bias_up,
            grad_bias_down,
            grad_bias_conv,
        ),
        ("img", "tile"),
    )
    return (
        pixels,
        grad_embed,
        sum_qkv,
        sum_bias_q,
        sum_bias_v,
        sum_out,
        sum_bias_out,
        sum_gain_one,
        sum_shift_one,
        sum_gain_two,
        sum_shift_two,
        sum_up,
        sum_bias_up,
        sum_down,
        sum_bias_down,
        sum_conv,
        sum_bias_conv,
    )


class Tag:
    def __getattr__(self, name):
        return name


tag = Tag()
MESH = pl.DeviceIdType.MESH
F32, BF16 = jnp.float32, jnp.bfloat16
DIM, TOKENS, SLOTS = 768, 512, 64
UNITS = 21
QKV, OUT, UP, DOWN, CONV = 0, 3, 4, 8, 12
EVERY = slice(None)


def aligned(start, unit=128):
    return start if isinstance(start, int) else pl.multiple_of(start, unit)


def cols(start, width=256):
    return pl.ds(aligned(start), width)


def place():
    img, tile = lax.axis_index("img"), lax.axis_index("tile")
    return img // 4, lax.rem(img // 2, 2), lax.rem(img, 2), tile


def device(z, y, c, x):
    return (z * 4 + y * 2 + c, x)


def neighbours():
    z, y, c, x = place()
    turn = [device(lax.rem(z + step, 4), y, c, x) for step in (1, 2, 3)]
    return turn, device(z, 1 - y, c, x), device(z, y, c, 1 - x), device(z, y, 1 - c, x)


def remote(src, dst, send, recv, dev):
    return pltpu.make_async_remote_copy(
        src_ref=src, dst_ref=dst, send_sem=send, recv_sem=recv, device_id=dev, device_id_type=MESH
    )


def within(number, count):
    return (number >= 0) & (number < count)


def nt_dot(a, b):
    return lax.dot_general(a, b, (((1,), (1,)), ((), ())), preferred_element_type=F32)


def tn_dot(a, b):
    return lax.dot_general(a, b, (((0,), (0,)), ((), ())), preferred_element_type=F32)


def dot(a, b):
    return jnp.dot(a, b, preferred_element_type=F32)


class Gather:
    LAG = (0, 2, 4, 6, 7, 8)
    TURN = (0, 1, 2, 3, 4, 5)

    def __init__(self, shards, full, send, recv, local):
        self.shards, self.full, self.send, self.recv, self.local = shards, full, send, recv, local
        z, y, c, x = place()
        self.z, self.y, self.c, self.x = z, y, c, x
        self.turn, self.dev_y, self.dev_x, self.dev_c = neighbours()
        self.now = [0, 0]
        self.done = 0

    def most(self, u):
        return (128 * self.x, 640) if self.wide(u) else (256 * self.x, 512)

    def mine(self, u):
        return (640 * self.x, 128) if self.wide(u) else (512 * self.x, 256)

    def theirs(self, u):
        return (640 - 640 * self.x, 128) if self.wide(u) else (512 - 512 * self.x, 256)

    def wide(self, u):
        return isinstance(u, int) and WIDE[0] <= u < WIDE[1]

    def at(self, u, z, y, c, columns):
        return self.full.at[u, z, y, c, :, cols(*columns)]

    def hop(self, u, slot, z, y, c, columns, dev):
        ref = self.at(u, z, y, c, columns)
        return remote(ref, ref, self.send.at[u, slot], self.recv.at[u, slot], dev)

    def shard(self, u):
        w_qkv, w_out, w_up, w_down, w_conv = self.shards
        start, width = self.most(u)
        if u < OUT:
            return w_qkv.at[:, cols(DIM * u + start, width)]
        if u < UP:
            return w_out.at[:, cols(start, width)]
        if u < DOWN:
            return w_up.at[:, cols(DIM * (u - UP) + start, width)]
        if u < CONV:
            return w_down.at[pl.ds(48 * (u - DOWN), 48), cols(start, width)]
        return w_conv.at[u - CONV, :, cols(start, width)]

    def own(self, u):
        if not isinstance(u, int):
            ref = self.at(u, self.z, self.y, self.c, self.most(u))
            return pltpu.make_async_copy(ref, ref, self.local.at[u])
        return pltpu.make_async_copy(
            self.shard(u), self.at(u, self.z, self.y, self.c, self.most(u)), self.local.at[u]
        )

    def along_z(self, u, turn):
        there = self.at(u, self.z, self.y, self.c, self.most(u))
        ref = self.shard(u) if isinstance(u, int) else there
        return remote(ref, there, self.send.at[u, turn], self.recv.at[u, turn], self.turn[turn])

    def came_z(self, u, turn):
        ref = self.at(u, lax.rem(self.z + 3 - turn, 4), self.y, self.c, self.most(u))
        return remote(ref, ref, self.send.at[u, turn], self.recv.at[u, turn], self.turn[turn])

    def along_y(self, u, came=False):
        return self.hop(u, 6, EVERY, 1 - self.y if came else self.y, self.c, self.most(u), self.dev_y)

    def along_x(self, u, n, came=False):
        y = 1 - self.y if n else self.y
        return self.hop(u, 7 + n, EVERY, y, self.c, self.theirs(u) if came else self.mine(u), self.dev_x)

    def to_core(self, u, n, came=False):
        c = 1 - self.c if came else self.c
        if n == 2:
            return self.hop(u, 11, EVERY, EVERY, c, self.theirs(u), self.dev_c)
        return self.hop(u, 9 + n, EVERY, 1 - self.y if n else self.y, c, self.most(u), self.dev_c)

    def stage(self, u, step):
        if step == 0:
            self.own(u).start()
            for turn in range(3):
                self.along_z(u, turn).start()
        if step == 1:
            self.own(u).wait()
            for turn in range(3):
                self.came_z(u, turn).wait_recv()
            self.along_y(u).start()
            self.along_x(u, 0).start()
            self.to_core(u, 0).start()
        if step == 2:
            self.along_y(u, True).wait_recv()
            self.along_x(u, 1).start()
            self.to_core(u, 1).start()
        if step == 3:
            self.along_x(u, 0, True).wait_recv()
            self.along_x(u, 1, True).wait_recv()
            self.to_core(u, 2).start()
        if step == 4:
            for n in range(3):
                self.to_core(u, n, True).wait_recv()
        if step == 5:
            for turn in range(3):
                self.along_z(u, turn).wait_send()
            self.along_y(u).wait_send()
            for n in (0, 1):
                self.along_x(u, n).wait_send()
            for n in range(3):
                self.to_core(u, n).wait_send()

    def step(self, count=1):
        while count > 0:
            if self.now[0] >= UNITS + self.LAG[5]:
                return
            stage = self.TURN[self.now[1]]
            u = self.now[0] - self.LAG[stage]
            if 0 <= u < UNITS:
                self.stage(u, stage)
                count -= 1
                if stage == 4:
                    self.done = u + 1
            self.now[1] += 1
            if self.now[1] == 6:
                self.now = [self.now[0] + 1, 0]

    def until(self, u):
        while self.done <= u:
            self.step()

    def round(self, tick, turns):
        for turn in turns:
            stage = self.TURN[turn]
            u = tick - self.LAG[stage]

            @pl.when(within(u, UNITS))
            def _(u=u, stage=stage):
                self.stage(u, stage)


def gelu_both(value):
    inner = 0.7978845608028654 * (value + 0.044715 * value * value * value)
    bend = jnp.tanh(inner)
    slope = 0.7978845608028654 * (1.0 + 3 * 0.044715 * value * value)
    half = 0.5 * (1.0 + bend)
    return value * half, half + 0.5 * value * (1.0 - bend * bend) * slope


def normed(value, gain, shift):
    center = value - jnp.mean(value, axis=-1, keepdims=True)
    spread = jnp.mean(center * center, axis=-1, keepdims=True)
    return center * lax.rsqrt(spread + EPS) * gain + shift


def shifted_copies(out):
    @pl.loop(0, 4)
    def _(b):
        value = out[1, b].astype(F32)
        column = lax.rem(lax.broadcasted_iota(jnp.int32, value.shape, 0), 16)
        rows = value.shape[0]
        out[0, b] = jnp.where(column == 0, 0.0, pltpu.roll(value, 1, axis=0)).astype(BF16)
        out[2, b] = jnp.where(column == 15, 0.0, pltpu.roll(value, rows - 1, axis=0)).astype(BF16)


FORWARD_IN = (
    [tag.indices, tag.table, tag.d_pixels, tag.bias_q, tag.bias_v, tag.bias_out, tag.gain_one, tag.shift_one]
    + [tag.gain_two, tag.shift_two, tag.bias_up, tag.bias_down, tag.s_qkv, tag.s_out, tag.s_up, tag.s_down, tag.s_conv]
)
KEPT = {
    tag.emb: ((TOKENS, DIM), BF16),
    tag.normed_one: ((TOKENS, DIM), BF16),
    tag.q: ((TOKENS, DIM), BF16),
    tag.keys: ((4, 256, DIM), BF16),
    tag.values: ((4, 256, DIM), BF16),
    tag.mixed: ((TOKENS, DIM), BF16),
    tag.stream_one: ((TOKENS, DIM), F32),
    tag.normed_two: ((TOKENS, DIM), BF16),
    tag.act: ((4, TOKENS, DIM), BF16),
    tag.slope: ((4, TOKENS, DIM), BF16),
    tag.d_two: ((TOKENS, DIM), F32),
    tag.surface: ((4, 128, DIM), BF16),
    tag.q_x: ((TOKENS, DIM), BF16),
}
FORWARD_OUT = {
    tag.full: ((UNITS, 4, 2, 2, 48, DIM), BF16),
    tag.grad_conv: ((9, 4, 2, 2, 48, DIM), BF16),
    **{tag.kept_ + name: kind for name, kind in KEPT.items()},
}
FORWARD_SCRATCH = {
    **KEPT,
    tag.ids: ((8, TOKENS), jnp.int32),
    tag.ids_all: ((16, 8, TOKENS), jnp.int32),
    tag.bias_qkv: ((3, DIM), F32),
    tag.onehot: None,
    tag.rows_out: ((16, SLOTS, DIM), BF16),
    tag.answers: ((16, SLOTS, DIM), BF16),
    tag.slot: ((TOKENS, 8), F32),
    tag.normed_x: ((TOKENS, DIM), BF16),
    tag.w_qkv: ((3, DIM, DIM), BF16),
    tag.w_out: ((DIM, DIM), BF16),
    tag.w_up: ((4, DIM, DIM), BF16),
    tag.w_down: ((16, 4, 48, DIM), BF16),
    tag.w_conv: ((2, DIM, DIM), BF16),
    tag.halo_cot: ((4, 16, DIM), BF16),
    tag.cot: ((3, 4, 160, DIM), BF16),
    tag.made: ((2, DIM, DIM), BF16),
}
FORWARD_SEMS = {
    tag.g_send: (UNITS, 12),
    tag.g_recv: (UNITS, 12),
    tag.g_local: (UNITS,),
    tag.load: (UNITS,),
    tag.ids_send: (16,),
    tag.ids_recv: (16,),
    tag.rows_send: (16,),
    tag.rows_recv: (16,),
    tag.x_send: (2,),
    tag.x_recv: (2,),
    tag.keep: (len(KEPT),),
    tag.made_sem: (9,),
}


class Refs:
    def __init__(self, names, refs):
        self.__dict__.update(dict(zip(names, refs)))


def extend(ext, own, halo, x):
    nothing = jnp.zeros((4, 16, DIM), BF16)
    came = halo[...]
    ext[1, :, 0:16] = jnp.where(x == 1, came, nothing)
    ext[1, :, 16:144] = own[...]
    ext[1, :, 144:160] = jnp.where(x == 0, came, nothing)
    shifted_copies(ext)


def forward_kernel(vocab, *refs):
    k = Refs(FORWARD_IN + list(FORWARD_OUT) + list(FORWARD_SCRATCH) + list(FORWARD_SEMS), refs)
    z, y, c, x = place()
    me = z * 4 + y * 2 + c
    turn, dev_y, dev_x, dev_c = neighbours()
    barrier = pltpu.get_barrier_semaphore()

    @pl.loop(1, 16)
    def _(step):
        pl.semaphore_signal(barrier, inc=1, device_id=(lax.rem(me + step, 16), x), device_id_type=MESH)

    pl.semaphore_signal(barrier, inc=1, device_id=dev_x, device_id_type=MESH)
    pl.semaphore_wait(barrier, 16)

    gather = Gather((k.s_qkv, k.s_out, k.s_up, k.s_down, k.s_conv), k.full, k.g_send, k.g_recv, k.g_local)

    def ids_copy(step):
        return remote(k.ids, k.ids_all.at[me], k.ids_send.at[step], k.ids_recv.at[me], (lax.rem(me + step, 16), x))

    def ids_came(step):
        there = lax.rem(me + 16 - step, 16)
        return remote(k.ids, k.ids_all.at[there], k.ids_send.at[step], k.ids_recv.at[there], (there, x))

    def rows_copy(step):
        there = lax.rem(me + step, 16)
        return remote(k.rows_out.at[there], k.answers.at[me], k.rows_send.at[step], k.rows_recv.at[me], (there, x))

    def rows_came(step):
        there = lax.rem(me + 16 - step, 16)
        return remote(k.rows_out.at[there], k.answers.at[there], k.rows_send.at[step], k.rows_recv.at[there], (there, x))

    grid = jnp.concatenate([k.indices[b] for b in range(4)], axis=0).astype(F32)
    spread = (
        lax.broadcasted_iota(jnp.int32, (16, TOKENS), 0)
        == lax.rem(lax.broadcasted_iota(jnp.int32, (16, TOKENS), 1), 16)
    ).astype(F32)
    wide = jnp.dot(grid, spread, precision=lax.Precision.HIGHEST, preferred_element_type=F32)
    line = lax.broadcasted_iota(jnp.int32, (32, TOKENS), 1) // 16
    wide = jnp.where(line == lax.broadcasted_iota(jnp.int32, (32, TOKENS), 0), wide, 0.0)
    ids = jnp.broadcast_to(jnp.sum(wide, axis=0, keepdims=True), (8, TOKENS)).astype(jnp.int32)
    k.ids[...] = ids

    @pl.loop(1, 16)
    def _(step):
        ids_copy(step).start()

    gather.step(3)
    edge = pl.ds(aligned(112 - 112 * x, 16), 16)
    halo_cot = remote(k.d_pixels.at[:, edge], k.halo_cot, k.x_send.at[0], k.x_recv.at[0], dev_x)
    halo_cot.start()
    k.bias_qkv[0:1] = k.bias_q[...].reshape(1, DIM)
    k.bias_qkv[1:2] = jnp.zeros((1, DIM), F32)
    k.bias_qkv[2:3] = k.bias_v[...].reshape(1, DIM)

    k.ids_all[me] = k.ids[...]
    before = (
        lax.broadcasted_iota(jnp.int32, (TOKENS, TOKENS), 0) < lax.broadcasted_iota(jnp.int32, (TOKENS, TOKENS), 1)
    ).astype(F32).astype(BF16)
    block = vocab


    @pl.loop(1, 16)
    def _(step):
        ids_came(step).wait_recv()

    asked = k.ids_all[:, 0, :] - vocab * me
    hit = (asked >= 0) & (asked < vocab)
    rank = dot(hit.astype(F32).astype(BF16), before)
    rank = jnp.where(hit, rank, -1.0)
    asked = jnp.where(hit, asked, 0).astype(F32)
    slots = lax.broadcasted_iota(jnp.int32, (SLOTS, TOKENS), 0).astype(F32)
    entries = lax.broadcasted_iota(jnp.int32, (SLOTS, block), 1).astype(F32)
    for d in range(16):
        entry = jnp.sum(jnp.where(slots == rank[d : d + 1], asked[d : d + 1], 0.0), axis=1, keepdims=True)
        k.onehot[SLOTS * d : SLOTS * d + SLOTS] = (entries == entry).astype(F32).astype(BF16)

    @pl.loop(0, 3)
    def _(nb):
        rows = dot(k.onehot[...], k.table[:, cols(256 * nb)]).astype(BF16)
        k.rows_out[:, :, cols(256 * nb)] = rows.reshape(16, SLOTS, 256)

    @pl.loop(1, 16)
    def _(step):
        rows_copy(step).start()

    k.answers[me] = k.rows_out[me]
    first = lax.broadcasted_iota(jnp.int32, (16, TOKENS), 0)
    own = (ids[0:1] >= vocab * first) & (ids[0:1] < vocab * (first + 1))
    rank = dot(own.astype(F32).astype(BF16), before)
    slot = jnp.sum(jnp.where(own, rank + (SLOTS * first).astype(F32), 0.0), axis=0, keepdims=True)
    k.slot[...] = jnp.broadcast_to(slot, (8, TOKENS)).T

    gather.step(EARLY[0])
    halo_cot.wait_recv()
    extend(k.cot, k.d_pixels, k.halo_cot, x)
    gather.step(EARLY[1])

    @pl.loop(1, 16)
    def _(step):
        rows_came(step).wait_recv()

    @pl.loop(0, 4)
    def _(b):
        rows = pl.ds(pl.multiple_of(b * 128, 128), 128)
        choice = (
            (lax.broadcasted_iota(jnp.int32, (128, 16 * SLOTS), 1).astype(F32) == k.slot[rows, 0:1])
            .astype(F32)
            .astype(BF16)
        )
        value = dot(choice, k.answers[...].reshape(16 * SLOTS, DIM))
        k.emb[rows] = value.astype(BF16)
        k.normed_one[rows] = normed(value, k.gain_one[...].reshape(1, DIM), k.shift_one[...].reshape(1, DIM)).astype(BF16)

    normed_x = remote(k.normed_one, k.normed_x, k.x_send.at[1], k.x_recv.at[1], dev_x)
    normed_x.start()

    def keep(name):
        n = list(KEPT).index(name)
        return pltpu.make_async_copy(getattr(k, name), getattr(k, tag.kept_ + name), k.keep.at[n])

    def load(u):
        source = k.full.at[u]
        if isinstance(u, int) and u < DOWN:
            to = k.w_qkv.at[u] if u < OUT else k.w_out if u == OUT else k.w_up.at[u - UP]
            return pltpu.make_async_copy(source.reshape(DIM, DIM), to, k.load.at[u])
        if isinstance(u, int) and u < CONV:
            return pltpu.make_async_copy(source.reshape(16, 48, DIM), k.w_down.at[:, u - DOWN], k.load.at[u])
        return pltpu.make_async_copy(source.reshape(DIM, DIM), k.w_conv.at[lax.rem(u, 2)], k.load.at[u])

    keep(tag.emb).start()
    keep(tag.normed_one).start()
    asked_for = set()

    def steps(count):
        gather.step(count)
        for u in range(min(gather.done, CONV)):
            if u not in asked_for:
                asked_for.add(u)
                load(u).start()

    def ready(u):
        while u not in asked_for:
            steps(1)
        load(u).wait()

    steps(0)
    ready(0)

    def query(into, source):
        @pl.loop(0, 3)
        def _(nb):
            at = cols(256 * nb)
            into[:, at] = (dot(source[...], k.w_qkv[0, :, at]) + k.bias_qkv[0:1, at]).astype(BF16)

    query(k.q, k.normed_one)
    keep(tag.q).start()
    steps(PACE[0])

    def project(into, which, source, start):
        @pl.loop(0, 3)
        def _(nb):
            at = cols(256 * nb)
            value = (dot(source[...], k.w_qkv[which, :, at]) + k.bias_qkv[which : which + 1, at]).astype(BF16)
            into[:, pl.ds(start, 128), at] = value.reshape(4, 128, 256)

    ready(1)
    project(k.keys, 1, k.normed_one, 0)
    steps(PACE[0])
    ready(2)
    project(k.values, 2, k.normed_one, 0)
    steps(PACE[0])
    normed_x.wait_recv()
    project(k.keys, 1, k.normed_x, 128)
    steps(PACE[0])
    project(k.values, 2, k.normed_x, 128)
    keep(tag.keys).start()
    keep(tag.values).start()
    query(k.q_x, k.normed_x)
    keep(tag.q_x).start()
    steps(PACE[0])

    def attend(b):
        rows = pl.ds(aligned(b * 128), 128)
        low = lax.broadcasted_iota(jnp.int32, (128, 128), 1) < 64
        for block in range(6):
            at = slice(128 * block, 128 * block + 128)
            q = k.q[rows, at]
            both = jnp.concatenate([jnp.where(low, q, 0), jnp.where(low, 0, q)], axis=0)
            scores = nt_dot(both, k.keys[b, :, at]) * 0.125
            power = jnp.exp(scores - jnp.max(scores, axis=-1, keepdims=True))
            probs = (power / jnp.sum(power, axis=-1, keepdims=True)).astype(BF16)
            value = dot(probs, k.values[b, :, at])
            k.mixed[rows, at] = jnp.where(low, value[:128], value[128:]).astype(BF16)

    for half in range(2):

        @pl.loop(2 * half, 2 * half + 2)
        def _(b):
            attend(b)

        steps(PACE[1])
    keep(tag.mixed).start()
    ready(OUT)

    @pl.loop(0, 4)
    def _(b):
        rows = pl.ds(pl.multiple_of(b * 128, 128), 128)
        value = k.emb[rows].astype(F32) + (dot(k.mixed[rows], k.w_out[...]) + k.bias_out[...].reshape(1, DIM))
        k.stream_one[rows] = value
        k.normed_two[rows] = normed(value, k.gain_two[...].reshape(1, DIM), k.shift_two[...].reshape(1, DIM)).astype(BF16)

    keep(tag.stream_one).start()
    keep(tag.normed_two).start()
    steps(PACE[2])
    for u in range(4):
        ready(UP + u)

        @pl.loop(0, 3)
        def _(nb):
            at = cols(256 * nb)
            value = dot(k.normed_two[...], k.w_up[u, :, at]) + k.bias_up[cols(256 * nb + DIM * u)].reshape(1, 256)
            act, slope = gelu_both(value)
            k.act[u, :, at] = act.astype(BF16)
            k.slope[u, :, at] = slope.astype(BF16)

        steps(PACE[2])
    keep(tag.act).start()
    keep(tag.slope).start()
    for u in range(DOWN, CONV):
        ready(u)

    @pl.loop(0, 3)
    def _(nb):
        at = cols(256 * nb)
        value = k.bias_down[at].reshape(1, 256)
        for u in range(4):
            value = value + dot(k.act[u], k.w_down[4 * u : 4 * u + 4, :, :, at].reshape(DIM, 256))
        k.surface[:, :, at] = (k.stream_one[:, at] + value).astype(BF16).reshape(4, 128, 256)

    keep(tag.surface).start()
    k.d_two[...] = jnp.zeros_like(k.d_two)
    while gather.now[1] or gather.done <= CONV:
        steps(1)
    start = gather.now[0]
    assert start - gather.LAG[5] >= WIDE[1]
    for u in range(start, UNITS):
        gather.stage(u, 0)
    load(CONV).start()

    def save_made(t):
        return pltpu.make_async_copy(k.made.at[lax.rem(t, 2)], k.grad_conv.at[t].reshape(DIM, DIM), k.made_sem.at[t])

    @pl.loop(0, 9)
    def _(t):
        i, j = t // 3, lax.rem(t, 3)
        slab = pl.ds(pl.multiple_of(16 * (2 - i), 16), 128)
        here = lax.rem(t, 2)
        gather.round(start + t, range(1, 3))

        @pl.when(t >= 2)
        def _():
            save_made(t - 2).wait()

        @pl.loop(0, 3)
        def _(nb):
            at = cols(256 * nb)
            cot = k.cot[2 - j, :, slab, at].reshape(TOKENS, 256)
            k.made[here, :, at] = tn_dot(k.surface[...].reshape(TOKENS, DIM), cot).astype(BF16)

        save_made(t).start()
        gather.round(start + t, range(3, 6))
        load(CONV + t).wait()

        @pl.when(t < 8)
        def _():
            load(CONV + t + 1).start()

        @pl.loop(0, 3)
        def _(nb):
            at = cols(256 * nb)
            k.d_two[:, at] += nt_dot(k.cot[2 - j, :, slab].reshape(TOKENS, DIM), k.w_conv[here, at, :])

    for tick in range(start + 9, UNITS + gather.LAG[5]):
        for step in range(6):
            if 0 <= tick - gather.LAG[step] < UNITS:
                gather.stage(tick - gather.LAG[step], step)
    keep(tag.d_two).start()
    save_made(7).wait()
    save_made(8).wait()
    for name in KEPT:
        keep(name).wait()
    halo_cot.wait_send()
    normed_x.wait_send()

    @pl.loop(1, 16)
    def _(step):
        ids_copy(step).wait_send()
        rows_copy(step).wait_send()


WIDE = (5, 10)
EARLY = (12, 16)
PACE = (5, 5, 5)


def forward_pass(vocab, *args):
    any_space, vmem = pl.BlockSpec(memory_space=pl.ANY), pl.BlockSpec(memory_space=pltpu.VMEM)
    scratch = dict(FORWARD_SCRATCH, onehot=((16 * SLOTS, vocab), BF16))
    outs = pl.pallas_call(
        functools.partial(forward_kernel, vocab),
        out_shape=[jax.ShapeDtypeStruct(*kind) for kind in FORWARD_OUT.values()],
        in_specs=[vmem] * len(FORWARD_IN),
        out_specs=[any_space] * len(FORWARD_OUT),
        scratch_shapes=[pltpu.VMEM(*kind) for kind in scratch.values()]
        + [pltpu.SemaphoreType.DMA(shape) for shape in FORWARD_SEMS.values()],
        compiler_params=pltpu.CompilerParams(
            collective_id=0, has_side_effects=True, vmem_limit_bytes=62 * 2**20
        ),
        name=tag.forward_pass,
    )(*args)
    return dict(zip(FORWARD_OUT, outs))


class Scatter:
    LAG = (0, 1, 3, 5, 7, 8)

    def __init__(self, k):
        self.k = k
        z, y, c, x = place()
        self.z, self.y, self.c, self.x = z, y, c, x
        self.turn, self.dev_y, self.dev_x, self.dev_c = neighbours()

    def more(self, n):
        return isinstance(n, int) and n < 9 and n % 2 == 0

    def one(self, n):
        return (0, 256) if self.more(n) else (0, 512)

    def mine(self, n):
        return (256 + 256 * self.x, 256) if self.more(n) else (512 + 128 * self.x, 128)

    def theirs(self, n):
        return (512 - 256 * self.x, 256) if self.more(n) else (640 - 128 * self.x, 128)

    def held(self, n):
        k = self.k
        if self.more(n):
            arrays = (k.more_ax, k.more_y_one, k.more_y_two, k.more_z_one, k.more_z_two, k.more_x_one, k.more_x_two)
            return [array.at[n // 2] for array in arrays]
        arrays = (k.ax, k.y_one, k.y_two, k.z_one, k.z_two, k.x_one, k.x_two)
        at = n // 2 if isinstance(n, int) and n < 9 else n - 5
        return [array.at[at] for array in arrays]

    def copy(self, n, slot, src, dst, dev):
        return remote(src, dst, self.k.s_send.at[n, slot], self.k.s_recv.at[n, slot], dev)

    def core(self, n):
        return self.k.core.at[lax.rem(n, CORE_SLOTS)]

    def sent(self, n, name, step=0, source=None):
        y, there = self.y, lax.rem(self.z + step + 1, 4)
        ax, y_one, y_two, z_one, z_two, x_one, x_two = self.held(n)
        if name == tag.core:
            return self.copy(n, 0, self.core(n) if source is None else source, self.core(n), self.dev_c)
        if name == tag.x:
            return self.copy(n, 1, self.core(n).at[:, :, :, cols(*self.theirs(n))], ax, self.dev_x)
        if name == tag.y1:
            return self.copy(n, 2, self.core(n).at[:, 1 - y, :, cols(*self.one(n))], y_one, self.dev_y)
        if name == tag.y2:
            return self.copy(n, 3, ax.at[:, 1 - y], y_two, self.dev_y)
        if name == tag.z1:
            return self.copy(n, 4 + step, y_one.at[there], z_one.at[step], self.turn[step])
        if name == tag.z2:
            return self.copy(n, 7 + step, y_two.at[there], z_two.at[step], self.turn[step])
        if name == tag.x1:
            return self.copy(n, 10, x_one.at[0], x_one.at[1], self.dev_x)
        return self.copy(n, 11, x_two.at[0], x_two.at[1], self.dev_x)

    def load(self, n, source):
        return pltpu.make_async_copy(source, self.k.own.at[lax.rem(n, 3)], self.k.s_local.at[n])

    def open(self, n, partial, index):
        k = self.k

        def go():
            pl.semaphore_wait(k.credit, 1)

        if isinstance(n, int):
            if n >= CORE_SLOTS:
                go()
        else:
            pl.when(n >= CORE_SLOTS)(go)
        self.sent(n, tag.core, source=partial.at[index, :, :, 1 - self.c]).start()
        self.load(n, partial.at[index, :, :, self.c]).start()

    def save(self, n):
        return pltpu.make_async_copy(self.k.total.at[lax.rem(n, 4)], self.k.sums.at[n], self.k.s_out.at[n])

    def stage(self, n, step):
        k = self.k
        core = self.core(n)
        ax, y_one, y_two, z_one, z_two, x_one, x_two = self.held(n)
        one, mine, theirs = cols(*self.one(n)), cols(*self.mine(n)), cols(*self.theirs(n))
        if step == 0:
            if isinstance(n, int) and n < 9:
                self.open(n, k.grad_conv, n)
            else:
                self.open(n, k.grad, n - 9)
        if step == 1:
            self.load(n, core).wait()
            self.sent(n, tag.core).wait_recv()
            own = k.own.at[lax.rem(n, 3)]

            @pl.loop(0, 4)
            def _(i):
                core[i] = (core[i].astype(F32) + own[i].astype(F32)).astype(BF16)

            self.sent(n, tag.x).start()
            self.sent(n, tag.y1).start()
        if step == 2:
            self.sent(n, tag.x).wait_recv()

            @pl.loop(0, 4)
            def _(i):
                ax[i] = (ax[i].astype(F32) + core[i, :, :, mine].astype(F32)).astype(BF16)

            self.sent(n, tag.y2).start()
            self.sent(n, tag.y1).wait_recv()

            @pl.loop(0, 4)
            def _(i):
                y_one[i] = (y_one[i].astype(F32) + core[i, self.y, :, one].astype(F32)).astype(BF16)

            for turn in range(3):
                self.sent(n, tag.z1, turn).start()
        if step == 3:
            self.sent(n, tag.y2).wait_recv()

            @pl.loop(0, 4)
            def _(i):
                y_two[i] = (y_two[i].astype(F32) + ax[i, self.y].astype(F32)).astype(BF16)

            for turn in range(3):
                self.sent(n, tag.z2, turn).start()
            for turn in range(3):
                self.sent(n, tag.z1, turn).wait_recv()
            total = y_one[self.z].astype(F32)
            for turn in range(3):
                total = total + z_one[turn].astype(F32)
            x_one[0] = total.astype(BF16)
            self.sent(n, tag.x1).start()
            self.sent(n, tag.x).wait_send()
            self.sent(n, tag.y1).wait_send()

            def release():
                pl.semaphore_signal(k.credit, inc=1, device_id=self.dev_c, device_id_type=MESH)

            if isinstance(n, int):
                if n < UNITS - CORE_SLOTS:
                    release()
            else:
                pl.when(n < UNITS - CORE_SLOTS)(release)
        if step == 4:
            if isinstance(n, int):
                if n >= 4:
                    self.save(n - 4).wait()
            else:

                @pl.when(n >= 4)
                def _():
                    self.save(lax.max(n - 4, 0)).wait()

            for turn in range(3):
                self.sent(n, tag.z2, turn).wait_recv()
            total = y_two[self.z].astype(F32)
            for turn in range(3):
                total = total + z_two[turn].astype(F32)
            x_two[0] = total.astype(BF16)
            self.sent(n, tag.x2).start()
            self.sent(n, tag.x1).wait_recv()
            out = k.total.at[lax.rem(n, 4)]
            out[:, one] = x_one[0].astype(F32) + x_one[1].astype(F32)
        if step == 5:
            self.sent(n, tag.x2).wait_recv()
            out = k.total.at[lax.rem(n, 4)]
            out[:, mine] = x_two[0].astype(F32)
            out[:, theirs] = x_two[1].astype(F32)
            self.save(n).start()
            for name in (tag.core, tag.y2, tag.x1, tag.x2):
                self.sent(n, name).wait_send()
            for turn in range(3):
                self.sent(n, tag.z1, turn).wait_send()
                self.sent(n, tag.z2, turn).wait_send()

    def part(self, tick, step):
        n = tick - self.LAG[step]
        if isinstance(tick, int):
            if 0 <= n < UNITS:
                self.stage(n, step)
                return True
            return False

        @pl.when(within(n, UNITS))
        def _():
            self.stage(n, step)

    def ticks(self, first, last):
        @pl.loop(first, last)
        def _(tick):
            for step in range(6):
                self.part(tick, step)


CORE_SLOTS = 6
BACKWARD_IN = [tag.gain_one, tag.gain_two, tag.bias_conv, tag.d_pixels, tag.full, tag.grad_conv] + [tag.kept_ + name for name in KEPT]
BACKWARD_OUT = {
    tag.grad: ((12, 4, 2, 2, 48, DIM), BF16),
    tag.pixels: ((TOKENS, DIM), F32),
    tag.sums: ((UNITS, 48, DIM), F32),
    tag.grad_embed: ((TOKENS, DIM), F32),
    tag.small_sum: ((16, DIM), F32),
}
BACKWARD_SCRATCH = {
    **{name: kind for name, kind in KEPT.items() if name != tag.surface},
    tag.halo: ((4, 16, DIM), BF16),
    tag.core: ((CORE_SLOTS, 4, 2, 48, DIM), BF16),
    tag.own: ((3, 4, 2, 48, DIM), BF16),
    tag.ax: ((16, 4, 2, 48, 128), BF16),
    tag.y_one: ((16, 4, 48, 512), BF16),
    tag.y_two: ((16, 4, 48, 128), BF16),
    tag.z_one: ((16, 3, 48, 512), BF16),
    tag.z_two: ((16, 3, 48, 128), BF16),
    tag.x_one: ((16, 2, 48, 512), BF16),
    tag.x_two: ((16, 2, 48, 128), BF16),
    tag.more_ax: ((5, 4, 2, 48, 256), BF16),
    tag.more_y_one: ((5, 4, 48, 256), BF16),
    tag.more_y_two: ((5, 4, 48, 256), BF16),
    tag.more_z_one: ((5, 3, 48, 256), BF16),
    tag.more_z_two: ((5, 3, 48, 256), BF16),
    tag.more_x_one: ((5, 2, 48, 256), BF16),
    tag.more_x_two: ((5, 2, 48, 256), BF16),
    tag.total: ((4, 48, DIM), F32),
    tag.w_down: ((4 * DIM, DIM), BF16),
    tag.w_up: ((4, DIM, DIM), BF16),
    tag.branch: ((TOKENS, DIM), BF16),
    tag.made: ((2, DIM, DIM), BF16),
    tag.d_mixed: ((TOKENS, DIM), BF16),
    tag.d_joined: ((3, TOKENS, DIM), BF16),
    tag.d_own: ((2, TOKENS, DIM), F32),
    tag.d_mixed_x: ((TOKENS, DIM), BF16),
    tag.small: ((4, 16, DIM), F32),
    tag.small_in: ((3, 16, DIM), F32),
    tag.small_z: ((4, 16, DIM), F32),
}
BACKWARD_SEMS = {
    tag.s_send: (UNITS, 12),
    tag.s_recv: (UNITS, 12),
    tag.s_local: (UNITS,),
    tag.s_out: (UNITS,),
    tag.fetch: (len(KEPT),),
    tag.load: (UNITS,),
    tag.made_sem: (4, 4),
    tag.x_send: (2,),
    tag.x_recv: (2,),
    tag.out_sem: (1,),
    tag.load_conv: (9,),
    tag.small_send: (6,),
    tag.small_recv: (6,),
}
SMALL = (
    [tag.bias_q, tag.bias_v, tag.bias_out, tag.gain_one, tag.shift_one, tag.gain_two, tag.shift_two]
    + [tag.bias_up0, tag.bias_up1, tag.bias_up2, tag.bias_up3, tag.bias_down, tag.bias_conv]
)


def norm_back(value, gain, change):
    center = value - jnp.mean(value, axis=-1, keepdims=True)
    scale = lax.rsqrt(jnp.mean(center * center, axis=-1, keepdims=True) + EPS)
    unit = center * scale
    scaled = change * gain
    back = scale * (
        scaled - jnp.mean(scaled, axis=-1, keepdims=True) - unit * jnp.mean(scaled * unit, axis=-1, keepdims=True)
    )
    return back, jnp.sum(change * unit, axis=0, keepdims=True), jnp.sum(change, axis=0, keepdims=True)


def column_sums(value):
    return jnp.sum(value.astype(F32), axis=0, keepdims=True)


def backward_kernel(*refs):
    names = BACKWARD_IN + list(BACKWARD_OUT) + list(BACKWARD_SCRATCH) + list(BACKWARD_SEMS) + [tag.credit]
    k = Refs(names, refs)
    z, y, c, x = place()
    turn, dev_y, dev_x, dev_c = neighbours()
    barrier = pltpu.get_barrier_semaphore()
    for other in turn + [dev_y, dev_x, dev_c]:
        pl.semaphore_signal(barrier, inc=1, device_id=other, device_id_type=MESH)

    k.surf = k.act.reshape(4 * TOKENS, DIM).at[pl.ds(0, 1920)].reshape(3, 4, 160, DIM)
    k.w_conv = k.slope.reshape(4 * TOKENS, DIM)
    k.surface = k.normed_two.reshape(4, 128, DIM)
    k.pixel_sum = k.stream_one

    def fetch(name):
        return pltpu.make_async_copy(getattr(k, tag.kept_ + name), getattr(k, name), k.fetch.at[list(KEPT).index(name)])

    def load(u):
        source = k.full.at[u]
        if u >= DOWN:
            to = k.w_down.reshape(16, 4, 48, DIM).at[:, u - DOWN]
            return pltpu.make_async_copy(source.reshape(16, 48, DIM), to, k.load.at[u])
        if u >= UP:
            return pltpu.make_async_copy(source.reshape(DIM, DIM), k.w_up.at[u - UP], k.load.at[u])
        return pltpu.make_async_copy(source.reshape(DIM, DIM), k.w_down.at[pl.ds(DIM * u, DIM)], k.load.at[u])

    order = [tag.d_two, tag.act, tag.slope, tag.normed_two, tag.stream_one, tag.mixed, tag.q, tag.keys, tag.values, tag.q_x, tag.normed_one, tag.emb]
    fetch(tag.d_two).start()
    fetch(tag.act).start()
    for u in range(DOWN, CONV):
        load(u).start()
    for name in order[2:]:
        fetch(name).start()
    for u in range(UP, DOWN):
        load(u).start()
    k.small[0] = jnp.zeros((16, DIM), F32)
    pl.semaphore_wait(barrier, 6)
    scatter = Scatter(k)
    state = {tag.tick: 0, tag.which: 0, tag.ready: 9}

    def step(count=1):
        while count > 0 and state[tag.tick] < UNITS + scatter.LAG[5]:
            which = state[tag.which]
            n = state[tag.tick] - scatter.LAG[which]
            if which == 0 and state[tag.ready] <= n < UNITS:
                return
            count -= scatter.part(state[tag.tick], which)
            state[tag.which] += 1
            if state[tag.which] == 6:
                state[tag.tick], state[tag.which] = state[tag.tick] + 1, 0

    def note(name, value, at=None):
        row = SMALL.index(name)
        where = EVERY if at is None else at
        k.small[0, row : row + 1, where] = value

    def add_note(name, value):
        row = SMALL.index(name)
        k.small[0, row : row + 1, :] += value

    step(RATE[0])
    fetch(tag.d_two).wait()
    k.branch[...] = k.d_two[...].astype(BF16)
    note(tag.bias_down, column_sums(k.branch[...]))
    note(tag.bias_conv, column_sums(k.d_pixels[...]))
    fetch(tag.act).wait()
    step(RATE[0])

    def save_down(m, piece):
        source = k.made.at[m % 2].reshape(2, 2, 4, 48, DIM).at[:, :, piece]
        return pltpu.make_async_copy(source, k.grad.at[piece, m], k.made_sem.at[m, piece])

    for m in range(4):
        if m >= 2:
            for piece in range(4):
                save_down(m - 2, piece).wait()

        @pl.loop(0, 3)
        def _(nb):
            at = cols(256 * nb)
            k.made[m % 2, :, at] = tn_dot(k.act[m], k.branch[:, at]).astype(BF16)

        for piece in range(4):
            save_down(m, piece).start()
        step(RATE[1])
    for m in (2, 3):
        for piece in range(4):
            save_down(m, piece).wait()
    state[tag.ready] = 13

    fetch(tag.slope).wait()
    for u in range(DOWN, CONV):
        load(u).wait()
    for part in range(4):

        @pl.loop(0, 3)
        def _(nb):
            at = cols(256 * nb)
            value = nt_dot(k.branch[...], k.w_down[cols(DIM * part + 256 * nb), :])
            value = (value * k.slope[part, :, at].astype(F32)).astype(BF16)
            k.slope[part, :, at] = value
            note(tag.bias_up + str(part), column_sums(value), cols(256 * nb))

        step(RATE[1])
    for u in range(QKV, UP):
        load(u).start()
    fetch(tag.normed_two).wait()

    def finish(n, slot):
        save_made(n, slot).wait()
        state[tag.ready] = 10 + n

    def save_made(n, slot):
        return pltpu.make_async_copy(k.made.at[slot], k.grad.at[n].reshape(DIM, DIM), k.made_sem.at[slot, n % 4])

    def weight_grad(n, slot, left, right, start=0):
        @pl.loop(0, 3)
        def _(nb):
            k.made[slot, :, cols(256 * nb)] = tn_dot(left[...], right[:, cols(start + 256 * nb)]).astype(BF16)

        save_made(n, slot).start()

    for part in range(4):
        if part >= 2:
            finish(2 + part, part % 2)
        weight_grad(4 + part, part % 2, k.normed_two, k.slope.at[part])
        step(RATE[1])

    for u in range(UP, DOWN):
        load(u).wait()
    k.grad_embed[...] = jnp.zeros_like(k.grad_embed)
    for part in range(4):

        @pl.loop(0, 3)
        def _(nb):
            at = cols(256 * nb)
            k.grad_embed[:, at] += nt_dot(k.slope[part], k.w_up[part, at, :])

        step(RATE[1])
        if part == 0:
            finish(6, 0)
            finish(7, 1)
    fetch(tag.surface).start()
    fetch(tag.stream_one).wait()

    @pl.loop(0, 8)
    def _(b):
        rows = pl.ds(pl.multiple_of(b * 64, 64), 64)
        back, gain, shift = norm_back(k.stream_one[rows], k.gain_two[...].reshape(1, DIM), k.grad_embed[rows])
        add_note(tag.gain_two, gain)
        add_note(tag.shift_two, shift)
        value = k.d_two[rows] + back
        k.d_two[rows] = value
        low = value.astype(BF16)
        k.branch[rows] = low
        add_note(tag.bias_out, column_sums(low))

    step(RATE[1])
    fetch(tag.mixed).wait()
    weight_grad(8, 0, k.mixed, k.branch)
    step(RATE[1])
    load(OUT).wait()

    @pl.loop(0, 3)
    def _(nb):
        at = cols(256 * nb)
        k.d_mixed[:, at] = nt_dot(k.branch[...], k.w_down[cols(DIM * OUT + 256 * nb), :]).astype(BF16)

    exchange = remote(k.d_mixed, k.d_mixed_x, k.x_send.at[0], k.x_recv.at[0], dev_x)
    exchange.start()
    finish(8, 0)
    step(RATE[1])
    for name in (tag.q, tag.keys, tag.values, tag.q_x, tag.normed_one, tag.emb):
        fetch(name).wait()

    def attend(b, own):
        rows = pl.ds(aligned(b * 128), 128)
        low = lax.broadcasted_iota(jnp.int32, (128, 128), 1) < 64

        def both(value):
            return jnp.concatenate([jnp.where(low, value, 0), jnp.where(low, 0, value)], axis=0)

        for block in range(6):
            at = slice(128 * block, 128 * block + 128)
            query = both((k.q if own else k.q_x)[rows, at])
            change = both((k.d_mixed if own else k.d_mixed_x)[rows, at])
            keys, values = k.keys[b, :, at], k.values[b, :, at]
            scores = nt_dot(keys, query) * 0.125
            power = jnp.exp(scores - jnp.max(scores, axis=0, keepdims=True))
            probs = power * (1.0 / jnp.sum(power, axis=0, keepdims=True))
            d_probs = nt_dot(values, change)
            inner = jnp.sum(probs * d_probs, axis=0, keepdims=True)
            if own:
                d_scores = (probs * (d_probs - inner)).astype(BF16)
                d_query = tn_dot(d_scores, keys) * 0.125
                k.d_joined[0, rows, at] = jnp.where(low, d_query[:128], d_query[128:]).astype(BF16)
                d_scores = d_scores[:128]
            else:
                d_scores = (probs[:128] * (d_probs[:128] - inner)).astype(BF16)
            d_keys = dot(d_scores, query) * 0.125
            d_values = dot(probs[:128].astype(BF16), change)
            if own:
                k.d_own[0, rows, at] = d_keys
                k.d_own[1, rows, at] = d_values
            else:
                k.d_joined[1, rows, at] = (k.d_own[0, rows, at] + d_keys).astype(BF16)
                k.d_joined[2, rows, at] = (k.d_own[1, rows, at] + d_values).astype(BF16)

    fetch(tag.surface).wait()
    edge = pl.ds(aligned(112 - 112 * x, 16), 16)
    halo = remote(k.surface.at[:, edge], k.halo, k.x_send.at[1], k.x_recv.at[1], dev_x)
    for half in range(2):

        @pl.loop(2 * half, 2 * half + 2)
        def _(b):
            attend(b, True)

        step(RATE[2])
    halo.start()
    weight_grad(9, 1, k.normed_one, k.d_joined.at[0])
    step(RATE[3])
    finish(9, 1)
    exchange.wait_recv()
    for half in range(2):

        @pl.loop(2 * half, 2 * half + 2)
        def _(b):
            attend(b, False)

        step(RATE[4])
    weight_grad(10, 0, k.normed_one, k.d_joined.at[1])
    step(RATE[5])
    weight_grad(11, 1, k.normed_one, k.d_joined.at[2])
    finish(10, 0)
    step(RATE[5])
    note(tag.bias_q, column_sums(k.d_joined[0]))
    note(tag.bias_v, column_sums(k.d_joined[2]))
    for u in range(QKV, OUT):
        load(u).wait()
    for part in range(3):

        @pl.loop(0, 3)
        def _(nb):
            at = cols(256 * nb)
            value = nt_dot(k.d_joined[part], k.w_down[cols(DIM * part + 256 * nb), :])
            if part == 0:
                k.grad_embed[:, at] = value
            else:
                k.grad_embed[:, at] += value

        if part == 0:
            finish(11, 1)
        step(RATE[5])

    @pl.loop(0, 8)
    def _(b):
        rows = pl.ds(pl.multiple_of(b * 64, 64), 64)
        back, gain, shift = norm_back(k.emb[rows].astype(F32), k.gain_one[...].reshape(1, DIM), k.grad_embed[rows])
        add_note(tag.gain_one, gain)
        add_note(tag.shift_one, shift)
        k.grad_embed[rows] = k.d_two[rows] + back


    def load_conv(t):
        to = k.w_conv.at[pl.ds(pl.multiple_of(DIM * lax.rem(t, 2), DIM), DIM)]
        return pltpu.make_async_copy(k.full.at[CONV + t].reshape(DIM, DIM), to, k.load_conv.at[t])

    load_conv(0).start()
    halo.wait_recv()
    extend(k.surf, k.surface, k.halo, x)
    k.pixel_sum[...] = jnp.broadcast_to(k.bias_conv[...].reshape(1, DIM), (TOKENS, DIM))
    def small(hop, dev):
        return remote(k.small.at[hop], k.small_in.at[hop], k.small_send.at[hop], k.small_recv.at[hop], dev)

    for hop, dev in enumerate((dev_c, dev_x, dev_y)):
        small(hop, dev).start()
        step(6)
        small(hop, dev).wait_recv()
        k.small[hop + 1] = k.small[hop] + k.small_in[hop]

    def small_z(step):
        return remote(
            k.small.at[3], k.small_z.at[z], k.small_send.at[3 + step], k.small_recv.at[3 + step], turn[step]
        )

    for step_z in range(3):
        small_z(step_z).start()
    k.small_z[z] = k.small[3]
    while state[tag.which]:
        step()
    rest = state[tag.tick]
    assert rest - scatter.LAG[5] >= 9

    @pl.loop(0, 9)
    def _(t):
        i, j = t // 3, lax.rem(t, 3)
        window = pl.ds(pl.multiple_of(16 * i, 16), 128)
        here = lax.rem(t, 2) * DIM
        load_conv(t).wait()

        @pl.when(t < 8)
        def _():
            load_conv(t + 1).start()

        for part in range(3):
            k.pixel_sum[:, 256 * part : 256 * part + 256] += dot(
                k.surf[j, :, window].reshape(TOKENS, DIM),
                k.w_conv[pl.ds(pl.multiple_of(here, DIM), DIM), 256 * part : 256 * part + 256],
            )
            for step in (2 * part, 2 * part + 1):
                scatter.part(rest + t, step)

    pixels = pltpu.make_async_copy(k.pixel_sum, k.pixels, k.out_sem.at[0])
    pixels.start()
    for tick in range(rest + 9, UNITS + scatter.LAG[5]):
        for which in range(6):
            scatter.part(tick, which)
    pixels.wait()
    for step_z in range(3):
        there = lax.rem(z + 3 - step_z, 4)
        remote(
            k.small.at[3], k.small_z.at[there], k.small_send.at[3 + step_z], k.small_recv.at[3 + step_z], turn[step_z]
        ).wait_recv()
    k.small_sum[...] = (k.small_z[0] + k.small_z[1]) + (k.small_z[2] + k.small_z[3])
    for hop, dev in enumerate((dev_c, dev_x, dev_y)):
        small(hop, dev).wait_send()
    for step_z in range(3):
        small_z(step_z).wait_send()
    halo.wait_send()
    exchange.wait_send()
    for n in range(UNITS - 4, UNITS):
        scatter.save(n).wait()


RATE = (3, 3, 6, 3, 6, 3)


def backward_pass(*args):
    any_space, vmem = pl.BlockSpec(memory_space=pl.ANY), pl.BlockSpec(memory_space=pltpu.VMEM)
    outs = pl.pallas_call(
        backward_kernel,
        out_shape=[jax.ShapeDtypeStruct(*kind) for kind in BACKWARD_OUT.values()],
        in_specs=[vmem] * 4 + [any_space] * (len(BACKWARD_IN) - 4),
        out_specs=[any_space] * 3 + [vmem] * 2,
        scratch_shapes=[pltpu.VMEM(*kind) for kind in BACKWARD_SCRATCH.values()]
        + [pltpu.SemaphoreType.DMA(shape) for shape in BACKWARD_SEMS.values()]
        + [pltpu.SemaphoreType.REGULAR],
        compiler_params=pltpu.CompilerParams(
            collective_id=1, has_side_effects=True, vmem_limit_bytes=63 * 2**20
        ),
        name=tag.backward_pass,
    )(*args)
    return dict(zip(BACKWARD_OUT, outs))


def deliver_kernel(sums, small, *refs):
    outs, sem = refs[:-1], refs[-1]
    qkv, out, up, down, conv = outs[:5]
    copies = [pltpu.make_async_copy(sums.at[pl.ds(0, 9)], conv, sem.at[0])]
    copies.append(pltpu.make_async_copy(sums.at[17], out, sem.at[1]))
    for n in range(3):
        copies.append(pltpu.make_async_copy(sums.at[18 + n], qkv.at[:, pl.ds(DIM * n, DIM)], sem.at[2 + n]))
    for n in range(4):
        copies.append(pltpu.make_async_copy(sums.at[13 + n], up.at[:, pl.ds(DIM * n, DIM)], sem.at[5 + n]))
        copies.append(pltpu.make_async_copy(sums.at[9 + n], down.at[pl.ds(48 * n, 48)], sem.at[9 + n]))
    for copy in copies:
        copy.start()
    rows = [(0,), (1,), (2,), (3,), (4,), (5,), (6,), (7, 8, 9, 10), (11,), (12,)]
    for ref, which in zip(outs[5:], rows):
        for n, row in enumerate(which):
            ref[pl.ds(DIM * n, DIM)] = small[row : row + 1].reshape(DIM)
    for copy in copies:
        copy.wait()


def deliver(sums, small):
    any_space, vmem = pl.BlockSpec(memory_space=pl.ANY), pl.BlockSpec(memory_space=pltpu.VMEM)
    large = [(48, 3 * DIM), (48, DIM), (48, 4 * DIM), (4 * 48, DIM), (9, 48, DIM)]
    vectors = [(DIM,)] * 7 + [(4 * DIM,)] + [(DIM,)] * 2
    return pl.pallas_call(
        deliver_kernel,
        out_shape=[jax.ShapeDtypeStruct(shape, F32) for shape in large + vectors],
        in_specs=[vmem] * 2,
        out_specs=[any_space] * 5 + [vmem] * 10,
        scratch_shapes=[pltpu.SemaphoreType.DMA((13,))],
        compiler_params=pltpu.CompilerParams(vmem_limit_bytes=16 * 2**20),
        name=tag.deliver,
    )(sums, small)


def fast_shards(
    indices,
    embed_table,
    w_qkv,
    bias_q,
    bias_v,
    w_out,
    bias_out,
    gain_one,
    shift_one,
    gain_two,
    shift_two,
    w_up,
    bias_up,
    w_down,
    bias_down,
    w_conv,
    bias_conv,
    d_pixels,
):
    out = forward_pass(
        embed_table.shape[0],
        indices,
        embed_table,
        d_pixels.reshape(4, 128, DIM),
        bias_q,
        bias_v,
        bias_out,
        gain_one,
        shift_one,
        gain_two,
        shift_two,
        bias_up,
        bias_down,
        w_qkv,
        w_out,
        w_up,
        w_down,
        w_conv,
    )
    kept = [out[tag.kept_ + name] for name in KEPT]
    back = backward_pass(gain_one, gain_two, bias_conv, d_pixels.reshape(TOKENS, DIM), out[tag.full], out[tag.grad_conv], *kept)
    g_qkv, g_out, g_up, g_down, g_conv, *small = deliver(back[tag.sums], back[tag.small_sum])
    g_bias_q, g_bias_v, g_bias_out, g_gain_one, g_shift_one, g_gain_two, g_shift_two = small[:7]
    g_bias_up, g_bias_down, g_bias_conv = small[7:]
    return (
        back[tag.pixels].reshape(4, 8, 16, DIM),
        back[tag.grad_embed].reshape(4, 8, 16, DIM),
        g_qkv,
        g_bias_q,
        g_bias_v,
        g_out,
        g_bias_out,
        g_gain_one,
        g_shift_one,
        g_gain_two,
        g_shift_two,
        g_up,
        g_bias_up,
        g_down,
        g_bias_down,
        g_conv,
        g_bias_conv,
    )


def solution(mesh):
    placed = (
        P("img", "tile", None),
        P("img", None),
        P("img", None),
        P(),
        P(),
        P("img", None),
        P(),
        P(),
        P(),
        P(),
        P(),
        P("img", None),
        P(),
        P("img", None),
        P(),
        P(None, "img", None),
        P(),
        P("img", "tile", None, None),
    )
    return jax.shard_map(
        fast_shards if dict(mesh.shape) == {"img": 16, "tile": 2} else shards,
        mesh=mesh,
        in_specs=placed,
        out_specs=(
            P("img", "tile", None, None),
            P("img", "tile", None, None),
            P("img", None),
            P(),
            P(),
            P("img", None),
            P(),
            P(),
            P(),
            P(),
            P(),
            P("img", None),
            P(),
            P("img", None),
            P(),
            P(None, "img", None),
            P(),
        ),
        check_vma=False,
    )
```

```python
import functools
import math

import jax
import jax.numpy as jnp
from jax import lax
from jax.experimental import pallas as pl
from jax.experimental.pallas import tpu as pltpu
from jax.sharding import PartitionSpec as P

HEADS = 12


EPS = 1e-06


def extended_2(block, sides, width):
    for axis, dim in sides:
        count = lax.axis_size(axis)
        forward = [(i, i + 1) for i in range(count - 1)]
        backward = [(target, source) for source, target in forward]
        low = lax.ppermute(
            lax.slice_in_dim(block, block.shape[dim] - width, None, axis=dim), axis, forward
        )
        high = lax.ppermute(lax.slice_in_dim(block, 0, width, axis=dim), axis, backward)
        block = jnp.concatenate([low, block, high], axis=dim)
    return block


def norm_rows(values, gain, shift):
    center = values - jnp.mean(values, axis=-1, keepdims=True)
    spread = jnp.mean(center * center, axis=-1, keepdims=True)
    return center * lax.rsqrt(spread + EPS) * gain + shift


def shards(
    indices,
    embed_table,
    w_qkv,
    bias_q,
    bias_v,
    w_out,
    bias_out,
    gain_one,
    shift_one,
    gain_two,
    shift_two,
    w_up,
    bias_up,
    w_down,
    bias_down,
    w_conv,
    bias_conv,
    d_pixels,
):
    n_images, half_rows, grid_cols = indices.shape
    vocab_rows, model_width = embed_table.shape
    n_img = lax.axis_size("img")
    local_tokens = half_rows * grid_cols
    all_tokens = n_images * local_tokens
    capacity = max(2, 2 * all_tokens // n_img)
    flat_ids = indices.reshape(all_tokens)
    owner_dev = flat_ids // vocab_rows
    within = flat_ids - owner_dev * vocab_rows
    hits = (owner_dev[:, None] == jnp.arange(n_img, dtype=jnp.int32)[None, :]).astype(jnp.int32)
    slot_rank = jnp.sum((jnp.cumsum(hits, axis=0) - hits) * hits, axis=1)
    slot_index = owner_dev * capacity + slot_rank
    requests = (
        jnp.zeros((n_img * capacity,), jnp.int32)
        .at[slot_index]
        .set(within)
        .reshape(n_img, capacity)
    )
    found = jnp.take(
        embed_table,
        lax.all_to_all(requests, "img", split_axis=0, concat_axis=0, tiled=True),
        axis=0,
    )
    answers = lax.all_to_all(found, "img", split_axis=0, concat_axis=0, tiled=True)
    embedded = jnp.take(answers.reshape(n_img * capacity, model_width), slot_index, axis=0)
    token_rows = embedded.astype(jnp.float32).reshape(n_images, local_tokens, model_width)
    full_qkv, full_out, full_up, full_down, full_conv = (
        lax.all_gather(w_qkv, "img", axis=0, tiled=True),
        lax.all_gather(w_out, "img", axis=0, tiled=True),
        lax.all_gather(w_up, "img", axis=0, tiled=True),
        lax.all_gather(w_down, "img", axis=0, tiled=True),
        lax.all_gather(w_conv, "img", axis=1, tiled=True),
    )
    normed_one, pull_one = jax.vjp(norm_rows, token_rows, gain_one, shift_one)
    normed_low = normed_one.astype(jnp.bfloat16)
    zeros_k = jnp.zeros_like(bias_q)
    joined = jnp.einsum("bte,ef->btf", normed_low, full_qkv, preferred_element_type=jnp.float32)
    joined = joined + jnp.concatenate([bias_q, zeros_k, bias_v])
    joined_low = joined.astype(jnp.bfloat16).reshape(n_images, local_tokens, 3, HEADS, -1)
    queries = joined_low[:, :, 0]
    own_keys = joined_low[:, :, 1]
    own_values = joined_low[:, :, 2]
    all_keys, all_values = (
        lax.all_gather(own_keys, "tile", axis=1, tiled=True),
        lax.all_gather(own_values, "tile", axis=1, tiled=True),
    )
    scale = 1.0 / math.sqrt(queries.shape[-1])
    scores = (
        jnp.einsum("bqhd,bkhd->bhqk", queries, all_keys, preferred_element_type=jnp.float32) * scale
    )
    row_max = jnp.max(scores, axis=-1, keepdims=True)
    shifted = jnp.exp(scores - row_max)
    row_total = jnp.sum(shifted, axis=-1, keepdims=True)
    log_total = row_max + jnp.log(row_total)
    probs_low = (shifted / row_total).astype(jnp.bfloat16)
    mixed = jnp.einsum("bhqk,bkhd->bqhd", probs_low, all_values, preferred_element_type=jnp.float32)
    mixed_low = mixed.reshape(n_images, local_tokens, model_width).astype(jnp.bfloat16)
    stream_one = token_rows + (
        jnp.einsum("bte,ef->btf", mixed_low, full_out, preferred_element_type=jnp.float32)
        + bias_out
    )
    normed_two, pull_two = jax.vjp(norm_rows, stream_one, gain_two, shift_two)
    normed_two_low = normed_two.astype(jnp.bfloat16)
    hidden = (
        jnp.einsum("bte,em->btm", normed_two_low, full_up, preferred_element_type=jnp.float32)
        + bias_up
    )
    activated, pull_act = jax.vjp(jax.nn.gelu, hidden)
    activated_low = activated.astype(jnp.bfloat16)
    stream_two = stream_one + (
        jnp.einsum("btm,me->bte", activated_low, full_down, preferred_element_type=jnp.float32)
        + bias_down
    )
    surface = stream_two.astype(jnp.bfloat16).reshape(n_images, half_rows, grid_cols, model_width)
    extended = extended_2(surface, (("tile", 1),), 1)
    padded = jnp.pad(extended, ((0, 0), (0, 0), (1, 1), (0, 0)))
    pixels = bias_conv
    for row_off in range(3):
        for col_off in range(3):
            window = padded[:, row_off : row_off + half_rows, col_off : col_off + grid_cols]
            pixels = pixels + jnp.einsum(
                "brce,ef->brcf",
                window,
                full_conv[3 * row_off + col_off],
                preferred_element_type=jnp.float32,
            )
    back_qkv, back_out, back_up, back_down, back_conv = (
        lax.all_gather(w_qkv, "img", axis=0, tiled=True),
        lax.all_gather(w_out, "img", axis=0, tiled=True),
        lax.all_gather(w_up, "img", axis=0, tiled=True),
        lax.all_gather(w_down, "img", axis=0, tiled=True),
        lax.all_gather(w_conv, "img", axis=1, tiled=True),
    )
    conv_terms = []
    for row_off in range(3):
        for col_off in range(3):
            window = padded[:, row_off : row_off + half_rows, col_off : col_off + grid_cols]
            conv_terms.append(
                jnp.einsum("brce,brcf->ef", window, d_pixels, preferred_element_type=jnp.float32)
            )
    grad_w_conv = jnp.stack(conv_terms)
    grad_bias_conv = jnp.sum(d_pixels.astype(jnp.float32), axis=(0, 1, 2))
    cot_ext = extended_2(d_pixels, (("tile", 1),), 1)
    cot_pad = jnp.pad(cot_ext, ((0, 0), (0, 0), (1, 1), (0, 0)))
    d_surface = jnp.zeros((n_images, half_rows, grid_cols, model_width), jnp.float32)
    for row_off in range(3):
        for col_off in range(3):
            window = cot_pad[
                :, 2 - row_off : 2 - row_off + half_rows, 2 - col_off : 2 - col_off + grid_cols
            ]
            d_surface = d_surface + jnp.einsum(
                "brcf,ef->brce",
                window,
                back_conv[3 * row_off + col_off],
                preferred_element_type=jnp.float32,
            )
    d_stream_two = d_surface.reshape(n_images, local_tokens, model_width)
    branch_two = d_stream_two.astype(jnp.bfloat16)
    grad_w_down = jnp.einsum(
        "btm,bte->me", activated_low, branch_two, preferred_element_type=jnp.float32
    )
    grad_bias_down = jnp.sum(branch_two.astype(jnp.float32), axis=(0, 1))
    d_activated = jnp.einsum(
        "bte,me->btm", branch_two, back_down, preferred_element_type=jnp.float32
    )
    (d_hidden,) = pull_act(d_activated)
    d_hidden_low = d_hidden.astype(jnp.bfloat16)
    grad_w_up = jnp.einsum(
        "bte,btm->em", normed_two_low, d_hidden_low, preferred_element_type=jnp.float32
    )
    grad_bias_up = jnp.sum(d_hidden_low.astype(jnp.float32), axis=(0, 1))
    d_normed_two = jnp.einsum(
        "btm,em->bte", d_hidden_low, back_up, preferred_element_type=jnp.float32
    )
    d_from_two, grad_gain_two, grad_shift_two = pull_two(d_normed_two)
    d_stream_one = d_stream_two + d_from_two
    branch_one = d_stream_one.astype(jnp.bfloat16)
    grad_w_out = jnp.einsum(
        "bte,btf->ef", mixed_low, branch_one, preferred_element_type=jnp.float32
    )
    grad_bias_out = jnp.sum(branch_one.astype(jnp.float32), axis=(0, 1))
    d_mixed = jnp.einsum("btf,ef->bte", branch_one, back_out, preferred_element_type=jnp.float32)
    d_mixed = d_mixed.astype(jnp.bfloat16).reshape(n_images, local_tokens, HEADS, -1)
    scores_again = (
        jnp.einsum("bqhd,bkhd->bhqk", queries, all_keys, preferred_element_type=jnp.float32) * scale
    )
    probs_again = jnp.exp(scores_again - log_total)
    d_probs = jnp.einsum("bqhd,bkhd->bhqk", d_mixed, all_values, preferred_element_type=jnp.float32)
    inner = jnp.sum(probs_again * d_probs, axis=-1, keepdims=True)
    d_scores = (probs_again * (d_probs - inner)).astype(jnp.bfloat16)
    d_queries = (
        jnp.einsum("bhqk,bkhd->bqhd", d_scores, all_keys, preferred_element_type=jnp.float32)
        * scale
    )
    d_keys_all = (
        jnp.einsum("bhqk,bqhd->bkhd", d_scores, queries, preferred_element_type=jnp.float32) * scale
    )
    d_values_all = jnp.einsum(
        "bhqk,bqhd->bkhd",
        probs_again.astype(jnp.bfloat16),
        d_mixed,
        preferred_element_type=jnp.float32,
    )
    d_keys, d_values = (
        lax.psum_scatter(
            d_keys_all.astype(jnp.bfloat16), "tile", scatter_dimension=1, tiled=True
        ).astype(jnp.float32),
        lax.psum_scatter(
            d_values_all.astype(jnp.bfloat16), "tile", scatter_dimension=1, tiled=True
        ).astype(jnp.float32),
    )
    d_joined = jnp.stack([d_queries, d_keys, d_values], axis=2).astype(jnp.bfloat16)
    d_joined = d_joined.reshape(n_images, local_tokens, 3 * model_width)
    grad_w_qkv = jnp.einsum("bte,btf->ef", normed_low, d_joined, preferred_element_type=jnp.float32)
    joined_sums = jnp.sum(d_joined.astype(jnp.float32), axis=(0, 1))
    grad_bias_q = joined_sums[:model_width]
    grad_bias_v = joined_sums[2 * model_width :]
    d_normed_one = jnp.einsum("btf,ef->bte", d_joined, back_qkv, preferred_element_type=jnp.float32)
    d_from_one, grad_gain_one, grad_shift_one = pull_one(d_normed_one)
    grad_embed = (d_stream_one + d_from_one).reshape(n_images, half_rows, grid_cols, model_width)
    part_qkv, part_out, part_up, part_down, part_conv = (
        lax.psum_scatter(grad_w_qkv, "img", scatter_dimension=0, tiled=True),
        lax.psum_scatter(grad_w_out, "img", scatter_dimension=0, tiled=True),
        lax.psum_scatter(grad_w_up, "img", scatter_dimension=0, tiled=True),
        lax.psum_scatter(grad_w_down, "img", scatter_dimension=0, tiled=True),
        lax.psum_scatter(grad_w_conv, "img", scatter_dimension=1, tiled=True),
    )
    sum_qkv, sum_out, sum_up, sum_down, sum_conv = (
        lax.psum(part_qkv.astype(jnp.bfloat16), "tile").astype(jnp.float32),
        lax.psum(part_out.astype(jnp.bfloat16), "tile").astype(jnp.float32),
        lax.psum(part_up.astype(jnp.bfloat16), "tile").astype(jnp.float32),
        lax.psum(part_down.astype(jnp.bfloat16), "tile").astype(jnp.float32),
        lax.psum(part_conv.astype(jnp.bfloat16), "tile").astype(jnp.float32),
    )
    (
        sum_bias_q,
        sum_bias_v,
        sum_bias_out,
        sum_gain_one,
        sum_shift_one,
        sum_gain_two,
        sum_shift_two,
        sum_bias_up,
        sum_bias_down,
        sum_bias_conv,
    ) = lax.psum(
        (
            grad_bias_q,
            grad_bias_v,
            grad_bias_out,
            grad_gain_one,
            grad_shift_one,
            grad_gain_two,
            grad_shift_two,
            grad_bias_up,
            grad_bias_down,
            grad_bias_conv,
        ),
        ("img", "tile"),
    )
    return (
        pixels,
        grad_embed,
        sum_qkv,
        sum_bias_q,
        sum_bias_v,
        sum_out,
        sum_bias_out,
        sum_gain_one,
        sum_shift_one,
        sum_gain_two,
        sum_shift_two,
        sum_up,
        sum_bias_up,
        sum_down,
        sum_bias_down,
        sum_conv,
        sum_bias_conv,
    )


class Tag:
    def __getattr__(self, name):
        return name


tag = Tag()
MESH = pl.DeviceIdType.MESH
F32, BF16 = jnp.float32, jnp.bfloat16
DIM, TOKENS, SLOTS = 768, 512, 64
UNITS = 21
QKV, OUT, UP, DOWN, CONV = 0, 3, 4, 8, 12
EVERY = slice(None)


def aligned(start, unit=128):
    return start if isinstance(start, int) else pl.multiple_of(start, unit)


def cols(start, width=256):
    return pl.ds(aligned(start), width)


def place():
    img, tile = lax.axis_index("img"), lax.axis_index("tile")
    return img // 4, lax.rem(img // 2, 2), lax.rem(img, 2), tile


def device(z, y, c, x):
    return (z * 4 + y * 2 + c, x)


def neighbours():
    z, y, c, x = place()
    turn = [device(lax.rem(z + step, 4), y, c, x) for step in (1, 2, 3)]
    return turn, device(z, 1 - y, c, x), device(z, y, c, 1 - x), device(z, y, 1 - c, x)


def remote(src, dst, send, recv, dev):
    return pltpu.make_async_remote_copy(
        src_ref=src, dst_ref=dst, send_sem=send, recv_sem=recv, device_id=dev, device_id_type=MESH
    )


def within(number, count):
    return (number >= 0) & (number < count)


def nt_dot(a, b):
    return lax.dot_general(a, b, (((1,), (1,)), ((), ())), preferred_element_type=F32)


def tn_dot(a, b):
    return lax.dot_general(a, b, (((0,), (0,)), ((), ())), preferred_element_type=F32)


def dot(a, b):
    return jnp.dot(a, b, preferred_element_type=F32)


class Gather:
    LAG = (0, 2, 4, 6, 7, 8)
    TURN = (0, 1, 2, 3, 4, 5)

    def __init__(self, shards, full, send, recv, local):
        self.shards, self.full, self.send, self.recv, self.local = shards, full, send, recv, local
        z, y, c, x = place()
        self.z, self.y, self.c, self.x = z, y, c, x
        self.turn, self.dev_y, self.dev_x, self.dev_c = neighbours()
        self.now = [0, 0]
        self.done = 0

    def most(self, u):
        return (128 * self.x, 640) if self.wide(u) else (256 * self.x, 512)

    def mine(self, u):
        return (640 * self.x, 128) if self.wide(u) else (512 * self.x, 256)

    def theirs(self, u):
        return (640 - 640 * self.x, 128) if self.wide(u) else (512 - 512 * self.x, 256)

    def wide(self, u):
        return isinstance(u, int) and WIDE[0] <= u < WIDE[1]

    def at(self, u, z, y, c, columns):
        return self.full.at[u, z, y, c, :, cols(*columns)]

    def hop(self, u, slot, z, y, c, columns, dev):
        ref = self.at(u, z, y, c, columns)
        return remote(ref, ref, self.send.at[u, slot], self.recv.at[u, slot], dev)

    def shard(self, u):
        w_qkv, w_out, w_up, w_down, w_conv = self.shards
        start, width = self.most(u)
        if u < OUT:
            return w_qkv.at[:, cols(DIM * u + start, width)]
        if u < UP:
            return w_out.at[:, cols(start, width)]
        if u < DOWN:
            return w_up.at[:, cols(DIM * (u - UP) + start, width)]
        if u < CONV:
            return w_down.at[pl.ds(48 * (u - DOWN), 48), cols(start, width)]
        return w_conv.at[u - CONV, :, cols(start, width)]

    def own(self, u):
        if not isinstance(u, int):
            ref = self.at(u, self.z, self.y, self.c, self.most(u))
            return pltpu.make_async_copy(ref, ref, self.local.at[u])
        return pltpu.make_async_copy(
            self.shard(u), self.at(u, self.z, self.y, self.c, self.most(u)), self.local.at[u]
        )

    def along_z(self, u, turn):
        there = self.at(u, self.z, self.y, self.c, self.most(u))
        ref = self.shard(u) if isinstance(u, int) else there
        return remote(ref, there, self.send.at[u, turn], self.recv.at[u, turn], self.turn[turn])

    def came_z(self, u, turn):
        ref = self.at(u, lax.rem(self.z + 3 - turn, 4), self.y, self.c, self.most(u))
        return remote(ref, ref, self.send.at[u, turn], self.recv.at[u, turn], self.turn[turn])

    def along_y(self, u, came=False):
        return self.hop(u, 6, EVERY, 1 - self.y if came else self.y, self.c, self.most(u), self.dev_y)

    def along_x(self, u, n, came=False):
        y = 1 - self.y if n else self.y
        return self.hop(u, 7 + n, EVERY, y, self.c, self.theirs(u) if came else self.mine(u), self.dev_x)

    def to_core(self, u, n, came=False):
        c = 1 - self.c if came else self.c
        if n == 2:
            return self.hop(u, 11, EVERY, EVERY, c, self.theirs(u), self.dev_c)
        return self.hop(u, 9 + n, EVERY, 1 - self.y if n else self.y, c, self.most(u), self.dev_c)

    def stage(self, u, step):
        if step == 0:
            self.own(u).start()
            for turn in range(3):
                self.along_z(u, turn).start()
        if step == 1:
            self.own(u).wait()
            for turn in range(3):
                self.came_z(u, turn).wait_recv()
            self.along_y(u).start()
            self.along_x(u, 0).start()
            self.to_core(u, 0).start()
        if step == 2:
            self.along_y(u, True).wait_recv()
            self.along_x(u, 1).start()
            self.to_core(u, 1).start()
        if step == 3:
            self.along_x(u, 0, True).wait_recv()
            self.along_x(u, 1, True).wait_recv()
            self.to_core(u, 2).start()
        if step == 4:
            for n in range(3):
                self.to_core(u, n, True).wait_recv()
        if step == 5:
            for turn in range(3):
                self.along_z(u, turn).wait_send()
            self.along_y(u).wait_send()
            for n in (0, 1):
                self.along_x(u, n).wait_send()
            for n in range(3):
                self.to_core(u, n).wait_send()

    def step(self, count=1):
        while count > 0:
            if self.now[0] >= UNITS + self.LAG[5]:
                return
            stage = self.TURN[self.now[1]]
            u = self.now[0] - self.LAG[stage]
            if 0 <= u < UNITS:
                self.stage(u, stage)
                count -= 1
                if stage == 4:
                    self.done = u + 1
            self.now[1] += 1
            if self.now[1] == 6:
                self.now = [self.now[0] + 1, 0]

    def until(self, u):
        while self.done <= u:
            self.step()

    def round(self, tick, turns):
        for turn in turns:
            stage = self.TURN[turn]
            u = tick - self.LAG[stage]

            @pl.when(within(u, UNITS))
            def _(u=u, stage=stage):
                self.stage(u, stage)


def gelu_both(value):
    inner = 0.7978845608028654 * (value + 0.044715 * value * value * value)
    bend = jnp.tanh(inner)
    slope = 0.7978845608028654 * (1.0 + 3 * 0.044715 * value * value)
    half = 0.5 * (1.0 + bend)
    return value * half, half + 0.5 * value * (1.0 - bend * bend) * slope


def normed(value, gain, shift):
    center = value - jnp.mean(value, axis=-1, keepdims=True)
    spread = jnp.mean(center * center, axis=-1, keepdims=True)
    return center * lax.rsqrt(spread + EPS) * gain + shift


def shifted_copies(out):
    @pl.loop(0, 4)
    def _(b):
        value = out[1, b].astype(F32)
        column = lax.rem(lax.broadcasted_iota(jnp.int32, value.shape, 0), 16)
        rows = value.shape[0]
        out[0, b] = jnp.where(column == 0, 0.0, pltpu.roll(value, 1, axis=0)).astype(BF16)
        out[2, b] = jnp.where(column == 15, 0.0, pltpu.roll(value, rows - 1, axis=0)).astype(BF16)


FORWARD_IN = (
    [tag.indices, tag.table, tag.d_pixels, tag.bias_q, tag.bias_v, tag.bias_out, tag.gain_one, tag.shift_one]
    + [tag.gain_two, tag.shift_two, tag.bias_up, tag.bias_down, tag.s_qkv, tag.s_out, tag.s_up, tag.s_down, tag.s_conv]
)
KEPT = {
    tag.emb: ((TOKENS, DIM), BF16),
    tag.normed_one: ((TOKENS, DIM), BF16),
    tag.q: ((TOKENS, DIM), BF16),
    tag.keys: ((4, 256, DIM), BF16),
    tag.values: ((4, 256, DIM), BF16),
    tag.mixed: ((TOKENS, DIM), BF16),
    tag.stream_one: ((TOKENS, DIM), F32),
    tag.normed_two: ((TOKENS, DIM), BF16),
    tag.act: ((4, TOKENS, DIM), BF16),
    tag.slope: ((4, TOKENS, DIM), BF16),
    tag.d_two: ((TOKENS, DIM), F32),
    tag.surface: ((4, 128, DIM), BF16),
    tag.q_x: ((TOKENS, DIM), BF16),
}
FORWARD_OUT = {
    tag.full: ((UNITS, 4, 2, 2, 48, DIM), BF16),
    tag.grad_conv: ((9, 4, 2, 2, 48, DIM), BF16),
    **{tag.kept_ + name: kind for name, kind in KEPT.items()},
}
FORWARD_SCRATCH = {
    **KEPT,
    tag.ids: ((8, TOKENS), jnp.int32),
    tag.ids_all: ((16, 8, TOKENS), jnp.int32),
    tag.bias_qkv: ((3, DIM), F32),
    tag.onehot: None,
    tag.rows_out: ((16, SLOTS, DIM), BF16),
    tag.answers: ((16, SLOTS, DIM), BF16),
    tag.slot: ((TOKENS, 8), F32),
    tag.normed_x: ((TOKENS, DIM), BF16),
    tag.w_qkv: ((3, DIM, DIM), BF16),
    tag.w_out: ((DIM, DIM), BF16),
    tag.w_up: ((4, DIM, DIM), BF16),
    tag.w_down: ((16, 4, 48, DIM), BF16),
    tag.w_conv: ((2, DIM, DIM), BF16),
    tag.halo_cot: ((4, 16, DIM), BF16),
    tag.cot: ((3, 4, 160, DIM), BF16),
    tag.made: ((2, DIM, DIM), BF16),
}
FORWARD_SEMS = {
    tag.g_send: (UNITS, 12),
    tag.g_recv: (UNITS, 12),
    tag.g_local: (UNITS,),
    tag.load: (UNITS,),
    tag.ids_send: (16,),
    tag.ids_recv: (16,),
    tag.rows_send: (16,),
    tag.rows_recv: (16,),
    tag.x_send: (5,),
    tag.x_recv: (5,),
    tag.keep: (len(KEPT),),
    tag.made_sem: (9,),
}


class Refs:
    def __init__(self, names, refs):
        self.__dict__.update(dict(zip(names, refs)))


def extend(ext, own, halo, x):
    nothing = jnp.zeros((4, 16, DIM), BF16)
    came = halo[...]
    ext[1, :, 0:16] = jnp.where(x == 1, came, nothing)
    ext[1, :, 16:144] = own[...]
    ext[1, :, 144:160] = jnp.where(x == 0, came, nothing)
    shifted_copies(ext)


def forward_kernel(vocab, *refs):
    k = Refs(FORWARD_IN + list(FORWARD_OUT) + list(FORWARD_SCRATCH) + list(FORWARD_SEMS), refs)
    z, y, c, x = place()
    me = z * 4 + y * 2 + c
    turn, dev_y, dev_x, dev_c = neighbours()
    barrier = pltpu.get_barrier_semaphore()

    @pl.loop(1, 16)
    def _(step):
        pl.semaphore_signal(barrier, inc=1, device_id=(lax.rem(me + step, 16), x), device_id_type=MESH)

    pl.semaphore_signal(barrier, inc=1, device_id=dev_x, device_id_type=MESH)
    pl.semaphore_wait(barrier, 16)

    gather = Gather((k.s_qkv, k.s_out, k.s_up, k.s_down, k.s_conv), k.full, k.g_send, k.g_recv, k.g_local)

    def ids_copy(step):
        return remote(k.ids, k.ids_all.at[me], k.ids_send.at[step], k.ids_recv.at[me], (lax.rem(me + step, 16), x))

    def ids_came(step):
        there = lax.rem(me + 16 - step, 16)
        return remote(k.ids, k.ids_all.at[there], k.ids_send.at[step], k.ids_recv.at[there], (there, x))

    def rows_copy(step):
        there = lax.rem(me + step, 16)
        return remote(k.rows_out.at[there], k.answers.at[me], k.rows_send.at[step], k.rows_recv.at[me], (there, x))

    def rows_came(step):
        there = lax.rem(me + 16 - step, 16)
        return remote(k.rows_out.at[there], k.answers.at[there], k.rows_send.at[step], k.rows_recv.at[there], (there, x))

    grid = jnp.concatenate([k.indices[b] for b in range(4)], axis=0).astype(F32)
    spread = (
        lax.broadcasted_iota(jnp.int32, (16, TOKENS), 0)
        == lax.rem(lax.broadcasted_iota(jnp.int32, (16, TOKENS), 1), 16)
    ).astype(F32)
    wide = jnp.dot(grid, spread, precision=lax.Precision.HIGHEST, preferred_element_type=F32)
    line = lax.broadcasted_iota(jnp.int32, (32, TOKENS), 1) // 16
    wide = jnp.where(line == lax.broadcasted_iota(jnp.int32, (32, TOKENS), 0), wide, 0.0)
    ids = jnp.broadcast_to(jnp.sum(wide, axis=0, keepdims=True), (8, TOKENS)).astype(jnp.int32)
    k.ids[...] = ids

    @pl.loop(1, 16)
    def _(step):
        ids_copy(step).start()

    gather.step(3)
    edge = pl.ds(aligned(112 - 112 * x, 16), 16)
    halo_cot = remote(k.d_pixels.at[:, edge], k.halo_cot, k.x_send.at[0], k.x_recv.at[0], dev_x)
    halo_cot.start()
    k.bias_qkv[0:1] = k.bias_q[...].reshape(1, DIM)
    k.bias_qkv[1:2] = jnp.zeros((1, DIM), F32)
    k.bias_qkv[2:3] = k.bias_v[...].reshape(1, DIM)

    k.ids_all[me] = k.ids[...]
    before = (
        lax.broadcasted_iota(jnp.int32, (TOKENS, TOKENS), 0) < lax.broadcasted_iota(jnp.int32, (TOKENS, TOKENS), 1)
    ).astype(F32).astype(BF16)
    block = vocab


    @pl.loop(1, 16)
    def _(step):
        ids_came(step).wait_recv()

    asked = k.ids_all[:, 0, :] - vocab * me
    hit = (asked >= 0) & (asked < vocab)
    rank = dot(hit.astype(F32).astype(BF16), before)
    rank = jnp.where(hit, rank, -1.0)
    asked = jnp.where(hit, asked, 0).astype(F32)
    slots = lax.broadcasted_iota(jnp.int32, (SLOTS, TOKENS), 0).astype(F32)
    entries = lax.broadcasted_iota(jnp.int32, (SLOTS, block), 1).astype(F32)
    for d in range(16):
        entry = jnp.sum(jnp.where(slots == rank[d : d + 1], asked[d : d + 1], 0.0), axis=1, keepdims=True)
        k.onehot[SLOTS * d : SLOTS * d + SLOTS] = (entries == entry).astype(F32).astype(BF16)

    @pl.loop(0, 3)
    def _(nb):
        rows = dot(k.onehot[...], k.table[:, cols(256 * nb)]).astype(BF16)
        k.rows_out[:, :, cols(256 * nb)] = rows.reshape(16, SLOTS, 256)

    @pl.loop(1, 16)
    def _(step):
        rows_copy(step).start()

    k.answers[me] = k.rows_out[me]
    first = lax.broadcasted_iota(jnp.int32, (16, TOKENS), 0)
    own = (ids[0:1] >= vocab * first) & (ids[0:1] < vocab * (first + 1))
    rank = dot(own.astype(F32).astype(BF16), before)
    slot = jnp.sum(jnp.where(own, rank + (SLOTS * first).astype(F32), 0.0), axis=0, keepdims=True)
    k.slot[...] = jnp.broadcast_to(slot, (8, TOKENS)).T

    gather.step(EARLY[0])
    halo_cot.wait_recv()
    extend(k.cot, k.d_pixels, k.halo_cot, x)
    gather.step(EARLY[1])

    @pl.loop(1, 16)
    def _(step):
        rows_came(step).wait_recv()

    def normed_x(b):
        rows = pl.ds(pl.multiple_of(b * 128, 128), 128)
        return remote(k.normed_one.at[rows], k.normed_x.at[rows], k.x_send.at[1 + b], k.x_recv.at[1 + b], dev_x)

    @pl.loop(0, 4)
    def _(b):
        rows = pl.ds(pl.multiple_of(b * 128, 128), 128)
        choice = (
            (lax.broadcasted_iota(jnp.int32, (128, 16 * SLOTS), 1).astype(F32) == k.slot[rows, 0:1])
            .astype(F32)
            .astype(BF16)
        )
        value = dot(choice, k.answers[...].reshape(16 * SLOTS, DIM))
        k.emb[rows] = value.astype(BF16)
        k.normed_one[rows] = normed(value, k.gain_one[...].reshape(1, DIM), k.shift_one[...].reshape(1, DIM)).astype(BF16)
        normed_x(b).start()


    def keep(name):
        n = list(KEPT).index(name)
        return pltpu.make_async_copy(getattr(k, name), getattr(k, tag.kept_ + name), k.keep.at[n])

    def load(u):
        source = k.full.at[u]
        if isinstance(u, int) and u < DOWN:
            to = k.w_qkv.at[u] if u < OUT else k.w_out if u == OUT else k.w_up.at[u - UP]
            return pltpu.make_async_copy(source.reshape(DIM, DIM), to, k.load.at[u])
        if isinstance(u, int) and u < CONV:
            return pltpu.make_async_copy(source.reshape(16, 48, DIM), k.w_down.at[:, u - DOWN], k.load.at[u])
        return pltpu.make_async_copy(source.reshape(DIM, DIM), k.w_conv.at[lax.rem(u, 2)], k.load.at[u])

    keep(tag.emb).start()
    keep(tag.normed_one).start()
    asked_for = set()

    def steps(count):
        gather.step(count)
        for u in range(min(gather.done, CONV)):
            if u not in asked_for:
                asked_for.add(u)
                load(u).start()

    def ready(u):
        while u not in asked_for:
            steps(1)
        load(u).wait()

    steps(0)
    ready(0)

    def query(into, source):
        @pl.loop(0, 3)
        def _(nb):
            at = cols(256 * nb)
            into[:, at] = (dot(source[...], k.w_qkv[0, :, at]) + k.bias_qkv[0:1, at]).astype(BF16)

    query(k.q, k.normed_one)
    keep(tag.q).start()
    steps(PACE[0])

    def project(into, which, source, start):
        @pl.loop(0, 3)
        def _(nb):
            at = cols(256 * nb)
            value = (dot(source[...], k.w_qkv[which, :, at]) + k.bias_qkv[which : which + 1, at]).astype(BF16)
            into[:, pl.ds(start, 128), at] = value.reshape(4, 128, 256)

    ready(1)
    project(k.keys, 1, k.normed_one, 0)
    steps(PACE[0])
    ready(2)
    project(k.values, 2, k.normed_one, 0)
    steps(PACE[0])
    @pl.loop(0, 4)
    def _(b):
        normed_x(b).wait_recv()

    project(k.keys, 1, k.normed_x, 128)
    steps(PACE[0])
    project(k.values, 2, k.normed_x, 128)
    keep(tag.keys).start()
    keep(tag.values).start()
    query(k.q_x, k.normed_x)
    keep(tag.q_x).start()
    steps(PACE[0])

    def attend(b):
        rows = pl.ds(aligned(b * 128), 128)
        low = lax.broadcasted_iota(jnp.int32, (128, 128), 1) < 64
        for block in range(6):
            at = slice(128 * block, 128 * block + 128)
            q = k.q[rows, at]
            both = jnp.concatenate([jnp.where(low, q, 0), jnp.where(low, 0, q)], axis=0)
            scores = nt_dot(both, k.keys[b, :, at]) * 0.125
            power = jnp.exp(scores - jnp.max(scores, axis=-1, keepdims=True))
            probs = (power / jnp.sum(power, axis=-1, keepdims=True)).astype(BF16)
            value = dot(probs, k.values[b, :, at])
            k.mixed[rows, at] = jnp.where(low, value[:128], value[128:]).astype(BF16)

    for half in range(2):

        @pl.loop(2 * half, 2 * half + 2)
        def _(b):
            attend(b)

        steps(PACE[1])
    keep(tag.mixed).start()
    ready(OUT)

    @pl.loop(0, 4)
    def _(b):
        rows = pl.ds(pl.multiple_of(b * 128, 128), 128)
        value = k.emb[rows].astype(F32) + (dot(k.mixed[rows], k.w_out[...]) + k.bias_out[...].reshape(1, DIM))
        k.stream_one[rows] = value
        k.normed_two[rows] = normed(value, k.gain_two[...].reshape(1, DIM), k.shift_two[...].reshape(1, DIM)).astype(BF16)

    keep(tag.stream_one).start()
    keep(tag.normed_two).start()
    steps(PACE[2])
    for u in range(4):
        ready(UP + u)

        @pl.loop(0, 3)
        def _(nb):
            at = cols(256 * nb)
            value = dot(k.normed_two[...], k.w_up[u, :, at]) + k.bias_up[cols(256 * nb + DIM * u)].reshape(1, 256)
            act, slope = gelu_both(value)
            k.act[u, :, at] = act.astype(BF16)
            k.slope[u, :, at] = slope.astype(BF16)

        steps(PACE[2])
    keep(tag.act).start()
    keep(tag.slope).start()
    for u in range(DOWN, CONV):
        ready(u)

    @pl.loop(0, 3)
    def _(nb):
        at = cols(256 * nb)
        value = k.bias_down[at].reshape(1, 256)
        for u in range(4):
            value = value + dot(k.act[u], k.w_down[4 * u : 4 * u + 4, :, :, at].reshape(DIM, 256))
        k.surface[:, :, at] = (k.stream_one[:, at] + value).astype(BF16).reshape(4, 128, 256)

    keep(tag.surface).start()
    k.d_two[...] = jnp.zeros_like(k.d_two)
    while gather.now[1] or gather.done <= CONV:
        steps(1)
    start = gather.now[0]
    assert start - gather.LAG[5] >= WIDE[1]
    for u in range(start, UNITS):
        gather.stage(u, 0)
    load(CONV).start()

    def save_made(t):
        return pltpu.make_async_copy(k.made.at[lax.rem(t, 2)], k.grad_conv.at[t].reshape(DIM, DIM), k.made_sem.at[t])

    @pl.loop(0, 9)
    def _(t):
        i, j = t // 3, lax.rem(t, 3)
        slab = pl.ds(pl.multiple_of(16 * (2 - i), 16), 128)
        here = lax.rem(t, 2)
        gather.round(start + t, range(1, 3))

        @pl.when(t >= 2)
        def _():
            save_made(t - 2).wait()

        @pl.loop(0, 3)
        def _(nb):
            at = cols(256 * nb)
            cot = k.cot[2 - j, :, slab, at].reshape(TOKENS, 256)
            k.made[here, :, at] = tn_dot(k.surface[...].reshape(TOKENS, DIM), cot).astype(BF16)

        save_made(t).start()
        gather.round(start + t, range(3, 6))
        load(CONV + t).wait()

        @pl.when(t < 8)
        def _():
            load(CONV + t + 1).start()

        @pl.loop(0, 3)
        def _(nb):
            at = cols(256 * nb)
            k.d_two[:, at] += nt_dot(k.cot[2 - j, :, slab].reshape(TOKENS, DIM), k.w_conv[here, at, :])

    for tick in range(start + 9, UNITS + gather.LAG[5]):
        for step in range(6):
            if 0 <= tick - gather.LAG[step] < UNITS:
                gather.stage(tick - gather.LAG[step], step)
    keep(tag.d_two).start()
    save_made(7).wait()
    save_made(8).wait()
    for name in KEPT:
        keep(name).wait()
    halo_cot.wait_send()

    @pl.loop(0, 4)
    def _(b):
        normed_x(b).wait_send()


    @pl.loop(1, 16)
    def _(step):
        ids_copy(step).wait_send()
        rows_copy(step).wait_send()


WIDE = (5, 10)
EARLY = (12, 16)
PACE = (5, 5, 5)


def forward_pass(vocab, *args):
    any_space, vmem = pl.BlockSpec(memory_space=pl.ANY), pl.BlockSpec(memory_space=pltpu.VMEM)
    scratch = dict(FORWARD_SCRATCH, onehot=((16 * SLOTS, vocab), BF16))
    outs = pl.pallas_call(
        functools.partial(forward_kernel, vocab),
        out_shape=[jax.ShapeDtypeStruct(*kind) for kind in FORWARD_OUT.values()],
        in_specs=[vmem] * len(FORWARD_IN),
        out_specs=[any_space] * len(FORWARD_OUT),
        scratch_shapes=[pltpu.VMEM(*kind) for kind in scratch.values()]
        + [pltpu.SemaphoreType.DMA(shape) for shape in FORWARD_SEMS.values()],
        compiler_params=pltpu.CompilerParams(
            collective_id=0, has_side_effects=True, vmem_limit_bytes=62 * 2**20
        ),
        name=tag.forward_pass,
    )(*args)
    return dict(zip(FORWARD_OUT, outs))


class Scatter:
    LAG = (0, 1, 3, 5, 7, 8)

    def __init__(self, k):
        self.k = k
        z, y, c, x = place()
        self.z, self.y, self.c, self.x = z, y, c, x
        self.turn, self.dev_y, self.dev_x, self.dev_c = neighbours()

    def more(self, n):
        return isinstance(n, int) and n < 9 and n % 2 == 0

    def one(self, n):
        return (0, 256) if self.more(n) else (0, 512)

    def mine(self, n):
        return (256 + 256 * self.x, 256) if self.more(n) else (512 + 128 * self.x, 128)

    def theirs(self, n):
        return (512 - 256 * self.x, 256) if self.more(n) else (640 - 128 * self.x, 128)

    def held(self, n):
        k = self.k
        if self.more(n):
            arrays = (k.more_ax, k.more_y_one, k.more_y_two, k.more_z_one, k.more_z_two, k.more_x_one, k.more_x_two)
            return [array.at[n // 2] for array in arrays]
        arrays = (k.ax, k.y_one, k.y_two, k.z_one, k.z_two, k.x_one, k.x_two)
        at = n // 2 if isinstance(n, int) and n < 9 else n - 5
        return [array.at[at] for array in arrays]

    def copy(self, n, slot, src, dst, dev):
        return remote(src, dst, self.k.s_send.at[n, slot], self.k.s_recv.at[n, slot], dev)

    def core(self, n):
        return self.k.core.at[lax.rem(n, CORE_SLOTS)]

    def sent(self, n, name, step=0, source=None):
        y, there = self.y, lax.rem(self.z + step + 1, 4)
        ax, y_one, y_two, z_one, z_two, x_one, x_two = self.held(n)
        if name == tag.core:
            return self.copy(n, 0, self.core(n) if source is None else source, self.core(n), self.dev_c)
        if name == tag.x:
            return self.copy(n, 1, self.core(n).at[:, :, :, cols(*self.theirs(n))], ax, self.dev_x)
        if name == tag.y1:
            return self.copy(n, 2, self.core(n).at[:, 1 - y, :, cols(*self.one(n))], y_one, self.dev_y)
        if name == tag.y2:
            return self.copy(n, 3, ax.at[:, 1 - y], y_two, self.dev_y)
        if name == tag.z1:
            return self.copy(n, 4 + step, y_one.at[there], z_one.at[step], self.turn[step])
        if name == tag.z2:
            return self.copy(n, 7 + step, y_two.at[there], z_two.at[step], self.turn[step])
        if name == tag.x1:
            return self.copy(n, 10, x_one.at[0], x_one.at[1], self.dev_x)
        return self.copy(n, 11, x_two.at[0], x_two.at[1], self.dev_x)

    def load(self, n, source):
        return pltpu.make_async_copy(source, self.k.own.at[lax.rem(n, 3)], self.k.s_local.at[n])

    def open(self, n, partial, index):
        k = self.k

        def go():
            pl.semaphore_wait(k.credit, 1)

        if isinstance(n, int):
            if n >= CORE_SLOTS:
                go()
        else:
            pl.when(n >= CORE_SLOTS)(go)
        self.sent(n, tag.core, source=partial.at[index, :, :, 1 - self.c]).start()
        self.load(n, partial.at[index, :, :, self.c]).start()

    def save(self, n):
        return pltpu.make_async_copy(self.k.total.at[lax.rem(n, 4)], self.k.sums.at[n], self.k.s_out.at[n])

    def stage(self, n, step):
        k = self.k
        core = self.core(n)
        ax, y_one, y_two, z_one, z_two, x_one, x_two = self.held(n)
        one, mine, theirs = cols(*self.one(n)), cols(*self.mine(n)), cols(*self.theirs(n))
        if step == 0:
            if isinstance(n, int) and n < 9:
                self.open(n, k.grad_conv, n)
            else:
                self.open(n, k.grad, n - 9)
        if step == 1:
            self.load(n, core).wait()
            self.sent(n, tag.core).wait_recv()
            own = k.own.at[lax.rem(n, 3)]

            @pl.loop(0, 4)
            def _(i):
                core[i] = (core[i].astype(F32) + own[i].astype(F32)).astype(BF16)

            self.sent(n, tag.x).start()
            self.sent(n, tag.y1).start()
        if step == 2:
            self.sent(n, tag.x).wait_recv()

            @pl.loop(0, 4)
            def _(i):
                ax[i] = (ax[i].astype(F32) + core[i, :, :, mine].astype(F32)).astype(BF16)

            self.sent(n, tag.y2).start()
            self.sent(n, tag.y1).wait_recv()

            @pl.loop(0, 4)
            def _(i):
                y_one[i] = (y_one[i].astype(F32) + core[i, self.y, :, one].astype(F32)).astype(BF16)

            for turn in range(3):
                self.sent(n, tag.z1, turn).start()
        if step == 3:
            self.sent(n, tag.y2).wait_recv()

            @pl.loop(0, 4)
            def _(i):
                y_two[i] = (y_two[i].astype(F32) + ax[i, self.y].astype(F32)).astype(BF16)

            for turn in range(3):
                self.sent(n, tag.z2, turn).start()
            for turn in range(3):
                self.sent(n, tag.z1, turn).wait_recv()
            total = y_one[self.z].astype(F32)
            for turn in range(3):
                total = total + z_one[turn].astype(F32)
            x_one[0] = total.astype(BF16)
            self.sent(n, tag.x1).start()
            self.sent(n, tag.x).wait_send()
            self.sent(n, tag.y1).wait_send()

            def release():
                pl.semaphore_signal(k.credit, inc=1, device_id=self.dev_c, device_id_type=MESH)

            if isinstance(n, int):
                if n < UNITS - CORE_SLOTS:
                    release()
            else:
                pl.when(n < UNITS - CORE_SLOTS)(release)
        if step == 4:
            if isinstance(n, int):
                if n >= 4:
                    self.save(n - 4).wait()
            else:

                @pl.when(n >= 4)
                def _():
                    self.save(lax.max(n - 4, 0)).wait()

            for turn in range(3):
                self.sent(n, tag.z2, turn).wait_recv()
            total = y_two[self.z].astype(F32)
            for turn in range(3):
                total = total + z_two[turn].astype(F32)
            x_two[0] = total.astype(BF16)
            self.sent(n, tag.x2).start()
            self.sent(n, tag.x1).wait_recv()
            out = k.total.at[lax.rem(n, 4)]
            out[:, one] = x_one[0].astype(F32) + x_one[1].astype(F32)
        if step == 5:
            self.sent(n, tag.x2).wait_recv()
            out = k.total.at[lax.rem(n, 4)]
            out[:, mine] = x_two[0].astype(F32)
            out[:, theirs] = x_two[1].astype(F32)
            self.save(n).start()
            for name in (tag.core, tag.y2, tag.x1, tag.x2):
                self.sent(n, name).wait_send()
            for turn in range(3):
                self.sent(n, tag.z1, turn).wait_send()
                self.sent(n, tag.z2, turn).wait_send()

    def part(self, tick, step):
        n = tick - self.LAG[step]
        if isinstance(tick, int):
            if 0 <= n < UNITS:
                self.stage(n, step)
                return True
            return False

        @pl.when(within(n, UNITS))
        def _():
            self.stage(n, step)

    def ticks(self, first, last):
        @pl.loop(first, last)
        def _(tick):
            for step in range(6):
                self.part(tick, step)


CORE_SLOTS = 6
BACKWARD_IN = [tag.gain_one, tag.gain_two, tag.bias_conv, tag.d_pixels, tag.full, tag.grad_conv] + [tag.kept_ + name for name in KEPT]
BACKWARD_OUT = {
    tag.grad: ((12, 4, 2, 2, 48, DIM), BF16),
    tag.pixels: ((TOKENS, DIM), F32),
    tag.sums: ((UNITS, 48, DIM), F32),
    tag.grad_embed: ((TOKENS, DIM), F32),
    tag.small_sum: ((16, DIM), F32),
}
BACKWARD_SCRATCH = {
    **{name: kind for name, kind in KEPT.items() if name != tag.surface},
    tag.halo: ((4, 16, DIM), BF16),
    tag.core: ((CORE_SLOTS, 4, 2, 48, DIM), BF16),
    tag.own: ((3, 4, 2, 48, DIM), BF16),
    tag.ax: ((16, 4, 2, 48, 128), BF16),
    tag.y_one: ((16, 4, 48, 512), BF16),
    tag.y_two: ((16, 4, 48, 128), BF16),
    tag.z_one: ((16, 3, 48, 512), BF16),
    tag.z_two: ((16, 3, 48, 128), BF16),
    tag.x_one: ((16, 2, 48, 512), BF16),
    tag.x_two: ((16, 2, 48, 128), BF16),
    tag.more_ax: ((5, 4, 2, 48, 256), BF16),
    tag.more_y_one: ((5, 4, 48, 256), BF16),
    tag.more_y_two: ((5, 4, 48, 256), BF16),
    tag.more_z_one: ((5, 3, 48, 256), BF16),
    tag.more_z_two: ((5, 3, 48, 256), BF16),
    tag.more_x_one: ((5, 2, 48, 256), BF16),
    tag.more_x_two: ((5, 2, 48, 256), BF16),
    tag.total: ((4, 48, DIM), F32),
    tag.w_down: ((4 * DIM, DIM), BF16),
    tag.w_up: ((4, DIM, DIM), BF16),
    tag.branch: ((TOKENS, DIM), BF16),
    tag.made: ((2, DIM, DIM), BF16),
    tag.d_mixed: ((TOKENS, DIM), BF16),
    tag.d_joined: ((3, TOKENS, DIM), BF16),
    tag.d_own: ((2, TOKENS, DIM), F32),
    tag.d_mixed_x: ((TOKENS, DIM), BF16),
    tag.small: ((4, 16, DIM), F32),
    tag.small_in: ((3, 16, DIM), F32),
    tag.small_z: ((4, 16, DIM), F32),
}
BACKWARD_SEMS = {
    tag.s_send: (UNITS, 12),
    tag.s_recv: (UNITS, 12),
    tag.s_local: (UNITS,),
    tag.s_out: (UNITS,),
    tag.fetch: (len(KEPT),),
    tag.load: (UNITS,),
    tag.made_sem: (4, 4),
    tag.x_send: (2,),
    tag.x_recv: (2,),
    tag.out_sem: (1,),
    tag.load_conv: (9,),
    tag.small_send: (6,),
    tag.small_recv: (6,),
}
SMALL = (
    [tag.bias_q, tag.bias_v, tag.bias_out, tag.gain_one, tag.shift_one, tag.gain_two, tag.shift_two]
    + [tag.bias_up0, tag.bias_up1, tag.bias_up2, tag.bias_up3, tag.bias_down, tag.bias_conv]
)


def norm_back(value, gain, change):
    center = value - jnp.mean(value, axis=-1, keepdims=True)
    scale = lax.rsqrt(jnp.mean(center * center, axis=-1, keepdims=True) + EPS)
    unit = center * scale
    scaled = change * gain
    back = scale * (
        scaled - jnp.mean(scaled, axis=-1, keepdims=True) - unit * jnp.mean(scaled * unit, axis=-1, keepdims=True)
    )
    return back, jnp.sum(change * unit, axis=0, keepdims=True), jnp.sum(change, axis=0, keepdims=True)


def column_sums(value):
    return jnp.sum(value.astype(F32), axis=0, keepdims=True)


def backward_kernel(*refs):
    names = BACKWARD_IN + list(BACKWARD_OUT) + list(BACKWARD_SCRATCH) + list(BACKWARD_SEMS) + [tag.credit]
    k = Refs(names, refs)
    z, y, c, x = place()
    turn, dev_y, dev_x, dev_c = neighbours()
    barrier = pltpu.get_barrier_semaphore()
    for other in turn + [dev_y, dev_x, dev_c]:
        pl.semaphore_signal(barrier, inc=1, device_id=other, device_id_type=MESH)

    k.surf = k.act.reshape(4 * TOKENS, DIM).at[pl.ds(0, 1920)].reshape(3, 4, 160, DIM)
    k.w_conv = k.slope.reshape(4 * TOKENS, DIM)
    k.surface = k.normed_two.reshape(4, 128, DIM)
    k.pixel_sum = k.stream_one

    def fetch(name):
        return pltpu.make_async_copy(getattr(k, tag.kept_ + name), getattr(k, name), k.fetch.at[list(KEPT).index(name)])

    def load(u):
        source = k.full.at[u]
        if u >= DOWN:
            to = k.w_down.reshape(16, 4, 48, DIM).at[:, u - DOWN]
            return pltpu.make_async_copy(source.reshape(16, 48, DIM), to, k.load.at[u])
        if u >= UP:
            return pltpu.make_async_copy(source.reshape(DIM, DIM), k.w_up.at[u - UP], k.load.at[u])
        return pltpu.make_async_copy(source.reshape(DIM, DIM), k.w_down.at[pl.ds(DIM * u, DIM)], k.load.at[u])

    order = [tag.d_two, tag.act, tag.slope, tag.normed_two, tag.stream_one, tag.mixed, tag.q, tag.keys, tag.values, tag.q_x, tag.normed_one, tag.emb]
    fetch(tag.d_two).start()
    fetch(tag.act).start()
    for u in range(DOWN, CONV):
        load(u).start()
    for name in order[2:]:
        fetch(name).start()
    for u in range(UP, DOWN):
        load(u).start()
    k.small[0] = jnp.zeros((16, DIM), F32)
    pl.semaphore_wait(barrier, 6)
    scatter = Scatter(k)
    state = {tag.tick: 0, tag.which: 0, tag.ready: 9}

    def step(count=1):
        while count > 0 and state[tag.tick] < UNITS + scatter.LAG[5]:
            which = state[tag.which]
            n = state[tag.tick] - scatter.LAG[which]
            if which == 0 and state[tag.ready] <= n < UNITS:
                return
            count -= scatter.part(state[tag.tick], which)
            state[tag.which] += 1
            if state[tag.which] == 6:
                state[tag.tick], state[tag.which] = state[tag.tick] + 1, 0

    def note(name, value, at=None):
        row = SMALL.index(name)
        where = EVERY if at is None else at
        k.small[0, row : row + 1, where] = value

    def add_note(name, value):
        row = SMALL.index(name)
        k.small[0, row : row + 1, :] += value

    step(RATE[0])
    fetch(tag.d_two).wait()
    k.branch[...] = k.d_two[...].astype(BF16)
    note(tag.bias_down, column_sums(k.branch[...]))
    note(tag.bias_conv, column_sums(k.d_pixels[...]))
    fetch(tag.act).wait()
    step(RATE[0])

    def save_down(m, piece):
        source = k.made.at[m % 2].reshape(2, 2, 4, 48, DIM).at[:, :, piece]
        return pltpu.make_async_copy(source, k.grad.at[piece, m], k.made_sem.at[m, piece])

    for m in range(4):
        if m >= 2:
            for piece in range(4):
                save_down(m - 2, piece).wait()

        @pl.loop(0, 3)
        def _(nb):
            at = cols(256 * nb)
            k.made[m % 2, :, at] = tn_dot(k.act[m], k.branch[:, at]).astype(BF16)

        for piece in range(4):
            save_down(m, piece).start()
        step(RATE[1])
    for m in (2, 3):
        for piece in range(4):
            save_down(m, piece).wait()
    state[tag.ready] = 13

    fetch(tag.slope).wait()
    for u in range(DOWN, CONV):
        load(u).wait()
    for part in range(4):

        @pl.loop(0, 3)
        def _(nb):
            at = cols(256 * nb)
            value = nt_dot(k.branch[...], k.w_down[cols(DIM * part + 256 * nb), :])
            value = (value * k.slope[part, :, at].astype(F32)).astype(BF16)
            k.slope[part, :, at] = value
            note(tag.bias_up + str(part), column_sums(value), cols(256 * nb))

        step(RATE[1])
    for u in range(QKV, UP):
        load(u).start()
    fetch(tag.normed_two).wait()

    def finish(n, slot):
        save_made(n, slot).wait()
        state[tag.ready] = 10 + n

    def save_made(n, slot):
        return pltpu.make_async_copy(k.made.at[slot], k.grad.at[n].reshape(DIM, DIM), k.made_sem.at[slot, n % 4])

    def weight_grad(n, slot, left, right, start=0):
        @pl.loop(0, 3)
        def _(nb):
            k.made[slot, :, cols(256 * nb)] = tn_dot(left[...], right[:, cols(start + 256 * nb)]).astype(BF16)

        save_made(n, slot).start()

    for part in range(4):
        if part >= 2:
            finish(2 + part, part % 2)
        weight_grad(4 + part, part % 2, k.normed_two, k.slope.at[part])
        step(RATE[1])

    for u in range(UP, DOWN):
        load(u).wait()
    k.grad_embed[...] = jnp.zeros_like(k.grad_embed)
    for part in range(4):

        @pl.loop(0, 3)
        def _(nb):
            at = cols(256 * nb)
            k.grad_embed[:, at] += nt_dot(k.slope[part], k.w_up[part, at, :])

        step(RATE[1])
        if part == 0:
            finish(6, 0)
            finish(7, 1)
    fetch(tag.surface).start()
    fetch(tag.stream_one).wait()

    @pl.loop(0, 8)
    def _(b):
        rows = pl.ds(pl.multiple_of(b * 64, 64), 64)
        back, gain, shift = norm_back(k.stream_one[rows], k.gain_two[...].reshape(1, DIM), k.grad_embed[rows])
        add_note(tag.gain_two, gain)
        add_note(tag.shift_two, shift)
        value = k.d_two[rows] + back
        k.d_two[rows] = value
        low = value.astype(BF16)
        k.branch[rows] = low
        add_note(tag.bias_out, column_sums(low))

    step(RATE[1])
    fetch(tag.mixed).wait()
    weight_grad(8, 0, k.mixed, k.branch)
    step(RATE[1])
    load(OUT).wait()

    @pl.loop(0, 3)
    def _(nb):
        at = cols(256 * nb)
        k.d_mixed[:, at] = nt_dot(k.branch[...], k.w_down[cols(DIM * OUT + 256 * nb), :]).astype(BF16)

    exchange = remote(k.d_mixed, k.d_mixed_x, k.x_send.at[0], k.x_recv.at[0], dev_x)
    exchange.start()
    finish(8, 0)
    step(RATE[1])
    for name in (tag.q, tag.keys, tag.values, tag.q_x, tag.normed_one, tag.emb):
        fetch(name).wait()

    def attend(b, own):
        rows = pl.ds(aligned(b * 128), 128)
        low = lax.broadcasted_iota(jnp.int32, (128, 128), 1) < 64

        def both(value):
            return jnp.concatenate([jnp.where(low, value, 0), jnp.where(low, 0, value)], axis=0)

        for block in range(6):
            at = slice(128 * block, 128 * block + 128)
            query = both((k.q if own else k.q_x)[rows, at])
            change = both((k.d_mixed if own else k.d_mixed_x)[rows, at])
            keys, values = k.keys[b, :, at], k.values[b, :, at]
            scores = nt_dot(keys, query) * 0.125
            power = jnp.exp(scores - jnp.max(scores, axis=0, keepdims=True))
            probs = power * (1.0 / jnp.sum(power, axis=0, keepdims=True))
            d_probs = nt_dot(values, change)
            inner = jnp.sum(probs * d_probs, axis=0, keepdims=True)
            if own:
                d_scores = (probs * (d_probs - inner)).astype(BF16)
                d_query = tn_dot(d_scores, keys) * 0.125
                k.d_joined[0, rows, at] = jnp.where(low, d_query[:128], d_query[128:]).astype(BF16)
                d_scores = d_scores[:128]
            else:
                d_scores = (probs[:128] * (d_probs[:128] - inner)).astype(BF16)
            d_keys = dot(d_scores, query) * 0.125
            d_values = dot(probs[:128].astype(BF16), change)
            if own:
                k.d_own[0, rows, at] = d_keys
                k.d_own[1, rows, at] = d_values
            else:
                k.d_joined[1, rows, at] = (k.d_own[0, rows, at] + d_keys).astype(BF16)
                k.d_joined[2, rows, at] = (k.d_own[1, rows, at] + d_values).astype(BF16)

    fetch(tag.surface).wait()
    edge = pl.ds(aligned(112 - 112 * x, 16), 16)
    halo = remote(k.surface.at[:, edge], k.halo, k.x_send.at[1], k.x_recv.at[1], dev_x)
    for half in range(2):

        @pl.loop(2 * half, 2 * half + 2)
        def _(b):
            attend(b, True)

        step(RATE[2])
    halo.start()
    weight_grad(9, 1, k.normed_one, k.d_joined.at[0])
    step(RATE[3])
    finish(9, 1)
    exchange.wait_recv()
    for half in range(2):

        @pl.loop(2 * half, 2 * half + 2)
        def _(b):
            attend(b, False)

        step(RATE[4])
    weight_grad(10, 0, k.normed_one, k.d_joined.at[1])
    step(RATE[5])
    weight_grad(11, 1, k.normed_one, k.d_joined.at[2])
    finish(10, 0)
    step(RATE[5])
    note(tag.bias_q, column_sums(k.d_joined[0]))
    note(tag.bias_v, column_sums(k.d_joined[2]))
    for u in range(QKV, OUT):
        load(u).wait()
    for part in range(3):

        @pl.loop(0, 3)
        def _(nb):
            at = cols(256 * nb)
            value = nt_dot(k.d_joined[part], k.w_down[cols(DIM * part + 256 * nb), :])
            if part == 0:
                k.grad_embed[:, at] = value
            else:
                k.grad_embed[:, at] += value

        if part == 0:
            finish(11, 1)
        step(RATE[5])

    @pl.loop(0, 8)
    def _(b):
        rows = pl.ds(pl.multiple_of(b * 64, 64), 64)
        back, gain, shift = norm_back(k.emb[rows].astype(F32), k.gain_one[...].reshape(1, DIM), k.grad_embed[rows])
        add_note(tag.gain_one, gain)
        add_note(tag.shift_one, shift)
        k.grad_embed[rows] = k.d_two[rows] + back


    def load_conv(t):
        to = k.w_conv.at[pl.ds(pl.multiple_of(DIM * lax.rem(t, 2), DIM), DIM)]
        return pltpu.make_async_copy(k.full.at[CONV + t].reshape(DIM, DIM), to, k.load_conv.at[t])

    load_conv(0).start()
    halo.wait_recv()
    extend(k.surf, k.surface, k.halo, x)
    k.pixel_sum[...] = jnp.broadcast_to(k.bias_conv[...].reshape(1, DIM), (TOKENS, DIM))
    def small(hop, dev):
        return remote(k.small.at[hop], k.small_in.at[hop], k.small_send.at[hop], k.small_recv.at[hop], dev)

    for hop, dev in enumerate((dev_c, dev_x, dev_y)):
        small(hop, dev).start()
        step(6)
        small(hop, dev).wait_recv()
        k.small[hop + 1] = k.small[hop] + k.small_in[hop]

    def small_z(step):
        return remote(
            k.small.at[3], k.small_z.at[z], k.small_send.at[3 + step], k.small_recv.at[3 + step], turn[step]
        )

    for step_z in range(3):
        small_z(step_z).start()
    k.small_z[z] = k.small[3]
    while state[tag.which]:
        step()
    rest = state[tag.tick]
    assert rest - scatter.LAG[5] >= 9

    @pl.loop(0, 9)
    def _(t):
        i, j = t // 3, lax.rem(t, 3)
        window = pl.ds(pl.multiple_of(16 * i, 16), 128)
        here = lax.rem(t, 2) * DIM
        load_conv(t).wait()

        @pl.when(t < 8)
        def _():
            load_conv(t + 1).start()

        for part in range(3):
            k.pixel_sum[:, 256 * part : 256 * part + 256] += dot(
                k.surf[j, :, window].reshape(TOKENS, DIM),
                k.w_conv[pl.ds(pl.multiple_of(here, DIM), DIM), 256 * part : 256 * part + 256],
            )
            for step in (2 * part, 2 * part + 1):
                scatter.part(rest + t, step)

    pixels = pltpu.make_async_copy(k.pixel_sum, k.pixels, k.out_sem.at[0])
    pixels.start()
    for tick in range(rest + 9, UNITS + scatter.LAG[5]):
        for which in range(6):
            scatter.part(tick, which)
    pixels.wait()
    for step_z in range(3):
        there = lax.rem(z + 3 - step_z, 4)
        remote(
            k.small.at[3], k.small_z.at[there], k.small_send.at[3 + step_z], k.small_recv.at[3 + step_z], turn[step_z]
        ).wait_recv()
    k.small_sum[...] = (k.small_z[0] + k.small_z[1]) + (k.small_z[2] + k.small_z[3])
    for hop, dev in enumerate((dev_c, dev_x, dev_y)):
        small(hop, dev).wait_send()
    for step_z in range(3):
        small_z(step_z).wait_send()
    halo.wait_send()
    exchange.wait_send()
    for n in range(UNITS - 4, UNITS):
        scatter.save(n).wait()


RATE = (3, 3, 6, 3, 6, 3)


def backward_pass(*args):
    any_space, vmem = pl.BlockSpec(memory_space=pl.ANY), pl.BlockSpec(memory_space=pltpu.VMEM)
    outs = pl.pallas_call(
        backward_kernel,
        out_shape=[jax.ShapeDtypeStruct(*kind) for kind in BACKWARD_OUT.values()],
        in_specs=[vmem] * 4 + [any_space] * (len(BACKWARD_IN) - 4),
        out_specs=[any_space] * 3 + [vmem] * 2,
        scratch_shapes=[pltpu.VMEM(*kind) for kind in BACKWARD_SCRATCH.values()]
        + [pltpu.SemaphoreType.DMA(shape) for shape in BACKWARD_SEMS.values()]
        + [pltpu.SemaphoreType.REGULAR],
        compiler_params=pltpu.CompilerParams(
            collective_id=1, has_side_effects=True, vmem_limit_bytes=63 * 2**20
        ),
        name=tag.backward_pass,
    )(*args)
    return dict(zip(BACKWARD_OUT, outs))


def deliver_kernel(sums, small, *refs):
    outs, sem = refs[:-1], refs[-1]
    qkv, out, up, down, conv = outs[:5]
    copies = [pltpu.make_async_copy(sums.at[pl.ds(0, 9)], conv, sem.at[0])]
    copies.append(pltpu.make_async_copy(sums.at[17], out, sem.at[1]))
    for n in range(3):
        copies.append(pltpu.make_async_copy(sums.at[18 + n], qkv.at[:, pl.ds(DIM * n, DIM)], sem.at[2 + n]))
    for n in range(4):
        copies.append(pltpu.make_async_copy(sums.at[13 + n], up.at[:, pl.ds(DIM * n, DIM)], sem.at[5 + n]))
        copies.append(pltpu.make_async_copy(sums.at[9 + n], down.at[pl.ds(48 * n, 48)], sem.at[9 + n]))
    for copy in copies:
        copy.start()
    rows = [(0,), (1,), (2,), (3,), (4,), (5,), (6,), (7, 8, 9, 10), (11,), (12,)]
    for ref, which in zip(outs[5:], rows):
        for n, row in enumerate(which):
            ref[pl.ds(DIM * n, DIM)] = small[row : row + 1].reshape(DIM)
    for copy in copies:
        copy.wait()


def deliver(sums, small):
    any_space, vmem = pl.BlockSpec(memory_space=pl.ANY), pl.BlockSpec(memory_space=pltpu.VMEM)
    large = [(48, 3 * DIM), (48, DIM), (48, 4 * DIM), (4 * 48, DIM), (9, 48, DIM)]
    vectors = [(DIM,)] * 7 + [(4 * DIM,)] + [(DIM,)] * 2
    return pl.pallas_call(
        deliver_kernel,
        out_shape=[jax.ShapeDtypeStruct(shape, F32) for shape in large + vectors],
        in_specs=[vmem] * 2,
        out_specs=[any_space] * 5 + [vmem] * 10,
        scratch_shapes=[pltpu.SemaphoreType.DMA((13,))],
        compiler_params=pltpu.CompilerParams(vmem_limit_bytes=16 * 2**20),
        name=tag.deliver,
    )(sums, small)


def fast_shards(
    indices,
    embed_table,
    w_qkv,
    bias_q,
    bias_v,
    w_out,
    bias_out,
    gain_one,
    shift_one,
    gain_two,
    shift_two,
    w_up,
    bias_up,
    w_down,
    bias_down,
    w_conv,
    bias_conv,
    d_pixels,
):
    out = forward_pass(
        embed_table.shape[0],
        indices,
        embed_table,
        d_pixels.reshape(4, 128, DIM),
        bias_q,
        bias_v,
        bias_out,
        gain_one,
        shift_one,
        gain_two,
        shift_two,
        bias_up,
        bias_down,
        w_qkv,
        w_out,
        w_up,
        w_down,
        w_conv,
    )
    kept = [out[tag.kept_ + name] for name in KEPT]
    back = backward_pass(gain_one, gain_two, bias_conv, d_pixels.reshape(TOKENS, DIM), out[tag.full], out[tag.grad_conv], *kept)
    g_qkv, g_out, g_up, g_down, g_conv, *small = deliver(back[tag.sums], back[tag.small_sum])
    g_bias_q, g_bias_v, g_bias_out, g_gain_one, g_shift_one, g_gain_two, g_shift_two = small[:7]
    g_bias_up, g_bias_down, g_bias_conv = small[7:]
    return (
        back[tag.pixels].reshape(4, 8, 16, DIM),
        back[tag.grad_embed].reshape(4, 8, 16, DIM),
        g_qkv,
        g_bias_q,
        g_bias_v,
        g_out,
        g_bias_out,
        g_gain_one,
        g_shift_one,
        g_gain_two,
        g_shift_two,
        g_up,
        g_bias_up,
        g_down,
        g_bias_down,
        g_conv,
        g_bias_conv,
    )


def solution(mesh):
    placed = (
        P("img", "tile", None),
        P("img", None),
        P("img", None),
        P(),
        P(),
        P("img", None),
        P(),
        P(),
        P(),
        P(),
        P(),
        P("img", None),
        P(),
        P("img", None),
        P(),
        P(None, "img", None),
        P(),
        P("img", "tile", None, None),
    )
    return jax.shard_map(
        fast_shards if dict(mesh.shape) == {"img": 16, "tile": 2} else shards,
        mesh=mesh,
        in_specs=placed,
        out_specs=(
            P("img", "tile", None, None),
            P("img", "tile", None, None),
            P("img", None),
            P(),
            P(),
            P("img", None),
            P(),
            P(),
            P(),
            P(),
            P(),
            P("img", None),
            P(),
            P("img", None),
            P(),
            P(None, "img", None),
            P(),
        ),
        check_vma=False,
    )
```
